32 devices in a mesh: grp: 2 (over y), exp: 4 (over z), dp: 4 (over x, core).
Axes of the slice: x: 2, y: 2, z: 4, core: 2. Of those that a mesh axis runs over, the one named last changes fastest.
Arguments:
- layer_inflows: bfloat16 [4096, 4096], P(('grp', 'exp', 'dp')), parts along dimension 0, may hold values from -6 to 6
- output_derivatives: bfloat16 [4096, 4096], P(('grp', 'exp', 'dp')), parts along dimension 0, may hold values from -6 to 6
- picked_specialists: int32 [4096, 8], P(('grp', 'exp', 'dp')), parts along dimension 0, may hold values from 0 to 127, as said below
- dispatch_shares: float32 [4096, 8], P(('grp', 'exp', 'dp')), parts along dimension 0, may hold values from 0.05 to 1
- item_sample: int32 [4096], P(('grp', 'exp', 'dp')), parts along dimension 0, may hold values from 0 to 7, as said below
- send_limits: int32 [256], P('grp'), parts along dimension 0, may hold values from 6 to 12, as said below
- gating_projection: bfloat16 [4, 4096, 768], P('exp', None, 'dp'), may hold values from -0.09375 to 0.09375
- raising_projection: bfloat16 [4, 4096, 768], P('exp', None, 'dp'), may hold values from -0.09375 to 0.09375
- inflow_compressor: bfloat16 [768, 64], replicated, may hold values from -0.21875 to 0.21875
- outgrad_compressor: bfloat16 [4096, 64], replicated, may hold values from -0.09375 to 0.09375
Outputs:
- sketches: float32 [16, 4, 4096], P(('grp', 'dp'), 'exp'), parts along dimension 0
The draws below stay inside these ranges and needn't reach their ends.
There are 2 independent parts, one for each index of `grp`. The reference program is written for one: setup_inputs(seed, part) draws one part's arguments, and reference() takes and returns one part's arrays. A program takes and returns all parts, laid end to end along the dimension named above; an argument that names none is the same for every part. Nothing has to cross between parts.
Inputs may be any that keep to these rules, and one draw needn't show every extreme that they name: `picked_specialists`: each row names 8 different experts; for some expert below 4 whose capacity is 12, every aligned block of 128 rows names it in 12 rows or more. `item_sample`: tokens held by dp index j belong to examples j * 2 to (j + 1) * 2 - 1; along the tokens of that index in exp order the example never falls, and every example has a token. `send_limits`: some expert below 4 has capacity exactly 12.
All inputs are finite; a program needn't handle non-finite values.
Results may differ from the reference program's by a relative error of at most 0.0085.
Values may be sent and summed in bfloat16 or wider, within the bound.
No kernel may reach another device: no remote copies, remote signals or barrier semaphores. Data moves between devices by JAX's collectives and lax.ppermute only.
A program may use at most 64 MiB of HBM per device.

```python
import math
import jax
import jax.numpy as jnp
from jax import lax

D = 4096
FF = 768
EXPERTS = 128
PICKS_PER_ITEM = 8
RANK = 64
LOCAL_ITEMS = 128
EX_DEV = 2
SUMMARY_SPECS = 4
LOCAL_SEATS = 12
TOKENS = 2048
EXAMPLES = 8
N_EXP = 4
N_DP = 4


def full_expert(key):
    return jax.random.randint(jax.random.fold_in(key, 101), (), 0, SUMMARY_SPECS)


def draw_send_limits(key, part):
    chosen = full_expert(key)
    key = jax.random.fold_in(key, 1)
    capacity = jax.random.randint(key, (EXPERTS,), LOCAL_SEATS // 2, LOCAL_SEATS + 1)
    return jnp.where(jnp.arange(EXPERTS) == chosen, LOCAL_SEATS, capacity).astype(jnp.int32)


def draw_picked_specialists(key, part):
    chosen = full_expert(key)
    key = jax.random.fold_in(key, 2)
    noise_key, favour_key, shuffle_key = jax.random.split(key, 3)
    noise = jax.random.randint(noise_key, (TOKENS, EXPERTS), 0, 65536)
    favour = jax.random.randint(favour_key, (EXPERTS,), 0, 4) * 16384
    specialist_groups = TOKENS // LOCAL_ITEMS
    shuffled = jax.random.randint(shuffle_key, (specialist_groups, LOCAL_ITEMS), 0, 1048576) * LOCAL_ITEMS + jnp.arange(LOCAL_ITEMS)[None, :]
    standing = jnp.argsort(jnp.argsort(shuffled, axis=1), axis=1).reshape(TOKENS)
    forced = standing < LOCAL_SEATS
    column = jnp.arange(EXPERTS)[None, :]
    scores = (noise + favour[None, :]) * EXPERTS + column
    scores = scores + jnp.where(forced[:, None] & (column == chosen), 33554432, 0)
    return lax.top_k(scores, PICKS_PER_ITEM)[1].astype(jnp.int32)


def draw_item_sample(key, part):
    key = jax.random.fold_in(key, 3)
    row_span = N_EXP * LOCAL_ITEMS
    row_keys = jax.random.split(key, N_DP)
    boundaries = jax.vmap(lambda sub_key: jax.random.permutation(sub_key, row_span - 1)[:EX_DEV - 1] + 1)(row_keys)
    standing = jnp.arange(row_span)
    within = jnp.sum((standing[None, :, None] >= boundaries[:, None, :]).astype(jnp.int32), axis=2)
    numbered = within + jnp.arange(N_DP)[:, None] * EX_DEV
    numbered = numbered.reshape(N_DP, N_EXP, LOCAL_ITEMS).transpose(1, 0, 2).reshape(TOKENS)
    return numbered.astype(jnp.int32)


def block_levels(stream_key, shape, cuts, smallest, top_value):
    factor_of = 1.0
    for axis_at, blocks in cuts:
        draws = jax.random.uniform(jax.random.fold_in(jax.random.fold_in(stream_key, 6), axis_at), (blocks,), jnp.float32, smallest / len(cuts), top_value / len(cuts))
        factor_of = factor_of * jnp.repeat(jnp.exp(draws), shape[axis_at] // blocks).reshape((-1,) + (1,) * (len(shape) - 1 - axis_at))
    return factor_of


def scatter_about(rng, extent, deviation, bound, shards=(), kind=jnp.bfloat16):
    level = block_levels(rng, extent, shards, -0.22, 0.18) if shards else 1.0
    entries = jax.random.normal(rng, extent, jnp.float32) * deviation * level
    return jnp.minimum(jnp.maximum(entries, -bound), bound).astype(kind)


def setup_inputs(seed: int = 0, part: int = 0) -> dict:
    splits = jax.random.split(jax.random.key(seed), 11)
    part_splits = jax.random.split(jax.random.fold_in(splits[10], part), 11)
    return {
        "layer_inflows": scatter_about(part_splits[0], (TOKENS, D), 1.0, 6.0, ((0, 16),)),
        "output_derivatives": scatter_about(part_splits[1], (TOKENS, D), 1.0, 6.0, ((0, 16),)),
        "picked_specialists": draw_picked_specialists(jax.random.fold_in(jax.random.fold_in(splits[10], part), 71), part),
        "dispatch_shares": jnp.clip(jnp.exp(math.log(1.0) - 2.9957323 * jax.random.uniform(part_splits[3], (TOKENS, PICKS_PER_ITEM), jnp.float32) ** block_levels(part_splits[3], (TOKENS, PICKS_PER_ITEM), ((0, 16),), -0.2, 0.2)), 0.05, 1.0),
        "item_sample": draw_item_sample(jax.random.fold_in(jax.random.fold_in(splits[10], part), 71), part),
        "send_limits": draw_send_limits(jax.random.fold_in(jax.random.fold_in(splits[10], part), 71), part),
        "gating_projection": scatter_about(splits[6], (SUMMARY_SPECS, D, FF), D ** -0.5, 0.09375, ((0, 4), (2, 4))),
        "raising_projection": scatter_about(splits[7], (SUMMARY_SPECS, D, FF), D ** -0.5, 0.09375, ((0, 4), (2, 4))),
        "inflow_compressor": scatter_about(splits[8], (FF, RANK), FF ** -0.5, 0.21875),
        "outgrad_compressor": scatter_about(splits[9], (D, RANK), D ** -0.5, 0.09375),
    }


def placement_lookup(dispatch_group, send_limits, compressed_specialists, occupied_total):
    flat_ids = dispatch_group.reshape(-1)
    experts = lax.broadcasted_iota(jnp.int32, (1, compressed_specialists), 1)
    equality_flags = (flat_ids[:, None] == experts).astype(jnp.int32)
    earlier = jnp.cumsum(equality_flags, axis=0) - equality_flags
    position = jnp.sum(earlier * equality_flags, axis=1)
    allowance_flags = jnp.sum(equality_flags * send_limits[:compressed_specialists][None, :], axis=1)
    accepted = (flat_ids < compressed_specialists) & (position < allowance_flags)
    target = jnp.where(accepted, flat_ids * occupied_total + position, compressed_specialists * occupied_total)
    pair_ids = jnp.arange(flat_ids.shape[0], dtype=jnp.int32)
    blank_slots = jnp.full((compressed_specialists * occupied_total,), flat_ids.shape[0], jnp.int32)
    return blank_slots.at[target].set(pair_ids, mode="drop")


def reference(layer_inflows, output_derivatives, picked_specialists, dispatch_shares, item_sample, send_limits, gating_projection, raising_projection, inflow_compressor, outgrad_compressor):
    specialist_groups = TOKENS // LOCAL_ITEMS
    placement_lookups = jax.vmap(lambda specialist_group: placement_lookup(specialist_group, send_limits, SUMMARY_SPECS, LOCAL_SEATS))(picked_specialists.reshape(specialist_groups, LOCAL_ITEMS, PICKS_PER_ITEM))
    offsets = (jnp.arange(specialist_groups, dtype=jnp.int32) * (LOCAL_ITEMS * PICKS_PER_ITEM))[:, None]
    occupied = placement_lookups < LOCAL_ITEMS * PICKS_PER_ITEM
    pair_index = jnp.where(occupied, placement_lookups + offsets, TOKENS * PICKS_PER_ITEM).astype(jnp.int32)
    token_index = (pair_index // PICKS_PER_ITEM).astype(jnp.int32)
    grad_proj = jnp.dot(output_derivatives, outgrad_compressor, preferred_element_type=jnp.float32)
    grad_pairs = (dispatch_shares[:, :, None] * grad_proj[:, None, :]).astype(jnp.bfloat16).reshape(TOKENS * PICKS_PER_ITEM, RANK)
    grad_pairs = jnp.concatenate([grad_pairs, jnp.zeros((1, RANK), jnp.bfloat16)], axis=0)
    padded_tokens = jnp.concatenate([layer_inflows, jnp.zeros((1, D), jnp.bfloat16)], axis=0)
    padded_examples = jnp.concatenate([item_sample, jnp.zeros((1,), jnp.int32)], axis=0)
    example_range = jnp.arange(EXAMPLES, dtype=jnp.int32)

    def one_expert(expert):
        slot_ids = lax.dynamic_slice_in_dim(token_index, (expert * LOCAL_SEATS).astype(jnp.int32), LOCAL_SEATS, 1).reshape(-1)
        pair_slots = lax.dynamic_slice_in_dim(pair_index, (expert * LOCAL_SEATS).astype(jnp.int32), LOCAL_SEATS, 1).reshape(-1)
        gathered = padded_tokens[slot_ids]
        gate_pre = jnp.dot(gathered, gating_projection[expert], preferred_element_type=jnp.float32)
        up_pre = jnp.dot(gathered, raising_projection[expert], preferred_element_type=jnp.float32)
        hidden = (jax.nn.silu(gate_pre) * up_pre).astype(jnp.bfloat16)
        sketch_rows = jnp.dot(hidden, inflow_compressor, preferred_element_type=jnp.float32).astype(jnp.bfloat16)
        grad_rows = grad_pairs[pair_slots].astype(jnp.float32)
        owners = padded_examples[slot_ids]
        selector = owners[:, None] == example_range[None, :]
        weighted = jnp.where(selector[:, :, None], sketch_rows[:, None, :].astype(jnp.float32), jnp.float32(0.0))
        weighted = weighted.reshape(-1, EXAMPLES * RANK)
        partial_value = jnp.dot(weighted.T, grad_rows, precision=lax.Precision.HIGHEST)
        return partial_value.reshape(EXAMPLES, RANK * RANK)

    stacked = lax.map(one_expert, jnp.arange(SUMMARY_SPECS, dtype=jnp.int32))
    return jnp.transpose(stacked, (1, 0, 2))
```

```python
import functools

import jax
import jax.numpy as jnp
from jax import lax
from jax.experimental import pallas as pl
from jax.experimental.pallas import tpu as pltpu
from jax.sharding import PartitionSpec as P

EX_DEV = 2
LOCAL_SEATS = 12
ROWS = 16
SPARE = ROWS - LOCAL_SEATS
PARTS = LOCAL_SEATS // SPARE
VMEM_LIMIT = 48 * 1024 * 1024
BF16 = jnp.bfloat16
F32 = jnp.float32


def dot(a, b):
    return jnp.dot(a, b, preferred_element_type=F32)


def seats_of(limits_ref, picked_ref, experts):
    tokens = picked_ref.shape[0]
    picked = picked_ref[...].T
    flags = [jnp.max((picked == e).astype(F32), axis=0, keepdims=True) for e in experts]
    flags = jnp.concatenate(flags, axis=0)
    earlier = lax.broadcasted_iota(jnp.int32, (tokens, tokens), 0)
    later = lax.broadcasted_iota(jnp.int32, (tokens, tokens), 1)
    before = (earlier < later).astype(F32).astype(BF16)
    position = dot(flags.astype(BF16), before).astype(jnp.int32)
    rows = []
    for i, e in enumerate(experts):
        limit = jnp.minimum(limits_ref[e], LOCAL_SEATS)
        at = position[i : i + 1]
        rows.append(jnp.where((flags[i : i + 1] > 0.0) & (at < limit), at, -1))
    return rows


def one_hot(mask):
    return mask.astype(F32).astype(BF16)


def rows_kernel(count, limits_ref, picked_ref, tokens_ref, *out_refs):
    me = lax.axis_index("exp")
    tokens, width = tokens_ref.shape
    chunk = width // (PARTS + 1)
    seats = seats_of(limits_ref, picked_ref, [jnp.bitwise_xor(me, q) for q in range(count)])
    slot = lax.broadcasted_iota(jnp.int32, (ROWS, tokens), 0)
    near = jnp.concatenate([one_hot(slot == s) for s in seats], axis=0)
    for i in range(PARTS):
        shifted = jnp.where(slot >= LOCAL_SEATS, slot - LOCAL_SEATS + SPARE * i, -2)
        far = jnp.concatenate([one_hot(shifted == s) for s in seats], axis=0)
        columns = slice(i * chunk, (i + 1) * chunk)
        source = jnp.concatenate([tokens_ref[:, columns], tokens_ref[:, PARTS * chunk :]], axis=0)
        packed = dot(jnp.concatenate([near, far], axis=1), source).astype(BF16)
        for q in range(count):
            out_refs[q][:, columns] = packed[q * ROWS : (q + 1) * ROWS]


def grads_kernel(
    count, limits_ref, picked_ref, shares_ref, owner_ref, derivs_ref, compressor_ref, *out_refs
):
    me = lax.axis_index("exp")
    first = lax.axis_index("dp") * EX_DEV
    tokens = derivs_ref.shape[0]
    experts = [jnp.bitwise_xor(me, q) for q in range(count)]
    seats = seats_of(limits_ref, picked_ref, experts)
    slot = lax.broadcasted_iota(jnp.int32, (ROWS, tokens), 0)
    owner = owner_ref[...] - first
    proj = dot(derivs_ref[...], compressor_ref[...])
    for q in range(count):
        share = jnp.sum(
            jnp.where(picked_ref[...] == experts[q], shares_ref[...], 0.0), axis=1, keepdims=True
        )
        grad = (share * proj).astype(BF16)
        halves = [
            dot(one_hot((slot == seats[q]) & (owner == n)), grad).astype(BF16)
            for n in range(EX_DEV)
        ]
        out_refs[q][...] = jnp.concatenate(halves, axis=1)


def hidden_kernel(
    sizes, gate_ref, up_ref, compressor_ref, *refs
):
    block_refs, out_refs = refs[: -len(sizes)], refs[-len(sizes) :]
    units = gate_ref.shape[1]
    chunk = gate_ref.shape[0] // (PARTS + 1)
    total = sum(sizes)
    acc = [None, None]
    far = [[], []]
    for i in range(PARTS):
        columns = slice(i * chunk, (i + 1) * chunk)
        left = jnp.concatenate([r[:, columns] for r in block_refs], axis=0)
        for k, w in enumerate((gate_ref, up_ref)):
            near = dot(left, w[columns, :])
            acc[k] = near if acc[k] is None else acc[k] + near
            tail = dot(left, w[PARTS * chunk :, :])
            far[k].append(tail.reshape(total // ROWS, 2, ROWS // 2, units)[:, 1])
    sub = lax.broadcasted_iota(jnp.int32, (1, ROWS // 2, 1), 1)
    low = sub < SPARE
    full = []
    for k in range(2):
        halves = acc[k].reshape(total // ROWS, 2, ROWS // 2, units)

        def turned(a):
            return jnp.concatenate([a[:, SPARE:], a[:, :SPARE]], axis=1)

        top = halves[:, 0] + jnp.where(low, turned(far[k][0]), far[k][1])
        bottom = jnp.where(low, halves[:, 1] + turned(far[k][2]), 0.0)
        full.append(jnp.stack([top, bottom], axis=1).reshape(total, units))
    gate, up = full
    hidden = (gate / (1.0 + jnp.exp(-gate)) * up).astype(BF16)
    start = pl.multiple_of(lax.axis_index("dp") * units, 16)
    sketch = dot(hidden, compressor_ref[pl.ds(start, units), :])
    at = 0
    for size, out in zip(sizes, out_refs):
        half = size // 2
        pair = jnp.concatenate([sketch[at : at + half], sketch[at + half : at + size]], axis=1)
        out[...] = pair.astype(out.dtype)
        at += size


def outer_kernel(n_partial, *refs):
    partial_refs, grad_refs, out_ref = refs[:n_partial], refs[n_partial:-1], refs[-1]
    total = partial_refs[0][...].astype(F32)
    for r in partial_refs[1:]:
        total = total + r[...].astype(F32)
    rows, lanes = total.shape
    width = lanes // 2
    source = lax.broadcasted_iota(jnp.int32, (lanes, lanes), 0)
    target = lax.broadcasted_iota(jnp.int32, (lanes, lanes), 1)
    inner = target % width
    wanted = (target - inner) + jnp.where(
        inner < width // 2, 2 * inner, 2 * (inner - width // 2) + 1
    )
    order = one_hot(source == wanted)
    turned = dot(total.astype(BF16), order).T.astype(BF16)
    grads = jnp.concatenate([r[...] for r in grad_refs], axis=0)
    product = dot(turned[:width], grads[:rows]) + dot(turned[width:], grads[rows:])
    even, odd = product[: width // 2], product[width // 2 :]
    for n in range(EX_DEV):
        columns = slice(n * width, (n + 1) * width)
        out_ref[n] = jnp.concatenate([even[:, columns], odd[:, columns]], axis=1)


VMEM = pl.BlockSpec(memory_space=pltpu.VMEM)
SMEM = pl.BlockSpec(memory_space=pltpu.SMEM)


def call(kernel, out_shape, n_in, limits_first=False, flops=0, moved=0):
    return pl.pallas_call(
        kernel,
        out_shape=out_shape,
        in_specs=[SMEM if limits_first and i == 0 else VMEM for i in range(n_in)],
        out_specs=jax.tree.map(lambda _: VMEM, out_shape),
        compiler_params=pltpu.CompilerParams(vmem_limit_bytes=VMEM_LIMIT),
        cost_estimate=pl.CostEstimate(flops=flops, bytes_accessed=moved, transcendentals=0),
    )


def swap(a, axis, q):
    n = lax.axis_size(axis)
    return lax.ppermute(a, axis, [(i, i ^ q) for i in range(n)])


def body(
    layer_inflows,
    output_derivatives,
    picked_specialists,
    dispatch_shares,
    item_sample,
    send_limits,
    gating_projection,
    raising_projection,
    inflow_compressor,
    outgrad_compressor,
):
    n_exp, n_dp = lax.axis_size("exp"), lax.axis_size("dp")
    small = n_exp * n_dp <= 32
    tokens, width = layer_inflows.shape
    rank = outgrad_compressor.shape[1]
    packed = width * LOCAL_SEATS // ROWS
    units = gating_projection.shape[2]
    shape = jax.ShapeDtypeStruct

    rows = call(
        functools.partial(rows_kernel, n_exp),
        [shape((ROWS, packed), BF16)] * n_exp,
        3,
        True,
        flops=2 * n_exp * ROWS * 2 * tokens * packed,
        moved=2 * tokens * width,
    )(send_limits, picked_specialists, layer_inflows)
    rows = [rows[0]] + [swap(rows[q], "exp", q) for q in range(1, n_exp)]
    grads = call(
        functools.partial(grads_kernel, n_exp),
        [shape((ROWS, EX_DEV * rank), BF16)] * n_exp,
        6,
        True,
        flops=2 * tokens * width * rank,
        moved=2 * tokens * width + 2 * width * rank,
    )(
        send_limits,
        picked_specialists,
        dispatch_shares,
        item_sample.reshape(1, tokens),
        output_derivatives,
        outgrad_compressor,
    )
    grads = [grads[0]] + [swap(grads[q], "exp", q) for q in range(1, n_exp)]

    blocks = {0: rows} if small else {0: [jnp.concatenate(rows, axis=0)]}
    step = n_dp // 2
    while step:
        for d in list(blocks):
            blocks[d ^ step] = [swap(r, "dp", step) for r in blocks[d]]
        step //= 2
    size = n_exp * ROWS
    gate, up = gating_projection[0], raising_projection[0]

    def sketch(ds):
        parts = [r for d in ds for r in blocks[d]]
        return call(
            functools.partial(hidden_kernel, [size] * len(ds)),
            [shape((size // 2, 2 * rank), BF16 if d else F32) for d in ds],
            3 + len(parts),
            flops=4 * len(ds) * size * width * units,
            moved=4 * width * units + 2 * len(ds) * size * packed,
        )(gate, up, inflow_compressor, *parts)

    every = list(range(n_dp))
    groups = [every] if small else [[d] for d in every]
    partials = [p for g in groups for p in sketch(g)]
    partials = [partials[0]] + [swap(partials[d], "dp", d) for d in range(1, n_dp)]
    out = call(
        functools.partial(outer_kernel, n_dp),
        shape((EX_DEV, rank * rank // 128, 128), F32),
        n_dp + n_exp,
        flops=2 * size * rank * 2 * rank,
        moved=4 * EX_DEV * rank * rank,
    )(*partials, *grads)
    return out.reshape(EX_DEV, 1, rank * rank)


def solution(mesh):
    in_specs = (
        P(("grp", "exp", "dp"), None),
        P(("grp", "exp", "dp"), None),
        P(("grp", "exp", "dp"), None),
        P(("grp", "exp", "dp"), None),
        P(("grp", "exp", "dp")),
        P("grp"),
        P("exp", None, "dp"),
        P("exp", None, "dp"),
        P(),
        P(),
    )
    out_specs = P(("grp", "dp"), "exp", None)
    return jax.shard_map(body, mesh=mesh, in_specs=in_specs, out_specs=out_specs, check_vma=False)
```

```python
import functools

import jax
import jax.numpy as jnp
from jax import lax
from jax.experimental import pallas as pl
from jax.experimental.pallas import tpu as pltpu
from jax.sharding import PartitionSpec as P

EX_DEV = 2
LOCAL_SEATS = 12
ROWS = 16
SPARE = ROWS - LOCAL_SEATS
PARTS = LOCAL_SEATS // SPARE
HALF = ROWS // 2
MIB = 1024 * 1024
BF16 = jnp.bfloat16
F32 = jnp.float32


def dot(a, b):
    return jnp.dot(a, b, preferred_element_type=F32)


def dot_t(a, b):
    return lax.dot_general(a, b, (((1,), (1,)), ((), ())), preferred_element_type=F32)


def one_hot(mask):
    return mask.astype(F32).astype(BF16)


def seats_of(limits_ref, picked, experts):
    tokens = picked.shape[1]
    flags = [jnp.max((picked == e).astype(F32), axis=0, keepdims=True) for e in experts]
    flags = jnp.concatenate(flags, axis=0)
    earlier = lax.broadcasted_iota(jnp.int32, (tokens, tokens), 0)
    later = lax.broadcasted_iota(jnp.int32, (tokens, tokens), 1)
    position = dot(flags.astype(BF16), one_hot(earlier < later)).astype(jnp.int32)
    rows = []
    for i, e in enumerate(experts):
        limit = jnp.minimum(limits_ref[e], LOCAL_SEATS)
        at = position[i : i + 1]
        rows.append(jnp.where((flags[i : i + 1] > 0.0) & (at < limit), at, -1))
    return rows


def rows_kernel(count, limits_hbm, picked_hbm, tokens_hbm, *refs):
    out_refs = refs[:count]
    limits_ref, picked_ref, tokens_ref, sems = refs[count:]
    tokens, width = tokens_ref.shape
    chunk = width // (PARTS + 1)
    columns = [slice(i * chunk, (i + 1) * chunk) for i in range(PARTS + 1)]
    small = [
        pltpu.make_async_copy(limits_hbm, limits_ref, sems.at[0]),
        pltpu.make_async_copy(picked_hbm, picked_ref, sems.at[1]),
    ]
    large = [
        pltpu.make_async_copy(tokens_hbm.at[:, c], tokens_ref.at[:, c], sems.at[2 + i])
        for i, c in enumerate(columns)
    ]
    for copy in small + [large[-1]] + large[:-1]:
        copy.start()
    for copy in small:
        copy.wait()
    me = lax.axis_index("exp")
    experts = [jnp.bitwise_xor(me, q) for q in range(count)]
    seats = seats_of(limits_ref, picked_ref[...], experts)
    slot = lax.broadcasted_iota(jnp.int32, (ROWS, tokens), 0)
    near = jnp.concatenate([one_hot(slot == s) for s in seats], axis=0)
    large[-1].wait()
    for i in range(PARTS):
        shifted = jnp.where(slot >= LOCAL_SEATS, slot - LOCAL_SEATS + SPARE * i, -2)
        far = jnp.concatenate([one_hot(shifted == s) for s in seats], axis=0)
        large[i].wait()
        source = jnp.concatenate([tokens_ref[:, columns[i]], tokens_ref[:, columns[-1]]], axis=0)
        packed = dot(jnp.concatenate([near, far], axis=1), source).astype(BF16)
        for q in range(count):
            out_refs[q][:, columns[i]] = packed[q * ROWS : (q + 1) * ROWS]


def grads_kernel(
    count,
    limits_ref,
    picked_ref,
    shares_ref,
    owner_ref,
    derivs_ref,
    out_compressor_ref,
    in_compressor_ref,
    *out_refs,
):
    me = lax.axis_index("exp")
    place = lax.axis_index("dp")
    tokens = derivs_ref.shape[0]
    experts = [jnp.bitwise_xor(me, q) for q in range(count)]
    picked = picked_ref[...]
    seats = seats_of(limits_ref, picked, experts)
    slot = lax.broadcasted_iota(jnp.int32, (ROWS, tokens), 0)
    owner = owner_ref[...] - place * EX_DEV
    proj = dot_t(derivs_ref[...], out_compressor_ref[...])
    share_rows = [
        jnp.sum(jnp.where(picked == e, shares_ref[...], 0.0), axis=0, keepdims=True)
        for e in experts
    ]
    pad = [jnp.zeros((-count % 8, tokens), F32)] if count % 8 else []
    shares = jnp.concatenate(share_rows + pad, axis=0).T
    for q in range(count):
        grad = (shares[:, q : q + 1] * proj).astype(BF16)
        halves = [
            dot(one_hot((slot == seats[q]) & (owner == n)), grad).astype(BF16)
            for n in range(EX_DEV)
        ]
        out_refs[q][...] = jnp.concatenate(halves, axis=1)
    rank, total = in_compressor_ref.shape
    units = out_refs[count].shape[1]
    to = lax.broadcasted_iota(jnp.int32, (rank, rank), 0)
    at = lax.broadcasted_iota(jnp.int32, (rank, rank), 1)
    order = one_hot(at == jnp.where(to < rank // 2, 2 * to, 2 * to - rank + 1))
    turned = dot(order, in_compressor_ref[...]).astype(BF16)
    line = lax.broadcasted_iota(jnp.int32, (total, units), 0)
    unit = lax.broadcasted_iota(jnp.int32, (total, units), 1)
    for k in range(2):
        first = jnp.bitwise_xor(place, k) * units
        out_refs[count + k][...] = dot(turned, one_hot(line == unit + first)).astype(BF16)


def hidden_kernel(n_blocks, *refs):
    weights = (refs[0:2], refs[2:4])
    compressors = refs[4:6]
    block_refs, out_ref = refs[6 : 6 + n_blocks], refs[-1]
    units, width = weights[0][0].shape
    chunk = width // (PARTS + 1)
    messages = sum(r.shape[0] for r in block_refs) // ROWS
    low = lax.broadcasted_iota(jnp.int32, (1, HALF, 1), 1) < SPARE

    def turn(a):
        return jnp.concatenate([a[:, SPARE:], a[:, :SPARE]], axis=1)

    columns = [slice(i * chunk, (i + 1) * chunk) for i in range(PARTS + 1)]
    lefts = [jnp.concatenate([r[:, c] for r in block_refs], axis=0) for c in columns[:PARTS]]
    tails = []
    for left in lefts:
        tail = left.astype(F32).reshape(messages // 2, 2, 2, HALF, chunk)[:, :, 1]
        tails.append(jnp.where(low, turn(tail[:, 0]), tail[:, 1]))
    tail = jnp.stack(tails, axis=0).reshape(PARTS * messages * SPARE, chunk).astype(BF16)

    def product(w):
        near = dot_t(lefts[0], w[:, columns[0]])
        for i in range(1, PARTS):
            near = near + dot_t(lefts[i], w[:, columns[i]])
        near = near.reshape(messages // 2, 2, 2, HALF, units)
        far = dot_t(tail, w[:, columns[PARTS]]).reshape(PARTS, messages // 2, HALF, units)
        spun = [turn(far[i]) for i in range(PARTS)]
        first_top = near[:, 0, 0] + jnp.where(low, far[0], spun[1])
        first_low = jnp.where(low, near[:, 0, 1] + far[2], 0.0)
        second_top = near[:, 1, 0] + jnp.where(low, spun[0], far[1])
        second_low = jnp.where(low, near[:, 1, 1] + spun[2], 0.0)
        parts = jnp.stack([first_top, first_low, second_top, second_low], axis=1)
        return parts.reshape(messages * ROWS, units)

    sketch = None
    for (gate_ref, up_ref), compressor in zip(weights, compressors):
        gate, up = product(gate_ref), product(up_ref)
        hidden = (gate / (1.0 + jnp.exp(-gate)) * up).astype(BF16)
        term = dot_t(compressor[...], hidden)
        sketch = term if sketch is None else sketch + term
    out_ref[...] = sketch.astype(out_ref.dtype)


def outer_kernel(n_partial, *refs):
    partial_refs, grad_refs, out_ref = refs[:n_partial], refs[n_partial:-1], refs[-1]
    total = partial_refs[0][...].astype(F32)
    for r in partial_refs[1:]:
        total = total + r[...].astype(F32)
    rank = total.shape[0]
    grads = jnp.concatenate([r[...] for r in grad_refs], axis=0)
    product = dot(total.astype(BF16), grads)
    even, odd = product[: rank // 2], product[rank // 2 :]
    for n in range(EX_DEV):
        columns = slice(n * rank, (n + 1) * rank)
        out_ref[n] = jnp.concatenate([even[:, columns], odd[:, columns]], axis=1)


VMEM = pl.BlockSpec(memory_space=pltpu.VMEM)
SMEM = pl.BlockSpec(memory_space=pltpu.SMEM)
HBM = pl.BlockSpec(memory_space=pltpu.HBM)


def call(kernel, out_shape, in_specs, limit, flops=0, moved=0, scratch=()):
    return pl.pallas_call(
        kernel,
        out_shape=out_shape,
        in_specs=in_specs,
        out_specs=jax.tree.map(lambda _: VMEM, out_shape),
        scratch_shapes=list(scratch),
        compiler_params=pltpu.CompilerParams(vmem_limit_bytes=limit),
        cost_estimate=pl.CostEstimate(flops=flops, bytes_accessed=moved, transcendentals=0),
    )


def swap(a, axis, q):
    n = lax.axis_size(axis)
    return lax.ppermute(a, axis, [(i, i ^ q) for i in range(n)])


def body(
    layer_inflows,
    output_derivatives,
    picked_specialists,
    dispatch_shares,
    item_sample,
    send_limits,
    gating_projection,
    raising_projection,
    inflow_compressor,
    outgrad_compressor,
):
    n_exp, n_dp = lax.axis_size("exp"), lax.axis_size("dp")
    small = n_exp <= 8
    tokens, width = layer_inflows.shape
    rank = outgrad_compressor.shape[1]
    packed = width * LOCAL_SEATS // ROWS
    units = gating_projection.shape[2]
    size = n_exp * ROWS
    shape = jax.ShapeDtypeStruct
    picked = picked_specialists.T

    gate, up = gating_projection[0].T, raising_projection[0].T
    pair_gate, pair_up = swap(gate, "dp", 1), swap(up, "dp", 1)

    rows = call(
        functools.partial(rows_kernel, n_exp),
        [shape((ROWS, packed), BF16)] * n_exp,
        [HBM] * 3,
        24 * MIB,
        flops=2 * size * 2 * tokens * packed,
        moved=2 * tokens * width,
        scratch=[
            pltpu.SMEM(send_limits.shape, jnp.int32),
            pltpu.VMEM(picked.shape, jnp.int32),
            pltpu.VMEM((tokens, width), BF16),
            pltpu.SemaphoreType.DMA((PARTS + 3,)),
        ],
    )(send_limits, picked, layer_inflows)
    rows = [rows[0]] + [swap(rows[q], "exp", q) for q in range(1, n_exp)]

    made = call(
        functools.partial(grads_kernel, n_exp),
        [shape((ROWS, EX_DEV * rank), BF16)] * n_exp + [shape((rank, units), BF16)] * 2,
        [SMEM] + [VMEM] * 6,
        24 * MIB,
        flops=2 * tokens * width * rank,
        moved=2 * tokens * width + 2 * width * rank,
    )(
        send_limits,
        picked,
        dispatch_shares.T,
        item_sample.reshape(1, tokens),
        output_derivatives,
        outgrad_compressor.T,
        inflow_compressor.T,
    )
    compressors = made[n_exp:]
    grads = [made[0]] + [swap(made[q], "exp", q) for q in range(1, n_exp)]

    blocks = {0: rows if small else [jnp.concatenate(rows, axis=0)]}
    step = n_dp // 2
    while step > 1:
        for d in list(blocks):
            blocks[d ^ step] = [swap(r, "dp", step) for r in blocks[d]]
        step //= 2

    def sketch(d, dtype):
        parts = blocks[d]
        return call(
            functools.partial(hidden_kernel, len(parts)),
            shape((rank, size), dtype),
            [VMEM] * (6 + len(parts)),
            24 * MIB,
            flops=8 * size * width * units,
            moved=8 * width * units + 2 * size * packed,
        )(gate, up, pair_gate, pair_up, *compressors, *parts)

    blocks[0], grads = lax.optimization_barrier((blocks[0], grads))
    partials = [sketch(0, F32)]
    partials += [swap(sketch(d, BF16), "dp", d) for d in sorted(blocks) if d]
    out = call(
        functools.partial(outer_kernel, len(partials)),
        shape((EX_DEV, rank * rank // 128, 128), F32),
        [VMEM] * (len(partials) + n_exp),
        8 * MIB,
        flops=2 * size * rank * 2 * rank,
        moved=4 * EX_DEV * rank * rank,
    )(*partials, *grads)
    return out.reshape(EX_DEV, 1, rank * rank)


def solution(mesh):
    in_specs = (
        P(("grp", "exp", "dp"), None),
        P(("grp", "exp", "dp"), None),
        P(("grp", "exp", "dp"), None),
        P(("grp", "exp", "dp"), None),
        P(("grp", "exp", "dp")),
        P("grp"),
        P("exp", None, "dp"),
        P("exp", None, "dp"),
        P(),
        P(),
    )
    out_specs = P(("grp", "dp"), "exp", None)
    return jax.shard_map(body, mesh=mesh, in_specs=in_specs, out_specs=out_specs, check_vma=False)
```

```python
import functools

import jax
import jax.numpy as jnp
from jax import lax
from jax.experimental import pallas as pl
from jax.experimental.pallas import tpu as pltpu
from jax.sharding import PartitionSpec as P

EX_DEV = 2
LOCAL_SEATS = 12
ROWS = 16
SPARE = ROWS - LOCAL_SEATS
PARTS = LOCAL_SEATS // SPARE
HALF = ROWS // 2
MIB = 1024 * 1024
BF16 = jnp.bfloat16
F32 = jnp.float32


def dot(a, b):
    return jnp.dot(a, b, preferred_element_type=F32)


def dot_t(a, b):
    return lax.dot_general(a, b, (((1,), (1,)), ((), ())), preferred_element_type=F32)


def one_hot(mask):
    return mask.astype(F32).astype(BF16)


def seats_of(limits_ref, picked, experts):
    tokens = picked.shape[1]
    flags = [jnp.max((picked == e).astype(F32), axis=0, keepdims=True) for e in experts]
    flags = jnp.concatenate(flags, axis=0)
    earlier = lax.broadcasted_iota(jnp.int32, (tokens, tokens), 0)
    later = lax.broadcasted_iota(jnp.int32, (tokens, tokens), 1)
    position = dot(flags.astype(BF16), one_hot(earlier < later)).astype(jnp.int32)
    rows = []
    for i, e in enumerate(experts):
        limit = jnp.minimum(limits_ref[e], LOCAL_SEATS)
        at = position[i : i + 1]
        rows.append(jnp.where((flags[i : i + 1] > 0.0) & (at < limit), at, -1))
    return rows


def send_kernel(count, limits_hbm, picked_hbm, shares_hbm, owner_hbm, tokens_hbm, derivs_hbm, compressor_hbm, *refs):
    out_refs = refs[:count]
    limits_ref, picked_ref, shares_ref, owner_ref, tokens_ref, derivs_ref, compressor_ref, sems = (
        refs[count:]
    )
    tokens, width = tokens_ref.shape
    chunk = width // (PARTS + 1)
    columns = [slice(i * chunk, (i + 1) * chunk) for i in range(PARTS + 1)]
    pairs = [
        (limits_hbm, limits_ref),
        (picked_hbm, picked_ref),
        (shares_hbm, shares_ref),
        (owner_hbm, owner_ref),
        (tokens_hbm, tokens_ref),
        (derivs_hbm, derivs_ref),
        (compressor_hbm, compressor_ref),
    ]
    copies = [pltpu.make_async_copy(a, b, sems.at[i]) for i, (a, b) in enumerate(pairs)]
    for copy in copies:
        copy.start()
    for copy in copies[:4]:
        copy.wait()
    me = lax.axis_index("exp")
    experts = [jnp.bitwise_xor(me, q) for q in range(count)]
    picked = picked_ref[...]
    seats = seats_of(limits_ref, picked, experts)
    slot = lax.broadcasted_iota(jnp.int32, (ROWS, tokens), 0)
    near = jnp.concatenate([one_hot(slot == s) for s in seats], axis=0)
    masks = []
    for i in range(PARTS):
        shifted = jnp.where(slot >= LOCAL_SEATS, slot - LOCAL_SEATS + SPARE * i, -2)
        far = jnp.concatenate([one_hot(shifted == s) for s in seats], axis=0)
        masks.append(jnp.concatenate([near, far], axis=1))
    owner = owner_ref[...] - lax.axis_index("dp") * EX_DEV
    owned = [
        jnp.concatenate([one_hot((slot == s) & (owner == n)) for n in range(EX_DEV)], axis=0)
        for s in seats
    ]
    share_rows = [
        jnp.sum(jnp.where(picked == e, shares_ref[...], 0.0), axis=0, keepdims=True)
        for e in experts
    ]
    pad = [jnp.zeros((-count % 8, tokens), F32)] if count % 8 else []
    shares = jnp.concatenate(share_rows + pad, axis=0).T
    for copy in copies[4:]:
        copy.wait()
    proj = dot_t(derivs_ref[...], compressor_ref[...])
    last = tokens_ref[:, columns[-1]]
    for i in range(PARTS):
        source = jnp.concatenate([tokens_ref[:, columns[i]], last], axis=0)
        packed = dot(masks[i], source).astype(BF16)
        for q in range(count):
            out_refs[q][:, columns[i]] = packed[q * ROWS : (q + 1) * ROWS]
    for q in range(count):
        grad = (shares[:, q : q + 1] * proj).astype(BF16)
        both = dot(owned[q], grad)
        halves = [both[n * ROWS : (n + 1) * ROWS] for n in range(EX_DEV)]
        out_refs[q][:, PARTS * chunk :] = jnp.concatenate(halves, axis=1).astype(BF16)


def pair_compressors(compressor_ref, units):
    place = lax.axis_index("dp")
    rank, total = compressor_ref.shape
    to = lax.broadcasted_iota(jnp.int32, (rank, rank), 0)
    at = lax.broadcasted_iota(jnp.int32, (rank, rank), 1)
    order = one_hot(at == jnp.where(to < rank // 2, 2 * to, 2 * to - rank + 1))
    turned = dot(order, compressor_ref[...]).astype(BF16)
    line = lax.broadcasted_iota(jnp.int32, (total, units), 0)
    unit = lax.broadcasted_iota(jnp.int32, (total, units), 1)
    return [
        dot(turned, one_hot(line == unit + jnp.bitwise_xor(place, k) * units)).astype(BF16)
        for k in range(2)
    ]


def sketch_of(weights, compressors, block_refs):
    width = weights[0][0].shape[1]
    chunk = width // (PARTS + 1)
    size = sum(r.shape[0] for r in block_refs)
    messages = size // ROWS
    low = lax.broadcasted_iota(jnp.int32, (1, HALF, 1), 1) < SPARE
    columns = [slice(i * chunk, (i + 1) * chunk) for i in range(PARTS + 1)]
    rows = [jnp.concatenate([r[:, c] for r in block_refs], axis=0) for c in columns[:PARTS]]
    tails = [r.astype(F32).reshape(messages, 2, HALF, chunk)[:, 1] for r in rows]

    def turn(a):
        return jnp.concatenate([a[:, SPARE:], a[:, :SPARE]], axis=1)

    top = jnp.where(low, turn(tails[0]), tails[1])
    bottom = jnp.where(low, turn(tails[2]), 0.0)
    rows.append(jnp.stack([top, bottom], axis=1).reshape(size, chunk).astype(BF16))
    seat = lax.broadcasted_iota(jnp.int32, (1, size), 1) % ROWS

    def product(w):
        total = dot_t(w[:, columns[0]], rows[0])
        for c, r in zip(columns[1:], rows[1:]):
            total = total + dot_t(w[:, c], r)
        return total

    sketch = None
    for (gate_ref, up_ref), compressor in zip(weights, compressors):
        gate, up = product(gate_ref), product(up_ref)
        hidden = gate / (1.0 + jnp.exp(-gate)) * up
        hidden = jnp.where(seat < LOCAL_SEATS, hidden, 0.0).astype(BF16)
        term = dot(compressor, hidden)
        sketch = term if sketch is None else sketch + term
    return sketch


def own_kernel(n_blocks, *refs):
    weights = (refs[0:2], refs[2:4])
    compressor_ref, block_refs = refs[4], refs[5 : 5 + n_blocks]
    sketch_ref, grads_ref, *chosen_refs = refs[5 + n_blocks :]
    units, width = weights[0][0].shape
    chosen = pair_compressors(compressor_ref, units)
    for ref, value in zip(chosen_refs, chosen):
        ref[...] = value
    grads_ref[...] = jnp.concatenate([r[:, width * LOCAL_SEATS // ROWS :] for r in block_refs], axis=0)
    sketch_ref[...] = sketch_of(weights, chosen, block_refs)


def far_kernel(n_blocks, *refs):
    weights = (refs[0:2], refs[2:4])
    chosen = [r[...] for r in refs[4:6]]
    refs[-1][...] = sketch_of(weights, chosen, refs[6 : 6 + n_blocks]).astype(refs[-1].dtype)


def outer_kernel(grads_ref, *refs):
    partial_refs, out_ref = refs[:-1], refs[-1]
    total = partial_refs[0][...]
    for r in partial_refs[1:]:
        total = total + r[...].astype(F32)
    rank = total.shape[0]
    product = dot(total.astype(BF16), grads_ref[...])
    even, odd = product[: rank // 2], product[rank // 2 :]
    for n in range(EX_DEV):
        columns = slice(n * rank, (n + 1) * rank)
        out_ref[n] = jnp.concatenate([even[:, columns], odd[:, columns]], axis=1)


VMEM = pl.BlockSpec(memory_space=pltpu.VMEM)
SMEM = pl.BlockSpec(memory_space=pltpu.SMEM)
HBM = pl.BlockSpec(memory_space=pltpu.HBM)


def call(kernel, out_shape, in_specs, limit, flops=0, moved=0, scratch=()):
    return pl.pallas_call(
        kernel,
        out_shape=out_shape,
        in_specs=in_specs,
        out_specs=jax.tree.map(lambda _: VMEM, out_shape),
        scratch_shapes=list(scratch),
        compiler_params=pltpu.CompilerParams(vmem_limit_bytes=limit),
        cost_estimate=pl.CostEstimate(flops=flops, bytes_accessed=moved, transcendentals=0),
    )


def swap(a, axis, q):
    n = lax.axis_size(axis)
    return lax.ppermute(a, axis, [(i, i ^ q) for i in range(n)])


def body(
    layer_inflows,
    output_derivatives,
    picked_specialists,
    dispatch_shares,
    item_sample,
    send_limits,
    gating_projection,
    raising_projection,
    inflow_compressor,
    outgrad_compressor,
):
    n_exp, n_dp = lax.axis_size("exp"), lax.axis_size("dp")
    small = n_exp <= 8
    tokens, width = layer_inflows.shape
    rank = outgrad_compressor.shape[1]
    packed = width * LOCAL_SEATS // ROWS
    units = gating_projection.shape[2]
    size = n_exp * ROWS
    shape = jax.ShapeDtypeStruct

    gate, up = gating_projection[0].T, raising_projection[0].T
    pair_gate, pair_up = swap(gate, "dp", 1), swap(up, "dp", 1)
    weights = (gate, up, pair_gate, pair_up)

    arguments = (
        send_limits,
        picked_specialists.T,
        dispatch_shares.T,
        item_sample.reshape(1, tokens),
        layer_inflows,
        output_derivatives,
        outgrad_compressor.T,
    )
    spaces = [pltpu.SMEM] + [pltpu.VMEM] * (len(arguments) - 1)
    rows = call(
        functools.partial(send_kernel, n_exp),
        [shape((ROWS, packed + EX_DEV * rank), BF16)] * n_exp,
        [HBM] * len(arguments),
        60 * MIB,
        flops=4 * size * tokens * packed + 2 * tokens * width * rank,
        moved=4 * tokens * width + 2 * rank * width,
        scratch=[space(a.shape, a.dtype) for space, a in zip(spaces, arguments)]
        + [pltpu.SemaphoreType.DMA((len(arguments),))],
    )(*arguments)
    rows = [rows[0]] + [swap(rows[q], "exp", q) for q in range(1, n_exp)]

    blocks = {0: rows if small else [jnp.concatenate(rows, axis=0)]}
    step = n_dp // 2
    while step > 1:
        for d in list(blocks):
            blocks[d ^ step] = [swap(r, "dp", step) for r in blocks[d]]
        step //= 2

    cost = dict(flops=8 * size * width * units, moved=8 * width * units + 2 * size * packed)
    chosen_shape = shape((rank, units), BF16)
    own, grads, *chosen = call(
        functools.partial(own_kernel, len(blocks[0])),
        [shape((rank, size), F32), shape((size, EX_DEV * rank), BF16), chosen_shape, chosen_shape],
        [VMEM] * (5 + len(blocks[0])),
        20 * MIB,
        **cost,
    )(*weights, inflow_compressor.T, *blocks[0])
    partials = [own]
    for d in sorted(blocks):
        if d:
            far = call(
                functools.partial(far_kernel, len(blocks[d])),
                shape((rank, size), BF16),
                [VMEM] * (6 + len(blocks[d])),
                20 * MIB,
                **cost,
            )(*weights, *chosen, *blocks[d])
            partials.append(swap(far, "dp", d))
    out = call(
        outer_kernel,
        shape((EX_DEV, rank * rank // 128, 128), F32),
        [VMEM] * (1 + len(partials)),
        8 * MIB,
        flops=2 * size * rank * 2 * rank,
        moved=4 * EX_DEV * rank * rank,
    )(grads, *partials)
    return out.reshape(EX_DEV, 1, rank * rank)


def solution(mesh):
    in_specs = (
        P(("grp", "exp", "dp"), None),
        P(("grp", "exp", "dp"), None),
        P(("grp", "exp", "dp"), None),
        P(("grp", "exp", "dp"), None),
        P(("grp", "exp", "dp")),
        P("grp"),
        P("exp", None, "dp"),
        P("exp", None, "dp"),
        P(),
        P(),
    )
    out_specs = P(("grp", "dp"), "exp", None)
    return jax.shard_map(body, mesh=mesh, in_specs=in_specs, out_specs=out_specs, check_vma=False)
```

```python
import functools

import jax
import jax.numpy as jnp
from jax import lax
from jax.experimental import pallas as pl
from jax.experimental.pallas import tpu as pltpu
from jax.sharding import PartitionSpec as P

EX_DEV = 2
LOCAL_SEATS = 12
ROWS = 16
SPARE = ROWS - LOCAL_SEATS
PARTS = LOCAL_SEATS // SPARE
HALF = ROWS // 2
MIB = 1024 * 1024
SEND_LIMIT = 56
OWN_LIMIT = 20
BF16 = jnp.bfloat16
F32 = jnp.float32


def dot(a, b):
    return jnp.dot(a, b, preferred_element_type=F32)


def dot_t(a, b):
    return lax.dot_general(a, b, (((1,), (1,)), ((), ())), preferred_element_type=F32)


def one_hot(mask):
    return mask.astype(F32).astype(BF16)


def seats_of(limits_ref, picked, experts):
    tokens = picked.shape[1]
    flags = [jnp.max((picked == e).astype(F32), axis=0, keepdims=True) for e in experts]
    flags = jnp.concatenate(flags, axis=0)
    earlier = lax.broadcasted_iota(jnp.int32, (tokens, tokens), 0)
    later = lax.broadcasted_iota(jnp.int32, (tokens, tokens), 1)
    position = dot(flags.astype(BF16), one_hot(earlier < later)).astype(jnp.int32)
    rows = []
    for i, e in enumerate(experts):
        limit = jnp.minimum(limits_ref[e], LOCAL_SEATS)
        at = position[i : i + 1]
        rows.append(jnp.where((flags[i : i + 1] > 0.0) & (at < limit), at, -1))
    return rows


def send_kernel(count, limits_hbm, picked_hbm, shares_hbm, owner_hbm, tokens_hbm, derivs_hbm, compressor_hbm, *refs):
    out_refs = refs[:count]
    limits_ref, picked_ref, shares_ref, owner_ref, tokens_ref, derivs_ref, compressor_ref, sems = (
        refs[count:]
    )
    tokens, width = tokens_ref.shape
    chunk = width // (PARTS + 1)
    columns = [slice(i * chunk, (i + 1) * chunk) for i in range(PARTS + 1)]
    pairs = [
        (limits_hbm, limits_ref),
        (picked_hbm, picked_ref),
        (shares_hbm, shares_ref),
        (owner_hbm, owner_ref),
        (tokens_hbm, tokens_ref),
        (derivs_hbm, derivs_ref),
        (compressor_hbm, compressor_ref),
    ]
    copies = [pltpu.make_async_copy(a, b, sems.at[i]) for i, (a, b) in enumerate(pairs)]
    for copy in copies:
        copy.start()
    for copy in copies[:4]:
        copy.wait()
    me = lax.axis_index("exp")
    experts = [jnp.bitwise_xor(me, q) for q in range(count)]
    picked = picked_ref[...]
    seats = seats_of(limits_ref, picked, experts)
    slot = lax.broadcasted_iota(jnp.int32, (ROWS, tokens), 0)
    near = jnp.concatenate([one_hot(slot == s) for s in seats], axis=0)
    masks = []
    for i in range(PARTS):
        shifted = jnp.where(slot >= LOCAL_SEATS, slot - LOCAL_SEATS + SPARE * i, -2)
        far = jnp.concatenate([one_hot(shifted == s) for s in seats], axis=0)
        masks.append(jnp.concatenate([near, far], axis=1))
    owner = owner_ref[...] - lax.axis_index("dp") * EX_DEV
    owned = [
        jnp.concatenate([one_hot((slot == s) & (owner == n)) for n in range(EX_DEV)], axis=0)
        for s in seats
    ]
    share_rows = [
        jnp.sum(jnp.where(picked == e, shares_ref[...], 0.0), axis=0, keepdims=True)
        for e in experts
    ]
    pad = [jnp.zeros((-count % 8, tokens), F32)] if count % 8 else []
    shares = jnp.concatenate(share_rows + pad, axis=0).T
    for copy in copies[4:]:
        copy.wait()
    proj = dot_t(derivs_ref[...], compressor_ref[...])
    last = tokens_ref[:, columns[-1]]
    for i in range(PARTS):
        source = jnp.concatenate([tokens_ref[:, columns[i]], last], axis=0)
        packed = dot(masks[i], source).astype(BF16)
        for q in range(count):
            out_refs[q][:, columns[i]] = packed[q * ROWS : (q + 1) * ROWS]
    for q in range(count):
        grad = (shares[:, q : q + 1] * proj).astype(BF16)
        both = dot(owned[q], grad)
        halves = [both[n * ROWS : (n + 1) * ROWS] for n in range(EX_DEV)]
        out_refs[q][:, PARTS * chunk :] = jnp.concatenate(halves, axis=1).astype(BF16)


def pair_compressor(compressor_ref, units):
    place = lax.axis_index("dp")
    rank, total = compressor_ref.shape
    to = lax.broadcasted_iota(jnp.int32, (rank, rank), 0)
    at = lax.broadcasted_iota(jnp.int32, (rank, rank), 1)
    order = one_hot(at == jnp.where(to < rank // 2, 2 * to, 2 * to - rank + 1))
    turned = dot(order, compressor_ref[...]).astype(BF16)
    line = lax.broadcasted_iota(jnp.int32, (total, 2 * units), 0)
    unit = lax.broadcasted_iota(jnp.int32, (total, 2 * units), 1)
    pair = jnp.bitwise_xor(place, 1)
    wanted = jnp.where(unit < units, place * units + unit, (pair - 1) * units + unit)
    return dot(turned, one_hot(line == wanted)).astype(BF16)


def sketch_of(weights_ref, compressor, block_refs, ready=lambda i: None):
    chunk = weights_ref.shape[1] // (PARTS + 1)
    size = sum(r.shape[0] for r in block_refs)
    messages = size // ROWS
    low = lax.broadcasted_iota(jnp.int32, (1, HALF, 1), 1) < SPARE
    columns = [slice(i * chunk, (i + 1) * chunk) for i in range(PARTS + 1)]
    rows = [jnp.concatenate([r[:, c] for r in block_refs], axis=0) for c in columns[:PARTS]]
    tails = [r.astype(F32).reshape(messages, 2, HALF, chunk)[:, 1] for r in rows]

    def turn(a):
        return jnp.concatenate([a[:, SPARE:], a[:, :SPARE]], axis=1)

    top = jnp.where(low, turn(tails[0]), tails[1])
    bottom = jnp.where(low, turn(tails[2]), 0.0)
    rows.append(jnp.stack([top, bottom], axis=1).reshape(size, chunk).astype(BF16))
    total = None
    for i, r in enumerate(rows):
        ready(i)
        term = dot_t(r, weights_ref[:, columns[i]])
        total = term if total is None else total + term
    half = total.shape[1] // 2
    gate, up = total[:, :half], total[:, half:]
    hidden = gate / (1.0 + jnp.exp(-gate)) * up
    seat = lax.broadcasted_iota(jnp.int32, (size, 1), 0) % ROWS
    hidden = jnp.where(seat < LOCAL_SEATS, hidden, 0.0).astype(BF16)
    return dot_t(compressor, hidden)


def own_kernel(gate_hbm, pair_gate_hbm, up_hbm, pair_up_hbm, compressor_ref, *refs):
    block_refs, (sketch_ref, grads_ref, chosen_ref, weights_ref, sems) = refs[:-5], refs[-5:]
    units, width = gate_hbm.shape
    chunk = width // (PARTS + 1)
    copies = []
    for i in range(PARTS + 1):
        columns = pl.ds(i * chunk, chunk)
        for k, source in enumerate((gate_hbm, pair_gate_hbm, up_hbm, pair_up_hbm)):
            target = weights_ref.at[pl.ds(k * units, units), columns]
            copies.append(
                pltpu.make_async_copy(source.at[:, columns], target, sems.at[len(copies)])
            )
    for copy in copies:
        copy.start()
    chosen = pair_compressor(compressor_ref, units)
    chosen_ref[...] = chosen
    grads_ref[...] = jnp.concatenate([r[:, PARTS * chunk :] for r in block_refs], axis=0)

    def ready(i):
        for copy in copies[4 * i : 4 * i + 4]:
            copy.wait()

    sketch_ref[...] = sketch_of(weights_ref, chosen, block_refs, ready)


def far_kernel(weights_ref, chosen_ref, *refs):
    refs[-1][...] = sketch_of(weights_ref, chosen_ref[...], refs[:-1]).astype(refs[-1].dtype)


def outer_kernel(grads_ref, *refs):
    partial_refs, out_ref = refs[:-1], refs[-1]
    total = partial_refs[0][...]
    for r in partial_refs[1:]:
        total = total + r[...].astype(F32)
    rank = total.shape[0]
    product = dot(total.astype(BF16), grads_ref[...])
    even, odd = product[: rank // 2], product[rank // 2 :]
    for n in range(EX_DEV):
        columns = slice(n * rank, (n + 1) * rank)
        out_ref[n] = jnp.concatenate([even[:, columns], odd[:, columns]], axis=1)


VMEM = pl.BlockSpec(memory_space=pltpu.VMEM)
SMEM = pl.BlockSpec(memory_space=pltpu.SMEM)
HBM = pl.BlockSpec(memory_space=pltpu.HBM)


def call(kernel, out_shape, in_specs, limit, flops=0, moved=0, scratch=()):
    return pl.pallas_call(
        kernel,
        out_shape=out_shape,
        in_specs=in_specs,
        out_specs=jax.tree.map(lambda _: VMEM, out_shape),
        scratch_shapes=list(scratch),
        compiler_params=pltpu.CompilerParams(vmem_limit_bytes=limit),
        cost_estimate=pl.CostEstimate(flops=flops, bytes_accessed=moved, transcendentals=0),
    )


def swap(a, axis, q):
    n = lax.axis_size(axis)
    return lax.ppermute(a, axis, [(i, i ^ q) for i in range(n)])


def body(
    layer_inflows,
    output_derivatives,
    picked_specialists,
    dispatch_shares,
    item_sample,
    send_limits,
    gating_projection,
    raising_projection,
    inflow_compressor,
    outgrad_compressor,
):
    n_exp, n_dp = lax.axis_size("exp"), lax.axis_size("dp")
    small = n_exp <= 8
    tokens, width = layer_inflows.shape
    rank = outgrad_compressor.shape[1]
    packed = width * LOCAL_SEATS // ROWS
    units = gating_projection.shape[2]
    size = n_exp * ROWS
    shape = jax.ShapeDtypeStruct

    gate, up = gating_projection[0].T, raising_projection[0].T
    pair_gate, pair_up = swap(gate, "dp", 1), swap(up, "dp", 1)
    arguments = (
        send_limits,
        picked_specialists.T,
        dispatch_shares.T,
        item_sample.reshape(1, tokens),
        layer_inflows,
        output_derivatives,
        outgrad_compressor.T,
    )
    spaces = [pltpu.SMEM] + [pltpu.VMEM] * (len(arguments) - 1)
    rows = call(
        functools.partial(send_kernel, n_exp),
        [shape((ROWS, packed + EX_DEV * rank), BF16)] * n_exp,
        [HBM] * len(arguments),
        SEND_LIMIT * MIB,
        flops=4 * size * tokens * packed + 2 * tokens * width * rank,
        moved=4 * tokens * width + 2 * rank * width,
        scratch=[space(a.shape, a.dtype) for space, a in zip(spaces, arguments)]
        + [pltpu.SemaphoreType.DMA((len(arguments),))],
    )(*arguments)
    hold = lax.optimization_barrier
    order = [n_exp - 1] + list(range(1, n_exp - 1))
    half = n_dp // 2
    rows = list(rows)
    pair_gate, pair_up, rows[0] = hold((pair_gate, pair_up, rows[0]))
    moved = {q: swap(rows[q], "exp", q) for q in order}
    rows[order[0]] = moved[order[0]]
    for q, r in zip(order, order[1:]):
        rows[q], rows[r] = hold((rows[q], moved[r]))
    if small:
        crossed = {q: swap(rows[q], "dp", half) for q in [0] + order[:-1]}
        last = order[-1]
        crossed[0], crossed[order[0]], rows[last] = hold((crossed[0], crossed[order[0]], rows[last]))
        crossed[last] = swap(rows[last], "dp", half)
        crossed = [crossed[q] for q in range(n_exp)]
    else:
        rows = [jnp.concatenate(rows, axis=0)]
        crossed = [swap(rows[0], "dp", half)]
    blocks = {0: rows, half: crossed}
    step = half // 2
    while step > 1:
        for d in list(blocks):
            blocks[d ^ step] = [swap(r, "dp", step) for r in blocks[d]]
        step //= 2

    cost = dict(flops=8 * size * width * units, moved=8 * width * units + 2 * size * packed)
    own, grads, chosen, weights = call(
        own_kernel,
        [
            shape((rank, size), F32),
            shape((size, EX_DEV * rank), BF16),
            shape((rank, 2 * units), BF16),
            shape((4 * units, width), BF16),
        ],
        [HBM] * 4 + [VMEM] * (1 + len(rows)),
        OWN_LIMIT * MIB,
        **cost,
        scratch=[pltpu.SemaphoreType.DMA((4 * (PARTS + 1),))],
    )(gate, pair_gate, up, pair_up, inflow_compressor.T, *rows)
    partials = [own]
    for d in sorted(blocks):
        if d:
            far = call(
                far_kernel,
                shape((rank, size), BF16),
                [VMEM] * (2 + len(blocks[d])),
                20 * MIB,
                **cost,
            )(weights, chosen, *blocks[d])
            partials.append(swap(far, "dp", d))
    out = call(
        outer_kernel,
        shape((EX_DEV, rank * rank // 128, 128), F32),
        [VMEM] * (1 + len(partials)),
        8 * MIB,
        flops=2 * size * rank * 2 * rank,
        moved=4 * EX_DEV * rank * rank,
    )(grads, *partials)
    return out.reshape(EX_DEV, 1, rank * rank)


def solution(mesh):
    in_specs = (
        P(("grp", "exp", "dp"), None),
        P(("grp", "exp", "dp"), None),
        P(("grp", "exp", "dp"), None),
        P(("grp", "exp", "dp"), None),
        P(("grp", "exp", "dp")),
        P("grp"),
        P("exp", None, "dp"),
        P("exp", None, "dp"),
        P(),
        P(),
    )
    out_specs = P(("grp", "dp"), "exp", None)
    return jax.shard_map(body, mesh=mesh, in_specs=in_specs, out_specs=out_specs, check_vma=False)
```

```python
import functools

import jax
import jax.numpy as jnp
from jax import lax
from jax.experimental import pallas as pl
from jax.experimental.pallas import tpu as pltpu
from jax.sharding import PartitionSpec as P

EX_DEV = 2
LOCAL_SEATS = 12
ROWS = 16
SPARE = ROWS - LOCAL_SEATS
PARTS = LOCAL_SEATS // SPARE
HALF = ROWS // 2
MIB = 1024 * 1024
KEEP_LIMIT = 48
SEND_LIMIT = 56
BF16 = jnp.bfloat16
F32 = jnp.float32


def dot(a, b):
    return jnp.dot(a, b, preferred_element_type=F32)


def dot_t(a, b):
    return lax.dot_general(a, b, (((1,), (1,)), ((), ())), preferred_element_type=F32)


def one_hot(mask):
    return mask.astype(F32).astype(BF16)


def seats_of(limits_ref, picked, experts):
    tokens = picked.shape[1]
    flags = [jnp.max((picked == e).astype(F32), axis=0, keepdims=True) for e in experts]
    flags = jnp.concatenate(flags, axis=0)
    earlier = lax.broadcasted_iota(jnp.int32, (tokens, tokens), 0)
    later = lax.broadcasted_iota(jnp.int32, (tokens, tokens), 1)
    position = dot(flags.astype(BF16), one_hot(earlier < later)).astype(jnp.int32)
    rows = []
    for i, e in enumerate(experts):
        limit = jnp.minimum(limits_ref[e], LOCAL_SEATS)
        at = position[i : i + 1]
        rows.append(jnp.where((flags[i : i + 1] > 0.0) & (at < limit), at, -1))
    return rows


def send_kernel(hops, *refs):
    count = len(hops)
    in_refs, (gate_hbm, up_hbm), refs = refs[:7], refs[7:9], refs[9:]
    out_refs, weights_ref, scratch, sems = refs[:count], refs[count], refs[count + 1 : -1], refs[-1]
    limits_ref, picked_ref, shares_ref, owner_ref, tokens_ref, derivs_ref, compressor_ref = scratch
    units = gate_hbm.shape[0]
    tokens, width = tokens_ref.shape
    chunk = width // (PARTS + 1)
    columns = [slice(i * chunk, (i + 1) * chunk) for i in range(PARTS + 1)]
    pairs = list(zip(in_refs, scratch)) + [
        (gate_hbm, weights_ref.at[:units]),
        (up_hbm, weights_ref.at[units:]),
    ]
    copies = [pltpu.make_async_copy(a, b, sems.at[i]) for i, (a, b) in enumerate(pairs)]
    for copy in copies:
        copy.start()
    for copy in copies[:4]:
        copy.wait()
    me = lax.axis_index("exp")
    experts = [jnp.bitwise_xor(me, q) for q in hops]
    picked = picked_ref[...]
    seats = seats_of(limits_ref, picked, experts)
    slot = lax.broadcasted_iota(jnp.int32, (ROWS, tokens), 0)
    near = jnp.concatenate([one_hot(slot == s) for s in seats], axis=0)
    masks = []
    for i in range(PARTS):
        shifted = jnp.where(slot >= LOCAL_SEATS, slot - LOCAL_SEATS + SPARE * i, -2)
        far = jnp.concatenate([one_hot(shifted == s) for s in seats], axis=0)
        masks.append(jnp.concatenate([near, far], axis=1))
    owner = owner_ref[...] - lax.axis_index("dp") * EX_DEV
    owned = [
        jnp.concatenate([one_hot((slot == s) & (owner == n)) for n in range(EX_DEV)], axis=0)
        for s in seats
    ]
    share_rows = [
        jnp.sum(jnp.where(picked == e, shares_ref[...], 0.0), axis=0, keepdims=True)
        for e in experts
    ]
    pad = [jnp.zeros((-count % 8, tokens), F32)] if count % 8 else []
    shares = jnp.concatenate(share_rows + pad, axis=0).T
    for copy in copies[4:7]:
        copy.wait()
    proj = dot_t(derivs_ref[...], compressor_ref[...])
    last = tokens_ref[:, columns[-1]]
    for i in range(PARTS):
        source = jnp.concatenate([tokens_ref[:, columns[i]], last], axis=0)
        packed = dot(masks[i], source).astype(BF16)
        for q in range(count):
            out_refs[q][:, columns[i]] = packed[q * ROWS : (q + 1) * ROWS]
    for q in range(count):
        grad = (shares[:, q : q + 1] * proj).astype(BF16)
        both = dot(owned[q], grad)
        halves = [both[n * ROWS : (n + 1) * ROWS] for n in range(EX_DEV)]
        out_refs[q][:, PARTS * chunk :] = jnp.concatenate(halves, axis=1).astype(BF16)
    for copy in copies[7:]:
        copy.wait()


def keep_kernel(compressor_ref, weights_hbm, rows_hbm, *refs):
    weights_ref, rows_ref, first_ref, second_ref, sems = refs
    copies = [
        pltpu.make_async_copy(weights_hbm, weights_ref, sems.at[0]),
        pltpu.make_async_copy(rows_hbm, rows_ref, sems.at[1]),
    ]
    for copy in copies:
        copy.start()
    chosen = chosen_compressors(compressor_ref, first_ref.shape[1])
    first_ref[...], second_ref[...] = chosen
    for copy in copies:
        copy.wait()


def chosen_compressors(compressor_ref, units):
    place = lax.axis_index("dp")
    rank, total = compressor_ref.shape
    to = lax.broadcasted_iota(jnp.int32, (rank, rank), 0)
    at = lax.broadcasted_iota(jnp.int32, (rank, rank), 1)
    order = one_hot(at == jnp.where(to < rank // 2, 2 * to, 2 * to - rank + 1))
    turned = dot(order, compressor_ref[...]).astype(BF16)
    line = lax.broadcasted_iota(jnp.int32, (total, units), 0)
    unit = lax.broadcasted_iota(jnp.int32, (total, units), 1)
    return [
        dot(turned, one_hot(line == unit + jnp.bitwise_xor(place, k) * units)).astype(BF16)
        for k in range(2)
    ]


def sketch_kernel(sizes, own_ref, pair_ref, first_ref, second_ref, *refs):
    out_refs, grads_ref = refs[-1 - len(sizes) : -1], refs[-1]
    block_refs = refs[: -1 - len(sizes)]
    units, width = own_ref.shape[0] // 2, own_ref.shape[1]
    chunk = width // (PARTS + 1)
    size = sum(sizes)
    messages = size // ROWS
    low = lax.broadcasted_iota(jnp.int32, (1, HALF, 1), 1) < SPARE
    columns = [slice(i * chunk, (i + 1) * chunk) for i in range(PARTS + 1)]
    rows = [jnp.concatenate([r[:, c] for r in block_refs], axis=0) for c in columns[:PARTS]]
    tails = [r.astype(F32).reshape(messages, 2, HALF, chunk)[:, 1] for r in rows]

    def turn(a):
        return jnp.concatenate([a[:, SPARE:], a[:, :SPARE]], axis=1)

    top = jnp.where(low, turn(tails[0]), tails[1])
    bottom = jnp.where(low, turn(tails[2]), 0.0)
    rows.append(jnp.stack([top, bottom], axis=1).reshape(size, chunk).astype(BF16))
    seat = lax.broadcasted_iota(jnp.int32, (size, 1), 0) % ROWS

    def product(w, lines):
        total = dot_t(rows[0], w[lines, columns[0]])
        for c, r in zip(columns[1:], rows[1:]):
            total = total + dot_t(r, w[lines, c])
        return total

    sketch = None
    for ref, compressor in ((own_ref, first_ref), (pair_ref, second_ref)):
        gate, up = product(ref, slice(0, units)), product(ref, slice(units, 2 * units))
        hidden = gate / (1.0 + jnp.exp(-gate)) * up
        hidden = jnp.where(seat < LOCAL_SEATS, hidden, 0.0).astype(BF16)
        term = dot_t(compressor[...], hidden)
        sketch = term if sketch is None else sketch + term
    at = 0
    for n, ref in zip(sizes, out_refs):
        ref[...] = sketch[:, at : at + n].astype(ref.dtype)
        at += n
    first = 0
    for r in block_refs:
        if first < sizes[0]:
            grads_ref[first : first + r.shape[0]] = r[:, PARTS * chunk :]
        first += r.shape[0]


def outer_kernel(grads_ref, *refs):
    partial_refs, out_ref = refs[:-1], refs[-1]
    total = partial_refs[0][...]
    for r in partial_refs[1:]:
        total = total + r[...].astype(F32)
    rank = total.shape[0]
    product = dot(total.astype(BF16), grads_ref[...])
    even, odd = product[: rank // 2], product[rank // 2 :]
    for n in range(EX_DEV):
        columns = slice(n * rank, (n + 1) * rank)
        out_ref[n] = jnp.concatenate([even[:, columns], odd[:, columns]], axis=1)


VMEM = pl.BlockSpec(memory_space=pltpu.VMEM)
SMEM = pl.BlockSpec(memory_space=pltpu.SMEM)
HBM = pl.BlockSpec(memory_space=pltpu.HBM)
ANY = pl.BlockSpec(memory_space=pl.ANY)


def call(kernel, out_shape, in_specs, limit, flops=0, moved=0, scratch=(), out_specs=None):
    return pl.pallas_call(
        kernel,
        out_shape=out_shape,
        in_specs=in_specs,
        out_specs=out_specs or jax.tree.map(lambda _: VMEM, out_shape),
        scratch_shapes=list(scratch),
        compiler_params=pltpu.CompilerParams(vmem_limit_bytes=limit),
        cost_estimate=pl.CostEstimate(flops=flops, bytes_accessed=moved, transcendentals=0),
    )


def swap(a, axis, q):
    n = lax.axis_size(axis)
    return lax.ppermute(a, axis, [(i, i ^ q) for i in range(n)])


def body(
    layer_inflows,
    output_derivatives,
    picked_specialists,
    dispatch_shares,
    item_sample,
    send_limits,
    gating_projection,
    raising_projection,
    inflow_compressor,
    outgrad_compressor,
):
    n_exp, n_dp = lax.axis_size("exp"), lax.axis_size("dp")
    small = n_exp <= 8
    tokens, width = layer_inflows.shape
    rank = outgrad_compressor.shape[1]
    packed = width * LOCAL_SEATS // ROWS
    units = gating_projection.shape[2]
    size = n_exp * ROWS
    shape = jax.ShapeDtypeStruct

    gate, up = gating_projection[0].T, raising_projection[0].T
    arguments = (
        send_limits,
        picked_specialists.T,
        dispatch_shares.T,
        item_sample.reshape(1, tokens),
        layer_inflows,
        output_derivatives,
        outgrad_compressor.T,
    )
    hops = [0, n_exp - 1] + list(range(1, n_exp - 1))
    spaces = [pltpu.SMEM] + [pltpu.VMEM] * (len(arguments) - 1)
    *rows, weights = call(
        functools.partial(send_kernel, hops),
        [shape((ROWS, packed + EX_DEV * rank), BF16)] * n_exp + [shape((2 * units, width), BF16)],
        [HBM] * (len(arguments) + 2),
        SEND_LIMIT * MIB,
        out_specs=[VMEM] * n_exp + [ANY],
        flops=4 * size * tokens * packed + 2 * tokens * width * rank,
        moved=4 * tokens * width + 2 * rank * width + 8 * units * width,
        scratch=[space(a.shape, a.dtype) for space, a in zip(spaces, arguments)]
        + [pltpu.SemaphoreType.DMA((len(arguments) + 2,))],
    )(*arguments, gate, up)
    pair_weights = swap(weights, "dp", 1)

    half = n_dp // 2
    crossed = [swap(rows[0], "dp", half)]
    chosen_shape = shape((rank, units), BF16)
    weights, rows[0], *chosen = call(
        keep_kernel,
        [shape(weights.shape, BF16), shape(rows[0].shape, BF16), chosen_shape, chosen_shape],
        [VMEM, ANY, ANY],
        KEEP_LIMIT * MIB,
        out_specs=[ANY, ANY, VMEM, VMEM],
        moved=8 * units * width,
        scratch=[pltpu.SemaphoreType.DMA((2,))],
    )(inflow_compressor.T, weights, rows[0])
    for i, q in enumerate(hops):
        if i:
            rows[i] = swap(rows[i], "exp", q)
            if i == 1:
                rows[i], weights = lax.optimization_barrier((rows[i], weights))
            crossed.append(swap(rows[i], "dp", half))
    blocks = {0: rows, half: crossed}
    step = half // 2
    while step > 1:
        for d in list(blocks):
            blocks[d ^ step] = [swap(r, "dp", step) for r in blocks[d]]
        step //= 2

    partials, grads = [], None
    ends = sorted(blocks)
    for ds in [ends] if small else [[d] for d in ends]:
        parts = [r for d in ds for r in blocks[d]]
        *made, first = call(
            functools.partial(sketch_kernel, [size] * len(ds)),
            [shape((rank, size), BF16 if d else F32) for d in ds]
            + [shape((size, EX_DEV * rank), BF16)],
            [VMEM] * (4 + len(parts)),
            20 * MIB,
            flops=8 * len(ds) * size * width * units,
            moved=8 * width * units + 2 * len(ds) * size * packed,
        )(weights, pair_weights, *chosen, *parts)
        grads = first if grads is None else grads
        partials += [swap(p, "dp", d) if d else p for d, p in zip(ds, made)]
    out = call(
        outer_kernel,
        shape((EX_DEV, rank * rank // 128, 128), F32),
        [VMEM] * (1 + len(partials)),
        8 * MIB,
        flops=2 * size * rank * 2 * rank,
        moved=4 * EX_DEV * rank * rank,
    )(grads, *partials)
    return out.reshape(EX_DEV, 1, rank * rank)


def solution(mesh):
    in_specs = (
        P(("grp", "exp", "dp"), None),
        P(("grp", "exp", "dp"), None),
        P(("grp", "exp", "dp"), None),
        P(("grp", "exp", "dp"), None),
        P(("grp", "exp", "dp")),
        P("grp"),
        P("exp", None, "dp"),
        P("exp", None, "dp"),
        P(),
        P(),
    )
    out_specs = P(("grp", "dp"), "exp", None)
    return jax.shard_map(body, mesh=mesh, in_specs=in_specs, out_specs=out_specs, check_vma=False)
```

```python
import functools

import jax
import jax.numpy as jnp
from jax import lax
from jax.experimental import pallas as pl
from jax.experimental.pallas import tpu as pltpu
from jax.sharding import PartitionSpec as P

EX_DEV = 2
LOCAL_SEATS = 12
ROWS = 16
SPARE = ROWS - LOCAL_SEATS
PARTS = LOCAL_SEATS // SPARE
HALF = ROWS // 2
MIB = 1024 * 1024
KEEP_LIMIT = 48
SEND_LIMIT = 56
BF16 = jnp.bfloat16
F32 = jnp.float32


def dot(a, b):
    return jnp.dot(a, b, preferred_element_type=F32)


def dot_t(a, b):
    return lax.dot_general(a, b, (((1,), (1,)), ((), ())), preferred_element_type=F32)


def one_hot(mask):
    return mask.astype(F32).astype(BF16)


def seats_of(limits_ref, picked, experts):
    tokens = picked.shape[1]
    flags = [jnp.max((picked == e).astype(F32), axis=0, keepdims=True) for e in experts]
    flags = jnp.concatenate(flags, axis=0)
    earlier = lax.broadcasted_iota(jnp.int32, (tokens, tokens), 0)
    later = lax.broadcasted_iota(jnp.int32, (tokens, tokens), 1)
    position = dot(flags.astype(BF16), one_hot(earlier < later)).astype(jnp.int32)
    rows = []
    for i, e in enumerate(experts):
        limit = jnp.minimum(limits_ref[e], LOCAL_SEATS)
        at = position[i : i + 1]
        rows.append(jnp.where((flags[i : i + 1] > 0.0) & (at < limit), at, -1))
    return rows


def send_kernel(hops, *refs):
    count = len(hops)
    in_refs, (gate_hbm, up_hbm), refs = refs[:7], refs[7:9], refs[9:]
    out_refs, weights_ref, scratch, sems = refs[:count], refs[count], refs[count + 1 : -1], refs[-1]
    *scratch, held_ref = scratch
    limits_ref, picked_ref, shares_ref, owner_ref, tokens_ref, derivs_ref, compressor_ref = scratch
    units = gate_hbm.shape[0]
    tokens, width = tokens_ref.shape
    chunk = width // (PARTS + 1)
    columns = [slice(i * chunk, (i + 1) * chunk) for i in range(PARTS + 1)]
    pairs = list(zip(in_refs, scratch)) + [
        (gate_hbm, held_ref.at[pl.ds(0, units)]),
        (up_hbm, held_ref.at[pl.ds(units, units)]),
    ]
    copies = [pltpu.make_async_copy(a, b, sems.at[i]) for i, (a, b) in enumerate(pairs)]
    for copy in copies:
        copy.start()
    for copy in copies[:4]:
        copy.wait()
    me = lax.axis_index("exp")
    experts = [jnp.bitwise_xor(me, q) for q in hops]
    picked = picked_ref[...]
    seats = seats_of(limits_ref, picked, experts)
    slot = lax.broadcasted_iota(jnp.int32, (ROWS, tokens), 0)
    near = jnp.concatenate([one_hot(slot == s) for s in seats], axis=0)
    masks = []
    for i in range(PARTS):
        shifted = jnp.where(slot >= LOCAL_SEATS, slot - LOCAL_SEATS + SPARE * i, -2)
        far = jnp.concatenate([one_hot(shifted == s) for s in seats], axis=0)
        masks.append(jnp.concatenate([near, far], axis=1))
    owner = owner_ref[...] - lax.axis_index("dp") * EX_DEV
    owned = [
        jnp.concatenate([one_hot((slot == s) & (owner == n)) for n in range(EX_DEV)], axis=0)
        for s in seats
    ]
    share_rows = [
        jnp.sum(jnp.where(picked == e, shares_ref[...], 0.0), axis=0, keepdims=True)
        for e in experts
    ]
    pad = [jnp.zeros((-count % 8, tokens), F32)] if count % 8 else []
    shares = jnp.concatenate(share_rows + pad, axis=0).T
    for copy in copies[4:]:
        copy.wait()
    store = pltpu.make_async_copy(held_ref, weights_ref, sems.at[len(pairs)])
    store.start()
    proj = dot_t(derivs_ref[...], compressor_ref[...])
    last = tokens_ref[:, columns[-1]]
    for i in range(PARTS):
        source = jnp.concatenate([tokens_ref[:, columns[i]], last], axis=0)
        packed = dot(masks[i], source).astype(BF16)
        for q in range(count):
            out_refs[q][:, columns[i]] = packed[q * ROWS : (q + 1) * ROWS]
    for q in range(count):
        grad = (shares[:, q : q + 1] * proj).astype(BF16)
        both = dot(owned[q], grad)
        halves = [both[n * ROWS : (n + 1) * ROWS] for n in range(EX_DEV)]
        out_refs[q][:, PARTS * chunk :] = jnp.concatenate(halves, axis=1).astype(BF16)
    store.wait()


def keep_kernel(compressor_ref, weights_hbm, rows_hbm, *refs):
    weights_ref, rows_ref, first_ref, second_ref, sems = refs
    copies = [
        pltpu.make_async_copy(weights_hbm, weights_ref, sems.at[0]),
        pltpu.make_async_copy(rows_hbm, rows_ref, sems.at[1]),
    ]
    for copy in copies:
        copy.start()
    chosen = chosen_compressors(compressor_ref, first_ref.shape[1])
    first_ref[...], second_ref[...] = chosen
    for copy in copies:
        copy.wait()


def chosen_compressors(compressor_ref, units):
    place = lax.axis_index("dp")
    rank, total = compressor_ref.shape
    to = lax.broadcasted_iota(jnp.int32, (rank, rank), 0)
    at = lax.broadcasted_iota(jnp.int32, (rank, rank), 1)
    order = one_hot(at == jnp.where(to < rank // 2, 2 * to, 2 * to - rank + 1))
    turned = dot(order, compressor_ref[...]).astype(BF16)
    line = lax.broadcasted_iota(jnp.int32, (total, units), 0)
    unit = lax.broadcasted_iota(jnp.int32, (total, units), 1)
    return [
        dot(turned, one_hot(line == unit + jnp.bitwise_xor(place, k) * units)).astype(BF16)
        for k in range(2)
    ]


def sketch_kernel(sizes, own_ref, pair_ref, first_ref, second_ref, *refs):
    out_refs, grads_ref = refs[-1 - len(sizes) : -1], refs[-1]
    block_refs = refs[: -1 - len(sizes)]
    units, width = own_ref.shape[0] // 2, own_ref.shape[1]
    chunk = width // (PARTS + 1)
    size = sum(sizes)
    messages = size // ROWS
    low = lax.broadcasted_iota(jnp.int32, (1, HALF, 1), 1) < SPARE
    columns = [slice(i * chunk, (i + 1) * chunk) for i in range(PARTS + 1)]
    rows = [jnp.concatenate([r[:, c] for r in block_refs], axis=0) for c in columns[:PARTS]]
    tails = [r.astype(F32).reshape(messages, 2, HALF, chunk)[:, 1] for r in rows]

    def turn(a):
        return jnp.concatenate([a[:, SPARE:], a[:, :SPARE]], axis=1)

    top = jnp.where(low, turn(tails[0]), tails[1])
    bottom = jnp.where(low, turn(tails[2]), 0.0)
    rows.append(jnp.stack([top, bottom], axis=1).reshape(size, chunk).astype(BF16))
    seat = lax.broadcasted_iota(jnp.int32, (size, 1), 0) % ROWS

    def product(w, lines):
        total = dot_t(rows[0], w[lines, columns[0]])
        for c, r in zip(columns[1:], rows[1:]):
            total = total + dot_t(r, w[lines, c])
        return total

    sketch = None
    for ref, compressor in ((own_ref, first_ref), (pair_ref, second_ref)):
        gate, up = product(ref, slice(0, units)), product(ref, slice(units, 2 * units))
        hidden = gate / (1.0 + jnp.exp(-gate)) * up
        hidden = jnp.where(seat < LOCAL_SEATS, hidden, 0.0).astype(BF16)
        term = dot_t(compressor[...], hidden)
        sketch = term if sketch is None else sketch + term
    at = 0
    for n, ref in zip(sizes, out_refs):
        ref[...] = sketch[:, at : at + n].astype(ref.dtype)
        at += n
    first = 0
    for r in block_refs:
        if first < sizes[0]:
            grads_ref[first : first + r.shape[0]] = r[:, PARTS * chunk :]
        first += r.shape[0]


def outer_kernel(grads_ref, *refs):
    partial_refs, out_ref = refs[:-1], refs[-1]
    total = partial_refs[0][...]
    for r in partial_refs[1:]:
        total = total + r[...].astype(F32)
    rank = total.shape[0]
    product = dot(total.astype(BF16), grads_ref[...])
    even, odd = product[: rank // 2], product[rank // 2 :]
    for n in range(EX_DEV):
        columns = slice(n * rank, (n + 1) * rank)
        out_ref[n] = jnp.concatenate([even[:, columns], odd[:, columns]], axis=1)


VMEM = pl.BlockSpec(memory_space=pltpu.VMEM)
SMEM = pl.BlockSpec(memory_space=pltpu.SMEM)
HBM = pl.BlockSpec(memory_space=pltpu.HBM)
ANY = pl.BlockSpec(memory_space=pl.ANY)


def call(kernel, out_shape, in_specs, limit, flops=0, moved=0, scratch=(), out_specs=None):
    return pl.pallas_call(
        kernel,
        out_shape=out_shape,
        in_specs=in_specs,
        out_specs=out_specs or jax.tree.map(lambda _: VMEM, out_shape),
        scratch_shapes=list(scratch),
        compiler_params=pltpu.CompilerParams(vmem_limit_bytes=limit),
        cost_estimate=pl.CostEstimate(flops=flops, bytes_accessed=moved, transcendentals=0),
    )


def swap(a, axis, q):
    n = lax.axis_size(axis)
    return lax.ppermute(a, axis, [(i, i ^ q) for i in range(n)])


def body(
    layer_inflows,
    output_derivatives,
    picked_specialists,
    dispatch_shares,
    item_sample,
    send_limits,
    gating_projection,
    raising_projection,
    inflow_compressor,
    outgrad_compressor,
):
    n_exp, n_dp = lax.axis_size("exp"), lax.axis_size("dp")
    small = n_exp <= 8
    tokens, width = layer_inflows.shape
    rank = outgrad_compressor.shape[1]
    packed = width * LOCAL_SEATS // ROWS
    units = gating_projection.shape[2]
    size = n_exp * ROWS
    shape = jax.ShapeDtypeStruct

    gate, up = gating_projection[0].T, raising_projection[0].T
    arguments = (
        send_limits,
        picked_specialists.T,
        dispatch_shares.T,
        item_sample.reshape(1, tokens),
        layer_inflows,
        output_derivatives,
        outgrad_compressor.T,
    )
    hops = [0, n_exp - 1] + list(range(1, n_exp - 1))
    spaces = [pltpu.SMEM] + [pltpu.VMEM] * (len(arguments) - 1)
    *rows, weights = call(
        functools.partial(send_kernel, hops),
        [shape((ROWS, packed + EX_DEV * rank), BF16)] * n_exp + [shape((2 * units, width), BF16)],
        [HBM] * (len(arguments) + 2),
        SEND_LIMIT * MIB,
        out_specs=[VMEM] * n_exp + [ANY],
        flops=4 * size * tokens * packed + 2 * tokens * width * rank,
        moved=4 * tokens * width + 2 * rank * width + 8 * units * width,
        scratch=[space(a.shape, a.dtype) for space, a in zip(spaces, arguments)]
        + [pltpu.VMEM((2 * units, width), BF16), pltpu.SemaphoreType.DMA((len(arguments) + 3,))],
    )(*arguments, gate, up)
    pair_weights = swap(weights, "dp", 1)

    half = n_dp // 2
    crossed = [swap(rows[0], "dp", half)]
    chosen_shape = shape((rank, units), BF16)
    weights, rows[0], *chosen = call(
        keep_kernel,
        [shape(weights.shape, BF16), shape(rows[0].shape, BF16), chosen_shape, chosen_shape],
        [VMEM, ANY, ANY],
        KEEP_LIMIT * MIB,
        out_specs=[ANY, ANY, VMEM, VMEM],
        moved=8 * units * width,
        scratch=[pltpu.SemaphoreType.DMA((2,))],
    )(inflow_compressor.T, weights, rows[0])
    for i, q in enumerate(hops):
        if i:
            rows[i] = swap(rows[i], "exp", q)
            if i == 1:
                rows[i], weights = lax.optimization_barrier((rows[i], weights))
            crossed.append(swap(rows[i], "dp", half))
    blocks = {0: rows, half: crossed}
    step = half // 2
    while step > 1:
        for d in list(blocks):
            blocks[d ^ step] = [swap(r, "dp", step) for r in blocks[d]]
        step //= 2

    partials, grads = [], None
    ends = sorted(blocks)
    for ds in [ends] if small else [[d] for d in ends]:
        parts = [r for d in ds for r in blocks[d]]
        *made, first = call(
            functools.partial(sketch_kernel, [size] * len(ds)),
            [shape((rank, size), BF16 if d else F32) for d in ds]
            + [shape((size, EX_DEV * rank), BF16)],
            [VMEM] * (4 + len(parts)),
            20 * MIB,
            flops=8 * len(ds) * size * width * units,
            moved=8 * width * units + 2 * len(ds) * size * packed,
        )(weights, pair_weights, *chosen, *parts)
        grads = first if grads is None else grads
        partials += [swap(p, "dp", d) if d else p for d, p in zip(ds, made)]
    out = call(
        outer_kernel,
        shape((EX_DEV, rank * rank // 128, 128), F32),
        [VMEM] * (1 + len(partials)),
        8 * MIB,
        flops=2 * size * rank * 2 * rank,
        moved=4 * EX_DEV * rank * rank,
    )(grads, *partials)
    return out.reshape(EX_DEV, 1, rank * rank)


def solution(mesh):
    in_specs = (
        P(("grp", "exp", "dp"), None),
        P(("grp", "exp", "dp"), None),
        P(("grp", "exp", "dp"), None),
        P(("grp", "exp", "dp"), None),
        P(("grp", "exp", "dp")),
        P("grp"),
        P("exp", None, "dp"),
        P("exp", None, "dp"),
        P(),
        P(),
    )
    out_specs = P(("grp", "dp"), "exp", None)
    return jax.shard_map(body, mesh=mesh, in_specs=in_specs, out_specs=out_specs, check_vma=False)
```

```python
import functools

import jax
import jax.numpy as jnp
from jax import lax
from jax.experimental import pallas as pl
from jax.experimental.pallas import tpu as pltpu
from jax.sharding import PartitionSpec as P

EX_DEV = 2
LOCAL_SEATS = 12
ROWS = 16
SPARE = ROWS - LOCAL_SEATS
PARTS = LOCAL_SEATS // SPARE
HALF = ROWS // 2
MIB = 1024 * 1024
KEEP_LIMIT = 48
SEND_LIMIT = 56
BF16 = jnp.bfloat16
F32 = jnp.float32


def dot(a, b):
    return jnp.dot(a, b, preferred_element_type=F32)


def dot_t(a, b):
    return lax.dot_general(a, b, (((1,), (1,)), ((), ())), preferred_element_type=F32)


def one_hot(mask):
    return mask.astype(F32).astype(BF16)


def seats_of(limits_ref, picked, experts):
    tokens = picked.shape[1]
    flags = [jnp.max((picked == e).astype(F32), axis=0, keepdims=True) for e in experts]
    flags = jnp.concatenate(flags, axis=0)
    earlier = lax.broadcasted_iota(jnp.int32, (tokens, tokens), 0)
    later = lax.broadcasted_iota(jnp.int32, (tokens, tokens), 1)
    position = dot(flags.astype(BF16), one_hot(earlier < later)).astype(jnp.int32)
    rows = []
    for i, e in enumerate(experts):
        limit = jnp.minimum(limits_ref[e], LOCAL_SEATS)
        at = position[i : i + 1]
        rows.append(jnp.where((flags[i : i + 1] > 0.0) & (at < limit), at, -1))
    return rows


def send_kernel(hops, *refs):
    count = len(hops)
    in_refs, out_refs, scratch, sems = refs[:7], refs[7 : 7 + count], refs[7 + count : -1], refs[-1]
    limits_ref, picked_ref, shares_ref, owner_ref, tokens_ref, derivs_ref, compressor_ref = scratch
    tokens, width = tokens_ref.shape
    chunk = width // (PARTS + 1)
    columns = [slice(i * chunk, (i + 1) * chunk) for i in range(PARTS + 1)]
    copies = [
        pltpu.make_async_copy(a, b, sems.at[i]) for i, (a, b) in enumerate(zip(in_refs, scratch))
    ]
    for copy in copies:
        copy.start()
    for copy in copies[:4]:
        copy.wait()
    me = lax.axis_index("exp")
    experts = [jnp.bitwise_xor(me, q) for q in hops]
    picked = picked_ref[...]
    seats = seats_of(limits_ref, picked, experts)
    slot = lax.broadcasted_iota(jnp.int32, (ROWS, tokens), 0)
    near = jnp.concatenate([one_hot(slot == s) for s in seats], axis=0)
    masks = []
    for i in range(PARTS):
        shifted = jnp.where(slot >= LOCAL_SEATS, slot - LOCAL_SEATS + SPARE * i, -2)
        far = jnp.concatenate([one_hot(shifted == s) for s in seats], axis=0)
        masks.append(jnp.concatenate([near, far], axis=1))
    owner = owner_ref[...] - lax.axis_index("dp") * EX_DEV
    owned = [
        jnp.concatenate([one_hot((slot == s) & (owner == n)) for n in range(EX_DEV)], axis=0)
        for s in seats
    ]
    share_rows = [
        jnp.sum(jnp.where(picked == e, shares_ref[...], 0.0), axis=0, keepdims=True)
        for e in experts
    ]
    pad = [jnp.zeros((-count % 8, tokens), F32)] if count % 8 else []
    shares = jnp.concatenate(share_rows + pad, axis=0).T
    for copy in copies[4:]:
        copy.wait()
    proj = dot_t(derivs_ref[...], compressor_ref[...])
    last = tokens_ref[:, columns[-1]]
    for i in range(PARTS):
        source = jnp.concatenate([tokens_ref[:, columns[i]], last], axis=0)
        packed = dot(masks[i], source).astype(BF16)
        for q in range(count):
            out_refs[q][:, columns[i]] = packed[q * ROWS : (q + 1) * ROWS]
    for q in range(count):
        grad = (shares[:, q : q + 1] * proj).astype(BF16)
        both = dot(owned[q], grad)
        halves = [both[n * ROWS : (n + 1) * ROWS] for n in range(EX_DEV)]
        out_refs[q][:, PARTS * chunk :] = jnp.concatenate(halves, axis=1).astype(BF16)


def keep_kernel(compressor_ref, gate_hbm, up_hbm, rows_hbm, *refs):
    gate_ref, up_ref, rows_ref, first_ref, second_ref, sems = refs
    pairs = ((gate_hbm, gate_ref), (up_hbm, up_ref), (rows_hbm, rows_ref))
    copies = [pltpu.make_async_copy(a, b, sems.at[i]) for i, (a, b) in enumerate(pairs)]
    for copy in copies:
        copy.start()
    chosen = chosen_compressors(compressor_ref, first_ref.shape[1])
    first_ref[...], second_ref[...] = chosen
    for copy in copies:
        copy.wait()


def chosen_compressors(compressor_ref, units):
    place = lax.axis_index("dp")
    rank, total = compressor_ref.shape
    to = lax.broadcasted_iota(jnp.int32, (rank, rank), 0)
    at = lax.broadcasted_iota(jnp.int32, (rank, rank), 1)
    order = one_hot(at == jnp.where(to < rank // 2, 2 * to, 2 * to - rank + 1))
    turned = dot(order, compressor_ref[...]).astype(BF16)
    line = lax.broadcasted_iota(jnp.int32, (total, units), 0)
    unit = lax.broadcasted_iota(jnp.int32, (total, units), 1)
    return [
        dot(turned, one_hot(line == unit + jnp.bitwise_xor(place, k) * units)).astype(BF16)
        for k in range(2)
    ]


def sketch_kernel(sizes, gate_ref, up_ref, pair_gate_ref, pair_up_ref, first_ref, second_ref, *refs):
    out_refs, grads_ref = refs[-1 - len(sizes) : -1], refs[-1]
    block_refs = refs[: -1 - len(sizes)]
    units, width = gate_ref.shape
    chunk = width // (PARTS + 1)
    size = sum(sizes)
    messages = size // ROWS
    low = lax.broadcasted_iota(jnp.int32, (1, HALF, 1), 1) < SPARE
    columns = [slice(i * chunk, (i + 1) * chunk) for i in range(PARTS + 1)]
    rows = [jnp.concatenate([r[:, c] for r in block_refs], axis=0) for c in columns[:PARTS]]
    tails = [r.astype(F32).reshape(messages, 2, HALF, chunk)[:, 1] for r in rows]

    def turn(a):
        return jnp.concatenate([a[:, SPARE:], a[:, :SPARE]], axis=1)

    top = jnp.where(low, turn(tails[0]), tails[1])
    bottom = jnp.where(low, turn(tails[2]), 0.0)
    rows.append(jnp.stack([top, bottom], axis=1).reshape(size, chunk).astype(BF16))
    seat = lax.broadcasted_iota(jnp.int32, (size, 1), 0) % ROWS

    def product(w):
        total = dot_t(rows[0], w[:, columns[0]])
        for c, r in zip(columns[1:], rows[1:]):
            total = total + dot_t(r, w[:, c])
        return total

    sketch = None
    for gate_w, up_w, compressor in (
        (gate_ref, up_ref, first_ref),
        (pair_gate_ref, pair_up_ref, second_ref),
    ):
        gate, up = product(gate_w), product(up_w)
        hidden = gate / (1.0 + jnp.exp(-gate)) * up
        hidden = jnp.where(seat < LOCAL_SEATS, hidden, 0.0).astype(BF16)
        term = dot_t(compressor[...], hidden)
        sketch = term if sketch is None else sketch + term
    at = 0
    for n, ref in zip(sizes, out_refs):
        ref[...] = sketch[:, at : at + n].astype(ref.dtype)
        at += n
    first = 0
    for r in block_refs:
        if first < sizes[0]:
            grads_ref[first : first + r.shape[0]] = r[:, PARTS * chunk :]
        first += r.shape[0]


def outer_kernel(grads_ref, *refs):
    partial_refs, out_ref = refs[:-1], refs[-1]
    total = partial_refs[0][...]
    for r in partial_refs[1:]:
        total = total + r[...].astype(F32)
    rank = total.shape[0]
    product = dot(total.astype(BF16), grads_ref[...])
    even, odd = product[: rank // 2], product[rank // 2 :]
    for n in range(EX_DEV):
        columns = slice(n * rank, (n + 1) * rank)
        out_ref[n] = jnp.concatenate([even[:, columns], odd[:, columns]], axis=1)


VMEM = pl.BlockSpec(memory_space=pltpu.VMEM)
SMEM = pl.BlockSpec(memory_space=pltpu.SMEM)
HBM = pl.BlockSpec(memory_space=pltpu.HBM)
ANY = pl.BlockSpec(memory_space=pl.ANY)


def call(kernel, out_shape, in_specs, limit, flops=0, moved=0, scratch=(), out_specs=None):
    return pl.pallas_call(
        kernel,
        out_shape=out_shape,
        in_specs=in_specs,
        out_specs=out_specs or jax.tree.map(lambda _: VMEM, out_shape),
        scratch_shapes=list(scratch),
        compiler_params=pltpu.CompilerParams(vmem_limit_bytes=limit),
        cost_estimate=pl.CostEstimate(flops=flops, bytes_accessed=moved, transcendentals=0),
    )


def swap(a, axis, q):
    n = lax.axis_size(axis)
    return lax.ppermute(a, axis, [(i, i ^ q) for i in range(n)])


def body(
    layer_inflows,
    output_derivatives,
    picked_specialists,
    dispatch_shares,
    item_sample,
    send_limits,
    gating_projection,
    raising_projection,
    inflow_compressor,
    outgrad_compressor,
):
    n_exp, n_dp = lax.axis_size("exp"), lax.axis_size("dp")
    small = n_exp <= 8
    tokens, width = layer_inflows.shape
    rank = outgrad_compressor.shape[1]
    packed = width * LOCAL_SEATS // ROWS
    units = gating_projection.shape[2]
    size = n_exp * ROWS
    shape = jax.ShapeDtypeStruct

    gate, up = gating_projection[0].T, raising_projection[0].T
    pair_gate, pair_up = swap(gate, "dp", 1), swap(up, "dp", 1)
    arguments = (
        send_limits,
        picked_specialists.T,
        dispatch_shares.T,
        item_sample.reshape(1, tokens),
        layer_inflows,
        output_derivatives,
        outgrad_compressor.T,
    )
    hops = [0, 1] + list(range(n_exp - 1, 1, -1))
    spaces = [pltpu.SMEM] + [pltpu.VMEM] * (len(arguments) - 1)
    rows = call(
        functools.partial(send_kernel, hops),
        [shape((ROWS, packed + EX_DEV * rank), BF16)] * n_exp,
        [HBM] * len(arguments),
        SEND_LIMIT * MIB,
        flops=4 * size * tokens * packed + 2 * tokens * width * rank,
        moved=4 * tokens * width + 2 * rank * width,
        scratch=[space(a.shape, a.dtype) for space, a in zip(spaces, arguments)]
        + [pltpu.SemaphoreType.DMA((len(arguments),))],
    )(*arguments)

    half = n_dp // 2
    hold = lax.optimization_barrier
    rows = list(rows)
    crossed = [swap(rows[0], "dp", half)]
    pair_gate, pair_up, rows[0] = hold((pair_gate, pair_up, rows[0]))
    chosen_shape = shape((rank, units), BF16)
    gate, up, rows[0], *chosen = call(
        keep_kernel,
        [shape(a.shape, BF16) for a in (gate, up, rows[0])] + [chosen_shape] * 2,
        [VMEM, ANY, ANY, ANY],
        KEEP_LIMIT * MIB,
        out_specs=[ANY, ANY, ANY, VMEM, VMEM],
        moved=8 * units * width,
        scratch=[pltpu.SemaphoreType.DMA((3,))],
    )(inflow_compressor.T, gate, up, rows[0])
    for i, q in enumerate(hops):
        if i:
            rows[i] = swap(rows[i], "exp", q)
            if i == n_exp - 1:
                rows[i], gate, up = hold((rows[i], gate, up))
            crossed.append(swap(rows[i], "dp", half))
    blocks = {0: rows, half: crossed}
    step = half // 2
    while step > 1:
        for d in list(blocks):
            blocks[d ^ step] = [swap(r, "dp", step) for r in blocks[d]]
        step //= 2

    partials, grads = [], None
    ends = sorted(blocks)
    for ds in [ends] if small else [[d] for d in ends]:
        parts = [r for d in ds for r in blocks[d]]
        *made, first = call(
            functools.partial(sketch_kernel, [size] * len(ds)),
            [shape((rank, size), BF16 if d else F32) for d in ds]
            + [shape((size, EX_DEV * rank), BF16)],
            [VMEM] * (6 + len(parts)),
            20 * MIB,
            flops=8 * len(ds) * size * width * units,
            moved=8 * width * units + 2 * len(ds) * size * packed,
        )(gate, up, pair_gate, pair_up, *chosen, *parts)
        grads = first if grads is None else grads
        partials += [swap(p, "dp", d) if d else p for d, p in zip(ds, made)]
    out = call(
        outer_kernel,
        shape((EX_DEV, rank * rank // 128, 128), F32),
        [VMEM] * (1 + len(partials)),
        8 * MIB,
        flops=2 * size * rank * 2 * rank,
        moved=4 * EX_DEV * rank * rank,
    )(grads, *partials)
    return out.reshape(EX_DEV, 1, rank * rank)


def solution(mesh):
    in_specs = (
        P(("grp", "exp", "dp"), None),
        P(("grp", "exp", "dp"), None),
        P(("grp", "exp", "dp"), None),
        P(("grp", "exp", "dp"), None),
        P(("grp", "exp", "dp")),
        P("grp"),
        P("exp", None, "dp"),
        P("exp", None, "dp"),
        P(),
        P(),
    )
    out_specs = P(("grp", "dp"), "exp", None)
    return jax.shard_map(body, mesh=mesh, in_specs=in_specs, out_specs=out_specs, check_vma=False)
```

```python
import functools

import jax
import jax.numpy as jnp
from jax import lax
from jax.experimental import pallas as pl
from jax.experimental.pallas import tpu as pltpu
from jax.sharding import PartitionSpec as P

EX_DEV = 2
LOCAL_SEATS = 12
ROWS = 16
SPARE = ROWS - LOCAL_SEATS
PARTS = LOCAL_SEATS // SPARE
HALF = ROWS // 2
MIB = 1024 * 1024
KEEP_LIMIT = 48
PIECES = 6
SEND_LIMIT = 56
BF16 = jnp.bfloat16
F32 = jnp.float32


def dot(a, b):
    return jnp.dot(a, b, preferred_element_type=F32)


def dot_t(a, b):
    return lax.dot_general(a, b, (((1,), (1,)), ((), ())), preferred_element_type=F32)


def one_hot(mask):
    return mask.astype(F32).astype(BF16)


def seats_of(limits_ref, picked, experts):
    tokens = picked.shape[1]
    flags = [jnp.max((picked == e).astype(F32), axis=0, keepdims=True) for e in experts]
    flags = jnp.concatenate(flags, axis=0)
    earlier = lax.broadcasted_iota(jnp.int32, (tokens, tokens), 0)
    later = lax.broadcasted_iota(jnp.int32, (tokens, tokens), 1)
    position = dot(flags.astype(BF16), one_hot(earlier < later)).astype(jnp.int32)
    rows = []
    for i, e in enumerate(experts):
        limit = jnp.minimum(limits_ref[e], LOCAL_SEATS)
        at = position[i : i + 1]
        rows.append(jnp.where((flags[i : i + 1] > 0.0) & (at < limit), at, -1))
    return rows


def send_kernel(hops, *refs):
    count = len(hops)
    in_refs, (gate_hbm, up_hbm), refs = refs[:7], refs[7:9], refs[9:]
    out_refs, weights_ref, scratch, sems = refs[:count], refs[count], refs[count + 1 : -1], refs[-1]
    *scratch, held_ref = scratch
    limits_ref, picked_ref, shares_ref, owner_ref, tokens_ref, derivs_ref, compressor_ref = scratch
    units = gate_hbm.shape[0]
    tokens, width = tokens_ref.shape
    chunk = width // (PARTS + 1)
    columns = [slice(i * chunk, (i + 1) * chunk) for i in range(PARTS + 1)]
    copies = [
        pltpu.make_async_copy(a, b, sems.at[i]) for i, (a, b) in enumerate(zip(in_refs, scratch))
    ]
    loads, stores = [], []
    piece = units // PIECES
    for k, source in enumerate((gate_hbm, up_hbm)):
        for j in range(PIECES):
            lines = pl.ds(k * units + j * piece, piece)
            load_sem, store_sem = [sems.at[len(copies) + len(loads) + n] for n in (0, 2 * PIECES)]
            loads.append(
                pltpu.make_async_copy(
                    source.at[pl.ds(j * piece, piece)], held_ref.at[lines], load_sem
                )
            )
            stores.append(
                pltpu.make_async_copy(held_ref.at[lines], weights_ref.at[lines], store_sem)
            )
    for copy in copies[:4] + copies[5:] + copies[4:5] + loads:
        copy.start()
    for copy in copies[:4]:
        copy.wait()
    me = lax.axis_index("exp")
    experts = [jnp.bitwise_xor(me, q) for q in hops]
    picked = picked_ref[...]
    seats = seats_of(limits_ref, picked, experts)
    slot = lax.broadcasted_iota(jnp.int32, (ROWS, tokens), 0)
    near = jnp.concatenate([one_hot(slot == s) for s in seats], axis=0)
    masks = []
    for i in range(PARTS):
        shifted = jnp.where(slot >= LOCAL_SEATS, slot - LOCAL_SEATS + SPARE * i, -2)
        far = jnp.concatenate([one_hot(shifted == s) for s in seats], axis=0)
        masks.append(jnp.concatenate([near, far], axis=1))
    owner = owner_ref[...] - lax.axis_index("dp") * EX_DEV
    owned = [
        jnp.concatenate([one_hot((slot == s) & (owner == n)) for n in range(EX_DEV)], axis=0)
        for s in seats
    ]
    share_rows = [
        jnp.sum(jnp.where(picked == e, shares_ref[...], 0.0), axis=0, keepdims=True)
        for e in experts
    ]
    pad = [jnp.zeros((-count % 8, tokens), F32)] if count % 8 else []
    shares = jnp.concatenate(share_rows + pad, axis=0).T
    for load, store in zip(loads, stores):
        load.wait()
        store.start()
    for copy in copies[4:]:
        copy.wait()
    proj = dot_t(derivs_ref[...], compressor_ref[...])
    last = tokens_ref[:, columns[-1]]
    for i in range(PARTS):
        source = jnp.concatenate([tokens_ref[:, columns[i]], last], axis=0)
        packed = dot(masks[i], source).astype(BF16)
        for q in range(count):
            out_refs[q][:, columns[i]] = packed[q * ROWS : (q + 1) * ROWS]
    for q in range(count):
        grad = (shares[:, q : q + 1] * proj).astype(BF16)
        both = dot(owned[q], grad)
        halves = [both[n * ROWS : (n + 1) * ROWS] for n in range(EX_DEV)]
        out_refs[q][:, PARTS * chunk :] = jnp.concatenate(halves, axis=1).astype(BF16)
    for store in stores:
        store.wait()


def keep_kernel(compressor_ref, weights_hbm, rows_hbm, *refs):
    weights_ref, rows_ref, first_ref, second_ref, sems = refs
    copies = [
        pltpu.make_async_copy(weights_hbm, weights_ref, sems.at[0]),
        pltpu.make_async_copy(rows_hbm, rows_ref, sems.at[1]),
    ]
    for copy in copies:
        copy.start()
    chosen = chosen_compressors(compressor_ref, first_ref.shape[1])
    first_ref[...], second_ref[...] = chosen
    for copy in copies:
        copy.wait()


def chosen_compressors(compressor_ref, units):
    place = lax.axis_index("dp")
    rank, total = compressor_ref.shape
    to = lax.broadcasted_iota(jnp.int32, (rank, rank), 0)
    at = lax.broadcasted_iota(jnp.int32, (rank, rank), 1)
    order = one_hot(at == jnp.where(to < rank // 2, 2 * to, 2 * to - rank + 1))
    turned = dot(order, compressor_ref[...]).astype(BF16)
    line = lax.broadcasted_iota(jnp.int32, (total, units), 0)
    unit = lax.broadcasted_iota(jnp.int32, (total, units), 1)
    return [
        dot(turned, one_hot(line == unit + jnp.bitwise_xor(place, k) * units)).astype(BF16)
        for k in range(2)
    ]


def sketch_kernel(sizes, own_ref, pair_ref, first_ref, second_ref, *refs):
    out_refs, grads_ref = refs[-1 - len(sizes) : -1], refs[-1]
    block_refs = refs[: -1 - len(sizes)]
    units, width = own_ref.shape[0] // 2, own_ref.shape[1]
    chunk = width // (PARTS + 1)
    size = sum(sizes)
    messages = size // ROWS
    low = lax.broadcasted_iota(jnp.int32, (1, HALF, 1), 1) < SPARE
    columns = [slice(i * chunk, (i + 1) * chunk) for i in range(PARTS + 1)]
    rows = [jnp.concatenate([r[:, c] for r in block_refs], axis=0) for c in columns[:PARTS]]
    tails = [r.astype(F32).reshape(messages, 2, HALF, chunk)[:, 1] for r in rows]

    def turn(a):
        return jnp.concatenate([a[:, SPARE:], a[:, :SPARE]], axis=1)

    top = jnp.where(low, turn(tails[0]), tails[1])
    bottom = jnp.where(low, turn(tails[2]), 0.0)
    rows.append(jnp.stack([top, bottom], axis=1).reshape(size, chunk).astype(BF16))
    seat = lax.broadcasted_iota(jnp.int32, (size, 1), 0) % ROWS

    def product(w, lines):
        total = dot_t(rows[0], w[lines, columns[0]])
        for c, r in zip(columns[1:], rows[1:]):
            total = total + dot_t(r, w[lines, c])
        return total

    sketch = None
    for ref, compressor in ((own_ref, first_ref), (pair_ref, second_ref)):
        gate, up = product(ref, slice(0, units)), product(ref, slice(units, 2 * units))
        hidden = gate / (1.0 + jnp.exp(-gate)) * up
        hidden = jnp.where(seat < LOCAL_SEATS, hidden, 0.0).astype(BF16)
        term = dot_t(compressor[...], hidden)
        sketch = term if sketch is None else sketch + term
    at = 0
    for n, ref in zip(sizes, out_refs):
        ref[...] = sketch[:, at : at + n].astype(ref.dtype)
        at += n
    first = 0
    for r in block_refs:
        if first < sizes[0]:
            grads_ref[first : first + r.shape[0]] = r[:, PARTS * chunk :]
        first += r.shape[0]


def outer_kernel(grads_ref, *refs):
    partial_refs, out_ref = refs[:-1], refs[-1]
    total = partial_refs[0][...]
    for r in partial_refs[1:]:
        total = total + r[...].astype(F32)
    rank = total.shape[0]
    product = dot(total.astype(BF16), grads_ref[...])
    even, odd = product[: rank // 2], product[rank // 2 :]
    for n in range(EX_DEV):
        columns = slice(n * rank, (n + 1) * rank)
        out_ref[n] = jnp.concatenate([even[:, columns], odd[:, columns]], axis=1)


VMEM = pl.BlockSpec(memory_space=pltpu.VMEM)
SMEM = pl.BlockSpec(memory_space=pltpu.SMEM)
HBM = pl.BlockSpec(memory_space=pltpu.HBM)
ANY = pl.BlockSpec(memory_space=pl.ANY)


def call(kernel, out_shape, in_specs, limit, flops=0, moved=0, scratch=(), out_specs=None):
    return pl.pallas_call(
        kernel,
        out_shape=out_shape,
        in_specs=in_specs,
        out_specs=out_specs or jax.tree.map(lambda _: VMEM, out_shape),
        scratch_shapes=list(scratch),
        compiler_params=pltpu.CompilerParams(vmem_limit_bytes=limit),
        cost_estimate=pl.CostEstimate(flops=flops, bytes_accessed=moved, transcendentals=0),
    )


def swap(a, axis, q):
    n = lax.axis_size(axis)
    return lax.ppermute(a, axis, [(i, i ^ q) for i in range(n)])


def body(
    layer_inflows,
    output_derivatives,
    picked_specialists,
    dispatch_shares,
    item_sample,
    send_limits,
    gating_projection,
    raising_projection,
    inflow_compressor,
    outgrad_compressor,
):
    n_exp, n_dp = lax.axis_size("exp"), lax.axis_size("dp")
    small = n_exp <= 8
    tokens, width = layer_inflows.shape
    rank = outgrad_compressor.shape[1]
    packed = width * LOCAL_SEATS // ROWS
    units = gating_projection.shape[2]
    size = n_exp * ROWS
    shape = jax.ShapeDtypeStruct

    gate, up = gating_projection[0].T, raising_projection[0].T
    arguments = (
        send_limits,
        picked_specialists.T,
        dispatch_shares.T,
        item_sample.reshape(1, tokens),
        layer_inflows,
        output_derivatives,
        outgrad_compressor.T,
    )
    hops = [0, n_exp - 1] + list(range(1, n_exp - 1))
    spaces = [pltpu.SMEM] + [pltpu.VMEM] * (len(arguments) - 1)
    *rows, weights = call(
        functools.partial(send_kernel, hops),
        [shape((ROWS, packed + EX_DEV * rank), BF16)] * n_exp + [shape((2 * units, width), BF16)],
        [HBM] * (len(arguments) + 2),
        SEND_LIMIT * MIB,
        out_specs=[VMEM] * n_exp + [ANY],
        flops=4 * size * tokens * packed + 2 * tokens * width * rank,
        moved=4 * tokens * width + 2 * rank * width + 8 * units * width,
        scratch=[space(a.shape, a.dtype) for space, a in zip(spaces, arguments)]
        + [pltpu.VMEM((2 * units, width), BF16), pltpu.SemaphoreType.DMA((len(arguments) + 4 * PIECES,))],
    )(*arguments, gate, up)
    pair_weights = swap(weights, "dp", 1)

    half = n_dp // 2
    crossed = [swap(rows[0], "dp", half)]
    chosen_shape = shape((rank, units), BF16)
    weights, rows[0], *chosen = call(
        keep_kernel,
        [shape(weights.shape, BF16), shape(rows[0].shape, BF16), chosen_shape, chosen_shape],
        [VMEM, ANY, ANY],
        KEEP_LIMIT * MIB,
        out_specs=[ANY, ANY, VMEM, VMEM],
        moved=8 * units * width,
        scratch=[pltpu.SemaphoreType.DMA((2,))],
    )(inflow_compressor.T, weights, rows[0])
    for i, q in enumerate(hops):
        if i:
            rows[i] = swap(rows[i], "exp", q)
            if i == 1:
                rows[i], weights = lax.optimization_barrier((rows[i], weights))
            crossed.append(swap(rows[i], "dp", half))
    blocks = {0: rows, half: crossed}
    step = half // 2
    while step > 1:
        for d in list(blocks):
            blocks[d ^ step] = [swap(r, "dp", step) for r in blocks[d]]
        step //= 2

    partials, grads = [], None
    ends = sorted(blocks)
    for ds in [ends] if small else [[d] for d in ends]:
        parts = [r for d in ds for r in blocks[d]]
        *made, first = call(
            functools.partial(sketch_kernel, [size] * len(ds)),
            [shape((rank, size), BF16 if d else F32) for d in ds]
            + [shape((size, EX_DEV * rank), BF16)],
            [VMEM] * (4 + len(parts)),
            20 * MIB,
            flops=8 * len(ds) * size * width * units,
            moved=8 * width * units + 2 * len(ds) * size * packed,
        )(weights, pair_weights, *chosen, *parts)
        grads = first if grads is None else grads
        partials += [swap(p, "dp", d) if d else p for d, p in zip(ds, made)]
    out = call(
        outer_kernel,
        shape((EX_DEV, rank * rank // 128, 128), F32),
        [VMEM] * (1 + len(partials)),
        8 * MIB,
        flops=2 * size * rank * 2 * rank,
        moved=4 * EX_DEV * rank * rank,
    )(grads, *partials)
    return out.reshape(EX_DEV, 1, rank * rank)


def solution(mesh):
    in_specs = (
        P(("grp", "exp", "dp"), None),
        P(("grp", "exp", "dp"), None),
        P(("grp", "exp", "dp"), None),
        P(("grp", "exp", "dp"), None),
        P(("grp", "exp", "dp")),
        P("grp"),
        P("exp", None, "dp"),
        P("exp", None, "dp"),
        P(),
        P(),
    )
    out_specs = P(("grp", "dp"), "exp", None)
    return jax.shard_map(body, mesh=mesh, in_specs=in_specs, out_specs=out_specs, check_vma=False)
```

```python
import functools

import jax
import jax.numpy as jnp
from jax import lax
from jax.experimental import pallas as pl
from jax.experimental.pallas import tpu as pltpu
from jax.sharding import PartitionSpec as P

EX_DEV = 2
LOCAL_SEATS = 12
ROWS = 16
SPARE = ROWS - LOCAL_SEATS
PARTS = LOCAL_SEATS // SPARE
HALF = ROWS // 2
MIB = 1024 * 1024
KEEP_LIMIT = 49
PIECES = 6
SEND_LIMIT = 56
BF16 = jnp.bfloat16
F32 = jnp.float32


def dot(a, b):
    return jnp.dot(a, b, preferred_element_type=F32)


def dot_t(a, b):
    return lax.dot_general(a, b, (((1,), (1,)), ((), ())), preferred_element_type=F32)


def one_hot(mask):
    return mask.astype(F32).astype(BF16)


def seats_of(limits_ref, picked, experts):
    tokens = picked.shape[1]
    flags = [jnp.max((picked == e).astype(F32), axis=0, keepdims=True) for e in experts]
    flags = jnp.concatenate(flags, axis=0)
    earlier = lax.broadcasted_iota(jnp.int32, (tokens, tokens), 0)
    later = lax.broadcasted_iota(jnp.int32, (tokens, tokens), 1)
    position = dot(flags.astype(BF16), one_hot(earlier < later)).astype(jnp.int32)
    rows = []
    for i, e in enumerate(experts):
        limit = jnp.minimum(limits_ref[e], LOCAL_SEATS)
        at = position[i : i + 1]
        rows.append(jnp.where((flags[i : i + 1] > 0.0) & (at < limit), at, -1))
    return rows


def send_kernel(hops, *refs):
    count = len(hops)
    in_refs, (gate_hbm, up_hbm), refs = refs[:7], refs[7:9], refs[9:]
    out_refs, weights_ref, scratch, sems = refs[:count], refs[count], refs[count + 1 : -1], refs[-1]
    *scratch, held_ref = scratch
    limits_ref, picked_ref, shares_ref, owner_ref, tokens_ref, derivs_ref, compressor_ref = scratch
    units = gate_hbm.shape[0]
    tokens, width = tokens_ref.shape
    chunk = width // (PARTS + 1)
    columns = [slice(i * chunk, (i + 1) * chunk) for i in range(PARTS + 1)]
    copies = [
        pltpu.make_async_copy(a, b, sems.at[i]) for i, (a, b) in enumerate(zip(in_refs, scratch))
    ]
    loads, stores = [], []
    piece = units // PIECES
    for k, source in enumerate((gate_hbm, up_hbm)):
        for j in range(PIECES):
            lines = pl.ds(k * units + j * piece, piece)
            load_sem, store_sem = [sems.at[len(copies) + len(loads) + n] for n in (0, 2 * PIECES)]
            loads.append(
                pltpu.make_async_copy(
                    source.at[pl.ds(j * piece, piece)], held_ref.at[lines], load_sem
                )
            )
            stores.append(
                pltpu.make_async_copy(held_ref.at[lines], weights_ref.at[lines], store_sem)
            )
    for copy in copies[:4] + copies[5:] + copies[4:5] + loads:
        copy.start()
    for copy in copies[:4]:
        copy.wait()
    me = lax.axis_index("exp")
    experts = [jnp.bitwise_xor(me, q) for q in hops]
    picked = picked_ref[...]
    seats = seats_of(limits_ref, picked, experts)
    slot = lax.broadcasted_iota(jnp.int32, (ROWS, tokens), 0)
    near = jnp.concatenate([one_hot(slot == s) for s in seats], axis=0)
    masks = []
    for i in range(PARTS):
        shifted = jnp.where(slot >= LOCAL_SEATS, slot - LOCAL_SEATS + SPARE * i, -2)
        far = jnp.concatenate([one_hot(shifted == s) for s in seats], axis=0)
        masks.append(jnp.concatenate([near, far], axis=1))
    owner = owner_ref[...] - lax.axis_index("dp") * EX_DEV
    owned = [
        jnp.concatenate([one_hot((slot == s) & (owner == n)) for n in range(EX_DEV)], axis=0)
        for s in seats
    ]
    share_rows = [
        jnp.sum(jnp.where(picked == e, shares_ref[...], 0.0), axis=0, keepdims=True)
        for e in experts
    ]
    pad = [jnp.zeros((-count % 8, tokens), F32)] if count % 8 else []
    shares = jnp.concatenate(share_rows + pad, axis=0).T
    for load, store in zip(loads, stores):
        load.wait()
        store.start()
    for copy in copies[4:]:
        copy.wait()
    proj = dot_t(derivs_ref[...], compressor_ref[...])
    last = tokens_ref[:, columns[-1]]
    for i in range(PARTS):
        source = jnp.concatenate([tokens_ref[:, columns[i]], last], axis=0)
        packed = dot(masks[i], source).astype(BF16)
        for q in range(count):
            out_refs[q][:, columns[i]] = packed[q * ROWS : (q + 1) * ROWS]
    for q in range(count):
        grad = (shares[:, q : q + 1] * proj).astype(BF16)
        both = dot(owned[q], grad)
        halves = [both[n * ROWS : (n + 1) * ROWS] for n in range(EX_DEV)]
        out_refs[q][:, PARTS * chunk :] = jnp.concatenate(halves, axis=1).astype(BF16)
    for store in stores:
        store.wait()


def keep_kernel(compressor_ref, weights_hbm, rows_hbm, *refs):
    weights_ref, rows_ref, first_ref, second_ref, sems = refs
    piece = weights_ref.shape[0] // PIECES
    copies = [
        pltpu.make_async_copy(
            weights_hbm.at[pl.ds(i * piece, piece)],
            weights_ref.at[pl.ds(i * piece, piece)],
            sems.at[i],
        )
        for i in range(PIECES)
    ]
    copies.append(pltpu.make_async_copy(rows_hbm, rows_ref, sems.at[PIECES]))
    for copy in copies:
        copy.start()
    chosen = chosen_compressors(compressor_ref, first_ref.shape[1])
    first_ref[...], second_ref[...] = chosen
    for copy in copies:
        copy.wait()


def chosen_compressors(compressor_ref, units):
    place = lax.axis_index("dp")
    rank, total = compressor_ref.shape
    to = lax.broadcasted_iota(jnp.int32, (rank, rank), 0)
    at = lax.broadcasted_iota(jnp.int32, (rank, rank), 1)
    order = one_hot(at == jnp.where(to < rank // 2, 2 * to, 2 * to - rank + 1))
    turned = dot(order, compressor_ref[...]).astype(BF16)
    line = lax.broadcasted_iota(jnp.int32, (total, units), 0)
    unit = lax.broadcasted_iota(jnp.int32, (total, units), 1)
    return [
        dot(turned, one_hot(line == unit + jnp.bitwise_xor(place, k) * units)).astype(BF16)
        for k in range(2)
    ]


def sketch_kernel(sizes, own_ref, pair_ref, first_ref, second_ref, *refs):
    out_refs, grads_ref = refs[-1 - len(sizes) : -1], refs[-1]
    block_refs = refs[: -1 - len(sizes)]
    units, width = own_ref.shape[0] // 2, own_ref.shape[1]
    chunk = width // (PARTS + 1)
    size = sum(sizes)
    messages = size // ROWS
    low = lax.broadcasted_iota(jnp.int32, (1, HALF, 1), 1) < SPARE
    columns = [slice(i * chunk, (i + 1) * chunk) for i in range(PARTS + 1)]
    rows = [jnp.concatenate([r[:, c] for r in block_refs], axis=0) for c in columns[:PARTS]]
    tails = [r.astype(F32).reshape(messages, 2, HALF, chunk)[:, 1] for r in rows]

    def turn(a):
        return jnp.concatenate([a[:, SPARE:], a[:, :SPARE]], axis=1)

    top = jnp.where(low, turn(tails[0]), tails[1])
    bottom = jnp.where(low, turn(tails[2]), 0.0)
    rows.append(jnp.stack([top, bottom], axis=1).reshape(size, chunk).astype(BF16))
    seat = lax.broadcasted_iota(jnp.int32, (size, 1), 0) % ROWS

    def product(w, lines):
        total = dot_t(rows[0], w[lines, columns[0]])
        for c, r in zip(columns[1:], rows[1:]):
            total = total + dot_t(r, w[lines, c])
        return total

    sketch = None
    for ref, compressor in ((own_ref, first_ref), (pair_ref, second_ref)):
        gate, up = product(ref, slice(0, units)), product(ref, slice(units, 2 * units))
        hidden = gate / (1.0 + jnp.exp(-gate)) * up
        hidden = jnp.where(seat < LOCAL_SEATS, hidden, 0.0).astype(BF16)
        term = dot_t(compressor[...], hidden)
        sketch = term if sketch is None else sketch + term
    at = 0
    for n, ref in zip(sizes, out_refs):
        ref[...] = sketch[:, at : at + n].astype(ref.dtype)
        at += n
    first = 0
    for r in block_refs:
        if first < sizes[0]:
            grads_ref[first : first + r.shape[0]] = r[:, PARTS * chunk :]
        first += r.shape[0]


def outer_kernel(grads_ref, *refs):
    partial_refs, out_ref = refs[:-1], refs[-1]
    total = partial_refs[0][...]
    for r in partial_refs[1:]:
        total = total + r[...].astype(F32)
    rank = total.shape[0]
    product = dot(total.astype(BF16), grads_ref[...])
    even, odd = product[: rank // 2], product[rank // 2 :]
    for n in range(EX_DEV):
        columns = slice(n * rank, (n + 1) * rank)
        out_ref[n] = jnp.concatenate([even[:, columns], odd[:, columns]], axis=1)


VMEM = pl.BlockSpec(memory_space=pltpu.VMEM)
SMEM = pl.BlockSpec(memory_space=pltpu.SMEM)
HBM = pl.BlockSpec(memory_space=pltpu.HBM)
ANY = pl.BlockSpec(memory_space=pl.ANY)


def call(kernel, out_shape, in_specs, limit, flops=0, moved=0, scratch=(), out_specs=None):
    return pl.pallas_call(
        kernel,
        out_shape=out_shape,
        in_specs=in_specs,
        out_specs=out_specs or jax.tree.map(lambda _: VMEM, out_shape),
        scratch_shapes=list(scratch),
        compiler_params=pltpu.CompilerParams(vmem_limit_bytes=limit),
        cost_estimate=pl.CostEstimate(flops=flops, bytes_accessed=moved, transcendentals=0),
    )


def swap(a, axis, q):
    n = lax.axis_size(axis)
    return lax.ppermute(a, axis, [(i, i ^ q) for i in range(n)])


def swap_both(a, q, d):
    n_exp, n_dp = lax.axis_size("exp"), lax.axis_size("dp")
    pairs = [
        (e * n_dp + i, (e ^ q) * n_dp + (i ^ d)) for e in range(n_exp) for i in range(n_dp)
    ]
    return lax.ppermute(a, ("exp", "dp"), pairs)


def body(
    layer_inflows,
    output_derivatives,
    picked_specialists,
    dispatch_shares,
    item_sample,
    send_limits,
    gating_projection,
    raising_projection,
    inflow_compressor,
    outgrad_compressor,
):
    n_exp, n_dp = lax.axis_size("exp"), lax.axis_size("dp")
    small = n_exp <= 8
    tokens, width = layer_inflows.shape
    rank = outgrad_compressor.shape[1]
    packed = width * LOCAL_SEATS // ROWS
    units = gating_projection.shape[2]
    size = n_exp * ROWS
    shape = jax.ShapeDtypeStruct

    gate, up = gating_projection[0].T, raising_projection[0].T
    arguments = (
        send_limits,
        picked_specialists.T,
        dispatch_shares.T,
        item_sample.reshape(1, tokens),
        layer_inflows,
        output_derivatives,
        outgrad_compressor.T,
    )
    hops = [0, n_exp - 1] + list(range(1, n_exp - 1))
    spaces = [pltpu.SMEM] + [pltpu.VMEM] * (len(arguments) - 1)
    *rows, weights = call(
        functools.partial(send_kernel, hops),
        [shape((ROWS, packed + EX_DEV * rank), BF16)] * n_exp + [shape((2 * units, width), BF16)],
        [HBM] * (len(arguments) + 2),
        SEND_LIMIT * MIB,
        out_specs=[VMEM] * n_exp + [ANY],
        flops=4 * size * tokens * packed + 2 * tokens * width * rank,
        moved=4 * tokens * width + 2 * rank * width + 8 * units * width,
        scratch=[space(a.shape, a.dtype) for space, a in zip(spaces, arguments)]
        + [pltpu.VMEM((2 * units, width), BF16), pltpu.SemaphoreType.DMA((len(arguments) + 4 * PIECES,))],
    )(*arguments, gate, up)
    pair_weights = swap(weights, "dp", 1)

    half = n_dp // 2
    crossed = [swap(rows[0], "dp", half)]
    chosen_shape = shape((rank, units), BF16)
    weights, rows[0], *chosen = call(
        keep_kernel,
        [shape(weights.shape, BF16), shape(rows[0].shape, BF16), chosen_shape, chosen_shape],
        [VMEM, ANY, ANY],
        KEEP_LIMIT * MIB,
        out_specs=[ANY, ANY, VMEM, VMEM],
        moved=8 * units * width,
        scratch=[pltpu.SemaphoreType.DMA((PIECES + 1,))],
    )(inflow_compressor.T, weights, rows[0])
    for i, q in enumerate(hops):
        if i:
            if q == 1:
                crossed.append(swap_both(rows[i], q, half))
            rows[i] = swap(rows[i], "exp", q)
            if q == 1:
                rows[i], weights = lax.optimization_barrier((rows[i], weights))
            if q != 1:
                crossed.append(swap(rows[i], "dp", half))
    blocks = {0: rows, half: crossed}
    step = half // 2
    while step > 1:
        for d in list(blocks):
            blocks[d ^ step] = [swap(r, "dp", step) for r in blocks[d]]
        step //= 2

    partials, grads = [], None
    ends = sorted(blocks)
    for ds in [ends] if small else [[d] for d in ends]:
        parts = [r for d in ds for r in blocks[d]]
        *made, first = call(
            functools.partial(sketch_kernel, [size] * len(ds)),
            [shape((rank, size), BF16 if d else F32) for d in ds]
            + [shape((size, EX_DEV * rank), BF16)],
            [VMEM] * (4 + len(parts)),
            20 * MIB,
            flops=8 * len(ds) * size * width * units,
            moved=8 * width * units + 2 * len(ds) * size * packed,
        )(weights, pair_weights, *chosen, *parts)
        grads = first if grads is None else grads
        partials += [swap(p, "dp", d) if d else p for d, p in zip(ds, made)]
    out = call(
        outer_kernel,
        shape((EX_DEV, rank * rank // 128, 128), F32),
        [VMEM] * (1 + len(partials)),
        8 * MIB,
        flops=2 * size * rank * 2 * rank,
        moved=4 * EX_DEV * rank * rank,
    )(grads, *partials)
    return out.reshape(EX_DEV, 1, rank * rank)


def solution(mesh):
    in_specs = (
        P(("grp", "exp", "dp"), None),
        P(("grp", "exp", "dp"), None),
        P(("grp", "exp", "dp"), None),
        P(("grp", "exp", "dp"), None),
        P(("grp", "exp", "dp")),
        P("grp"),
        P("exp", None, "dp"),
        P("exp", None, "dp"),
        P(),
        P(),
    )
    out_specs = P(("grp", "dp"), "exp", None)
    return jax.shard_map(body, mesh=mesh, in_specs=in_specs, out_specs=out_specs, check_vma=False)
```

```python
import functools

import jax
import jax.numpy as jnp
from jax import lax
from jax.experimental import pallas as pl
from jax.experimental.pallas import tpu as pltpu
from jax.sharding import PartitionSpec as P

EX_DEV = 2
LOCAL_SEATS = 12
ROWS = 16
SPARE = ROWS - LOCAL_SEATS
PARTS = LOCAL_SEATS // SPARE
HALF = ROWS // 2
MIB = 1024 * 1024
KEEP_LIMIT = 49
PIECES = 6
SEND_LIMIT = 56
BF16 = jnp.bfloat16
F32 = jnp.float32


def dot(a, b):
    return jnp.dot(a, b, preferred_element_type=F32)


def dot_t(a, b):
    return lax.dot_general(a, b, (((1,), (1,)), ((), ())), preferred_element_type=F32)


def one_hot(mask):
    return mask.astype(F32).astype(BF16)


def seats_of(limits_ref, picked, experts):
    tokens = picked.shape[1]
    flags = [jnp.max((picked == e).astype(F32), axis=0, keepdims=True) for e in experts]
    flags = jnp.concatenate(flags, axis=0)
    earlier = lax.broadcasted_iota(jnp.int32, (tokens, tokens), 0)
    later = lax.broadcasted_iota(jnp.int32, (tokens, tokens), 1)
    position = dot(flags.astype(BF16), one_hot(earlier < later)).astype(jnp.int32)
    rows = []
    for i, e in enumerate(experts):
        limit = jnp.minimum(limits_ref[e], LOCAL_SEATS)
        at = position[i : i + 1]
        rows.append(jnp.where((flags[i : i + 1] > 0.0) & (at < limit), at, -1))
    return rows


def send_kernel(hops, *refs):
    count = len(hops)
    in_refs, (gate_hbm, up_hbm), refs = refs[:7], refs[7:9], refs[9:]
    out_refs, weights_ref, scratch, sems = refs[:count], refs[count], refs[count + 1 : -1], refs[-1]
    *scratch, held_ref = scratch
    limits_ref, picked_ref, shares_ref, owner_ref, tokens_ref, derivs_ref, compressor_ref = scratch
    units = gate_hbm.shape[0]
    tokens, width = tokens_ref.shape
    chunk = width // (PARTS + 1)
    columns = [slice(i * chunk, (i + 1) * chunk) for i in range(PARTS + 1)]
    copies = [
        pltpu.make_async_copy(a, b, sems.at[i]) for i, (a, b) in enumerate(zip(in_refs, scratch))
    ]
    loads, stores = [], []
    piece = units // PIECES
    for k, source in enumerate((gate_hbm, up_hbm)):
        for j in range(PIECES):
            lines = pl.ds(k * units + j * piece, piece)
            load_sem, store_sem = [sems.at[len(copies) + len(loads) + n] for n in (0, 2 * PIECES)]
            loads.append(
                pltpu.make_async_copy(
                    source.at[pl.ds(j * piece, piece)], held_ref.at[lines], load_sem
                )
            )
            stores.append(
                pltpu.make_async_copy(held_ref.at[lines], weights_ref.at[lines], store_sem)
            )
    for copy in copies[:4] + copies[5:] + copies[4:5] + loads:
        copy.start()
    for copy in copies[:4]:
        copy.wait()
    me = lax.axis_index("exp")
    experts = [jnp.bitwise_xor(me, q) for q in hops]
    picked = picked_ref[...]
    seats = seats_of(limits_ref, picked, experts)
    slot = lax.broadcasted_iota(jnp.int32, (ROWS, tokens), 0)
    near = jnp.concatenate([one_hot(slot == s) for s in seats], axis=0)
    masks = []
    for i in range(PARTS):
        shifted = jnp.where(slot >= LOCAL_SEATS, slot - LOCAL_SEATS + SPARE * i, -2)
        far = jnp.concatenate([one_hot(shifted == s) for s in seats], axis=0)
        masks.append(jnp.concatenate([near, far], axis=1))
    owner = owner_ref[...] - lax.axis_index("dp") * EX_DEV
    owned = [
        jnp.concatenate([one_hot((slot == s) & (owner == n)) for n in range(EX_DEV)], axis=0)
        for s in seats
    ]
    share_rows = [
        jnp.sum(jnp.where(picked == e, shares_ref[...], 0.0), axis=0, keepdims=True)
        for e in experts
    ]
    pad = [jnp.zeros((-count % 8, tokens), F32)] if count % 8 else []
    shares = jnp.concatenate(share_rows + pad, axis=0).T
    for load, store in zip(loads, stores):
        load.wait()
        store.start()
    for copy in copies[4:]:
        copy.wait()
    proj = dot_t(derivs_ref[...], compressor_ref[...])
    last = tokens_ref[:, columns[-1]]
    for i in range(PARTS):
        source = jnp.concatenate([tokens_ref[:, columns[i]], last], axis=0)
        packed = dot(masks[i], source).astype(BF16)
        for q in range(count):
            out_refs[q][:, columns[i]] = packed[q * ROWS : (q + 1) * ROWS]
    for q in range(count):
        grad = (shares[:, q : q + 1] * proj).astype(BF16)
        both = dot(owned[q], grad)
        halves = [both[n * ROWS : (n + 1) * ROWS] for n in range(EX_DEV)]
        out_refs[q][:, PARTS * chunk :] = jnp.concatenate(halves, axis=1).astype(BF16)
    for store in stores:
        store.wait()


def keep_kernel(compressor_ref, weights_hbm, rows_hbm, *refs):
    weights_ref, rows_ref, first_ref, second_ref, sems = refs
    piece = weights_ref.shape[0] // PIECES
    copies = [
        pltpu.make_async_copy(
            weights_hbm.at[pl.ds(i * piece, piece)],
            weights_ref.at[pl.ds(i * piece, piece)],
            sems.at[i],
        )
        for i in range(PIECES)
    ]
    copies.append(pltpu.make_async_copy(rows_hbm, rows_ref, sems.at[PIECES]))
    for copy in copies:
        copy.start()
    chosen = chosen_compressors(compressor_ref, first_ref.shape[1])
    first_ref[...], second_ref[...] = chosen
    for copy in copies:
        copy.wait()


def chosen_compressors(compressor_ref, units):
    place = lax.axis_index("dp")
    rank, total = compressor_ref.shape
    to = lax.broadcasted_iota(jnp.int32, (rank, rank), 0)
    at = lax.broadcasted_iota(jnp.int32, (rank, rank), 1)
    order = one_hot(at == jnp.where(to < rank // 2, 2 * to, 2 * to - rank + 1))
    turned = dot(order, compressor_ref[...]).astype(BF16)
    line = lax.broadcasted_iota(jnp.int32, (total, units), 0)
    unit = lax.broadcasted_iota(jnp.int32, (total, units), 1)
    return [
        dot(turned, one_hot(line == unit + jnp.bitwise_xor(place, k) * units)).astype(BF16)
        for k in range(2)
    ]


def sketch_kernel(sizes, own_ref, pair_ref, first_ref, second_ref, *refs):
    out_refs, grads_ref = refs[-1 - len(sizes) : -1], refs[-1]
    block_refs = refs[: -1 - len(sizes)]
    units, width = own_ref.shape[0] // 2, own_ref.shape[1]
    chunk = width // (PARTS + 1)
    size = sum(sizes)
    messages = size // ROWS
    low = lax.broadcasted_iota(jnp.int32, (1, HALF, 1), 1) < SPARE
    columns = [slice(i * chunk, (i + 1) * chunk) for i in range(PARTS + 1)]
    rows = [jnp.concatenate([r[:, c] for r in block_refs], axis=0) for c in columns[:PARTS]]
    tails = [r.astype(F32).reshape(messages, 2, HALF, chunk)[:, 1] for r in rows]

    def turn(a):
        return jnp.concatenate([a[:, SPARE:], a[:, :SPARE]], axis=1)

    top = jnp.where(low, turn(tails[0]), tails[1])
    bottom = jnp.where(low, turn(tails[2]), 0.0)
    rows.append(jnp.stack([top, bottom], axis=1).reshape(size, chunk).astype(BF16))
    seat = lax.broadcasted_iota(jnp.int32, (size, 1), 0) % ROWS

    def product(w, lines):
        total = dot_t(rows[0], w[lines, columns[0]])
        for c, r in zip(columns[1:], rows[1:]):
            total = total + dot_t(r, w[lines, c])
        return total

    sketch = None
    for ref, compressor in ((own_ref, first_ref), (pair_ref, second_ref)):
        gate, up = product(ref, slice(0, units)), product(ref, slice(units, 2 * units))
        hidden = gate / (1.0 + jnp.exp(-gate)) * up
        hidden = jnp.where(seat < LOCAL_SEATS, hidden, 0.0).astype(BF16)
        term = dot_t(compressor[...], hidden)
        sketch = term if sketch is None else sketch + term
    at = 0
    for n, ref in zip(sizes, out_refs):
        ref[...] = sketch[:, at : at + n].astype(ref.dtype)
        at += n
    first = 0
    for r in block_refs:
        if first < sizes[0]:
            grads_ref[first : first + r.shape[0]] = r[:, PARTS * chunk :]
        first += r.shape[0]


def outer_kernel(grads_ref, *refs):
    partial_refs, out_ref = refs[:-1], refs[-1]
    total = partial_refs[0][...]
    for r in partial_refs[1:]:
        total = total + r[...].astype(F32)
    rank = total.shape[0]
    product = dot(total.astype(BF16), grads_ref[...])
    even, odd = product[: rank // 2], product[rank // 2 :]
    for n in range(EX_DEV):
        columns = slice(n * rank, (n + 1) * rank)
        out_ref[n] = jnp.concatenate([even[:, columns], odd[:, columns]], axis=1)


VMEM = pl.BlockSpec(memory_space=pltpu.VMEM)
SMEM = pl.BlockSpec(memory_space=pltpu.SMEM)
HBM = pl.BlockSpec(memory_space=pltpu.HBM)
ANY = pl.BlockSpec(memory_space=pl.ANY)


def call(kernel, out_shape, in_specs, limit, flops=0, moved=0, scratch=(), out_specs=None):
    return pl.pallas_call(
        kernel,
        out_shape=out_shape,
        in_specs=in_specs,
        out_specs=out_specs or jax.tree.map(lambda _: VMEM, out_shape),
        scratch_shapes=list(scratch),
        compiler_params=pltpu.CompilerParams(vmem_limit_bytes=limit),
        cost_estimate=pl.CostEstimate(flops=flops, bytes_accessed=moved, transcendentals=0),
    )


def swap(a, axis, q):
    n = lax.axis_size(axis)
    return lax.ppermute(a, axis, [(i, i ^ q) for i in range(n)])


def body(
    layer_inflows,
    output_derivatives,
    picked_specialists,
    dispatch_shares,
    item_sample,
    send_limits,
    gating_projection,
    raising_projection,
    inflow_compressor,
    outgrad_compressor,
):
    n_exp, n_dp = lax.axis_size("exp"), lax.axis_size("dp")
    small = n_exp <= 8
    tokens, width = layer_inflows.shape
    rank = outgrad_compressor.shape[1]
    packed = width * LOCAL_SEATS // ROWS
    units = gating_projection.shape[2]
    size = n_exp * ROWS
    shape = jax.ShapeDtypeStruct

    gate, up = gating_projection[0].T, raising_projection[0].T
    arguments = (
        send_limits,
        picked_specialists.T,
        dispatch_shares.T,
        item_sample.reshape(1, tokens),
        layer_inflows,
        output_derivatives,
        outgrad_compressor.T,
    )
    hops = [0, n_exp - 1] + list(range(1, n_exp - 1))
    spaces = [pltpu.SMEM] + [pltpu.VMEM] * (len(arguments) - 1)
    *rows, weights = call(
        functools.partial(send_kernel, hops),
        [shape((ROWS, packed + EX_DEV * rank), BF16)] * n_exp + [shape((2 * units, width), BF16)],
        [HBM] * (len(arguments) + 2),
        SEND_LIMIT * MIB,
        out_specs=[VMEM] * n_exp + [ANY],
        flops=4 * size * tokens * packed + 2 * tokens * width * rank,
        moved=4 * tokens * width + 2 * rank * width + 8 * units * width,
        scratch=[space(a.shape, a.dtype) for space, a in zip(spaces, arguments)]
        + [pltpu.VMEM((2 * units, width), BF16), pltpu.SemaphoreType.DMA((len(arguments) + 4 * PIECES,))],
    )(*arguments, gate, up)
    pair_weights = swap(weights, "dp", 1)

    half = n_dp // 2
    crossed = [swap(rows[0], "dp", half)]
    chosen_shape = shape((rank, units), BF16)
    weights, rows[0], *chosen = call(
        keep_kernel,
        [shape(weights.shape, BF16), shape(rows[0].shape, BF16), chosen_shape, chosen_shape],
        [VMEM, ANY, ANY],
        KEEP_LIMIT * MIB,
        out_specs=[ANY, ANY, VMEM, VMEM],
        moved=8 * units * width,
        scratch=[pltpu.SemaphoreType.DMA((PIECES + 1,))],
    )(inflow_compressor.T, weights, rows[0])
    for i, q in enumerate(hops):
        if i:
            rows[i] = swap(rows[i], "exp", q)
            crossed.append(swap(rows[i], "dp", half))
    blocks = {0: rows, half: crossed}
    step = half // 2
    while step > 1:
        for d in list(blocks):
            blocks[d ^ step] = [swap(r, "dp", step) for r in blocks[d]]
        step //= 2

    partials, grads = [], None
    ends = sorted(blocks)
    for ds in [ends] if small else [[d] for d in ends]:
        parts = [r for d in ds for r in blocks[d]]
        *made, first = call(
            functools.partial(sketch_kernel, [size] * len(ds)),
            [shape((rank, size), BF16 if d else F32) for d in ds]
            + [shape((size, EX_DEV * rank), BF16)],
            [VMEM] * (4 + len(parts)),
            20 * MIB,
            flops=8 * len(ds) * size * width * units,
            moved=8 * width * units + 2 * len(ds) * size * packed,
        )(weights, pair_weights, *chosen, *parts)
        grads = first if grads is None else grads
        partials += [swap(p, "dp", d) if d else p for d, p in zip(ds, made)]
    out = call(
        outer_kernel,
        shape((EX_DEV, rank * rank // 128, 128), F32),
        [VMEM] * (1 + len(partials)),
        8 * MIB,
        flops=2 * size * rank * 2 * rank,
        moved=4 * EX_DEV * rank * rank,
    )(grads, *partials)
    return out.reshape(EX_DEV, 1, rank * rank)


def solution(mesh):
    in_specs = (
        P(("grp", "exp", "dp"), None),
        P(("grp", "exp", "dp"), None),
        P(("grp", "exp", "dp"), None),
        P(("grp", "exp", "dp"), None),
        P(("grp", "exp", "dp")),
        P("grp"),
        P("exp", None, "dp"),
        P("exp", None, "dp"),
        P(),
        P(),
    )
    out_specs = P(("grp", "dp"), "exp", None)
    return jax.shard_map(body, mesh=mesh, in_specs=in_specs, out_specs=out_specs, check_vma=False)
```

```python
import functools

import jax
import jax.numpy as jnp
from jax import lax
from jax.experimental import pallas as pl
from jax.experimental.pallas import tpu as pltpu
from jax.sharding import PartitionSpec as P

EX_DEV = 2
LOCAL_SEATS = 12
ROWS = 16
SPARE = ROWS - LOCAL_SEATS
PARTS = LOCAL_SEATS // SPARE
HALF = ROWS // 2
MIB = 1024 * 1024
KEEP_LIMIT = 48
SEND_LIMIT = 56
BF16 = jnp.bfloat16
F32 = jnp.float32


def dot(a, b):
    return jnp.dot(a, b, preferred_element_type=F32)


def dot_t(a, b):
    return lax.dot_general(a, b, (((1,), (1,)), ((), ())), preferred_element_type=F32)


def one_hot(mask):
    return mask.astype(F32).astype(BF16)


def seats_of(limits_ref, picked, experts):
    tokens = picked.shape[1]
    flags = [jnp.max((picked == e).astype(F32), axis=0, keepdims=True) for e in experts]
    flags = jnp.concatenate(flags, axis=0)
    earlier = lax.broadcasted_iota(jnp.int32, (tokens, tokens), 0)
    later = lax.broadcasted_iota(jnp.int32, (tokens, tokens), 1)
    position = dot(flags.astype(BF16), one_hot(earlier < later)).astype(jnp.int32)
    rows = []
    for i, e in enumerate(experts):
        limit = jnp.minimum(limits_ref[e], LOCAL_SEATS)
        at = position[i : i + 1]
        rows.append(jnp.where((flags[i : i + 1] > 0.0) & (at < limit), at, -1))
    return rows


def send_kernel(hops, *refs):
    count = len(hops)
    in_refs, out_refs, scratch, sems = refs[:7], refs[7 : 7 + count], refs[7 + count : -1], refs[-1]
    limits_ref, picked_ref, shares_ref, owner_ref, tokens_ref, derivs_ref, compressor_ref = scratch
    tokens, width = tokens_ref.shape
    chunk = width // (PARTS + 1)
    columns = [slice(i * chunk, (i + 1) * chunk) for i in range(PARTS + 1)]
    copies = [
        pltpu.make_async_copy(a, b, sems.at[i]) for i, (a, b) in enumerate(zip(in_refs, scratch))
    ]
    for copy in copies:
        copy.start()
    for copy in copies[:4]:
        copy.wait()
    me = lax.axis_index("exp")
    experts = [jnp.bitwise_xor(me, q) for q in hops]
    picked = picked_ref[...]
    seats = seats_of(limits_ref, picked, experts)
    slot = lax.broadcasted_iota(jnp.int32, (ROWS, tokens), 0)
    near = jnp.concatenate([one_hot(slot == s) for s in seats], axis=0)
    masks = []
    for i in range(PARTS):
        shifted = jnp.where(slot >= LOCAL_SEATS, slot - LOCAL_SEATS + SPARE * i, -2)
        far = jnp.concatenate([one_hot(shifted == s) for s in seats], axis=0)
        masks.append(jnp.concatenate([near, far], axis=1))
    owner = owner_ref[...] - lax.axis_index("dp") * EX_DEV
    owned = [
        jnp.concatenate([one_hot((slot == s) & (owner == n)) for n in range(EX_DEV)], axis=0)
        for s in seats
    ]
    share_rows = [
        jnp.sum(jnp.where(picked == e, shares_ref[...], 0.0), axis=0, keepdims=True)
        for e in experts
    ]
    pad = [jnp.zeros((-count % 8, tokens), F32)] if count % 8 else []
    shares = jnp.concatenate(share_rows + pad, axis=0).T
    for copy in copies[4:]:
        copy.wait()
    proj = dot_t(derivs_ref[...], compressor_ref[...])
    last = tokens_ref[:, columns[-1]]
    for i in range(PARTS):
        source = jnp.concatenate([tokens_ref[:, columns[i]], last], axis=0)
        packed = dot(masks[i], source).astype(BF16)
        for q in range(count):
            out_refs[q][:, columns[i]] = packed[q * ROWS : (q + 1) * ROWS]
    for q in range(count):
        grad = (shares[:, q : q + 1] * proj).astype(BF16)
        both = dot(owned[q], grad)
        halves = [both[n * ROWS : (n + 1) * ROWS] for n in range(EX_DEV)]
        out_refs[q][:, PARTS * chunk :] = jnp.concatenate(halves, axis=1).astype(BF16)


def keep_kernel(compressor_ref, gate_hbm, up_hbm, rows_hbm, *refs):
    gate_ref, up_ref, rows_ref, first_ref, second_ref, sems = refs
    pairs = ((gate_hbm, gate_ref), (up_hbm, up_ref), (rows_hbm, rows_ref))
    copies = [pltpu.make_async_copy(a, b, sems.at[i]) for i, (a, b) in enumerate(pairs)]
    for copy in copies:
        copy.start()
    chosen = chosen_compressors(compressor_ref, first_ref.shape[1])
    first_ref[...], second_ref[...] = chosen
    for copy in copies:
        copy.wait()


def chosen_compressors(compressor_ref, units):
    place = lax.axis_index("dp")
    rank, total = compressor_ref.shape
    to = lax.broadcasted_iota(jnp.int32, (rank, rank), 0)
    at = lax.broadcasted_iota(jnp.int32, (rank, rank), 1)
    order = one_hot(at == jnp.where(to < rank // 2, 2 * to, 2 * to - rank + 1))
    turned = dot(order, compressor_ref[...]).astype(BF16)
    line = lax.broadcasted_iota(jnp.int32, (total, units), 0)
    unit = lax.broadcasted_iota(jnp.int32, (total, units), 1)
    return [
        dot(turned, one_hot(line == unit + jnp.bitwise_xor(place, k) * units)).astype(BF16)
        for k in range(2)
    ]


def sketch_kernel(sizes, gate_ref, up_ref, pair_gate_ref, pair_up_ref, first_ref, second_ref, *refs):
    out_refs, grads_ref = refs[-1 - len(sizes) : -1], refs[-1]
    block_refs = refs[: -1 - len(sizes)]
    units, width = gate_ref.shape
    chunk = width // (PARTS + 1)
    size = sum(sizes)
    messages = size // ROWS
    low = lax.broadcasted_iota(jnp.int32, (1, HALF, 1), 1) < SPARE
    columns = [slice(i * chunk, (i + 1) * chunk) for i in range(PARTS + 1)]
    rows = [jnp.concatenate([r[:, c] for r in block_refs], axis=0) for c in columns[:PARTS]]
    tails = [r.astype(F32).reshape(messages, 2, HALF, chunk)[:, 1] for r in rows]

    def turn(a):
        return jnp.concatenate([a[:, SPARE:], a[:, :SPARE]], axis=1)

    top = jnp.where(low, turn(tails[0]), tails[1])
    bottom = jnp.where(low, turn(tails[2]), 0.0)
    rows.append(jnp.stack([top, bottom], axis=1).reshape(size, chunk).astype(BF16))
    seat = lax.broadcasted_iota(jnp.int32, (size, 1), 0) % ROWS

    def product(w):
        total = dot_t(rows[0], w[:, columns[0]])
        for c, r in zip(columns[1:], rows[1:]):
            total = total + dot_t(r, w[:, c])
        return total

    sketch = None
    for gate_w, up_w, compressor in (
        (gate_ref, up_ref, first_ref),
        (pair_gate_ref, pair_up_ref, second_ref),
    ):
        gate, up = product(gate_w), product(up_w)
        hidden = gate / (1.0 + jnp.exp(-gate)) * up
        hidden = jnp.where(seat < LOCAL_SEATS, hidden, 0.0).astype(BF16)
        term = dot_t(compressor[...], hidden)
        sketch = term if sketch is None else sketch + term
    at = 0
    for n, ref in zip(sizes, out_refs):
        ref[...] = sketch[:, at : at + n].astype(ref.dtype)
        at += n
    first = 0
    for r in block_refs:
        if first < sizes[0]:
            grads_ref[first : first + r.shape[0]] = r[:, PARTS * chunk :]
        first += r.shape[0]


def outer_kernel(grads_ref, *refs):
    partial_refs, out_ref = refs[:-1], refs[-1]
    total = partial_refs[0][...]
    for r in partial_refs[1:]:
        total = total + r[...].astype(F32)
    rank = total.shape[0]
    product = dot(total.astype(BF16), grads_ref[...])
    even, odd = product[: rank // 2], product[rank // 2 :]
    for n in range(EX_DEV):
        columns = slice(n * rank, (n + 1) * rank)
        out_ref[n] = jnp.concatenate([even[:, columns], odd[:, columns]], axis=1)


VMEM = pl.BlockSpec(memory_space=pltpu.VMEM)
SMEM = pl.BlockSpec(memory_space=pltpu.SMEM)
HBM = pl.BlockSpec(memory_space=pltpu.HBM)
ANY = pl.BlockSpec(memory_space=pl.ANY)


def call(kernel, out_shape, in_specs, limit, flops=0, moved=0, scratch=(), out_specs=None):
    return pl.pallas_call(
        kernel,
        out_shape=out_shape,
        in_specs=in_specs,
        out_specs=out_specs or jax.tree.map(lambda _: VMEM, out_shape),
        scratch_shapes=list(scratch),
        compiler_params=pltpu.CompilerParams(vmem_limit_bytes=limit),
        cost_estimate=pl.CostEstimate(flops=flops, bytes_accessed=moved, transcendentals=0),
    )


def swap(a, axis, q):
    n = lax.axis_size(axis)
    return lax.ppermute(a, axis, [(i, i ^ q) for i in range(n)])


def body(
    layer_inflows,
    output_derivatives,
    picked_specialists,
    dispatch_shares,
    item_sample,
    send_limits,
    gating_projection,
    raising_projection,
    inflow_compressor,
    outgrad_compressor,
):
    n_exp, n_dp = lax.axis_size("exp"), lax.axis_size("dp")
    small = n_exp <= 8
    tokens, width = layer_inflows.shape
    rank = outgrad_compressor.shape[1]
    packed = width * LOCAL_SEATS // ROWS
    units = gating_projection.shape[2]
    size = n_exp * ROWS
    shape = jax.ShapeDtypeStruct

    gate, up = gating_projection[0].T, raising_projection[0].T
    pair_gate, pair_up = swap(gate, "dp", 1), swap(up, "dp", 1)
    arguments = (
        send_limits,
        picked_specialists.T,
        dispatch_shares.T,
        item_sample.reshape(1, tokens),
        layer_inflows,
        output_derivatives,
        outgrad_compressor.T,
    )
    hops = [0, n_exp - 1] + list(range(1, n_exp - 1))
    spaces = [pltpu.SMEM] + [pltpu.VMEM] * (len(arguments) - 1)
    rows = call(
        functools.partial(send_kernel, hops),
        [shape((ROWS, packed + EX_DEV * rank), BF16)] * n_exp,
        [HBM] * len(arguments),
        SEND_LIMIT * MIB,
        flops=4 * size * tokens * packed + 2 * tokens * width * rank,
        moved=4 * tokens * width + 2 * rank * width,
        scratch=[space(a.shape, a.dtype) for space, a in zip(spaces, arguments)]
        + [pltpu.SemaphoreType.DMA((len(arguments),))],
    )(*arguments)

    half = n_dp // 2
    hold = lax.optimization_barrier
    rows = list(rows)
    crossed = [swap(rows[0], "dp", half)]
    pair_gate, pair_up, rows[0] = hold((pair_gate, pair_up, rows[0]))
    chosen_shape = shape((rank, units), BF16)
    gate, up, rows[0], *chosen = call(
        keep_kernel,
        [shape(a.shape, BF16) for a in (gate, up, rows[0])] + [chosen_shape] * 2,
        [VMEM, ANY, ANY, ANY],
        KEEP_LIMIT * MIB,
        out_specs=[ANY, ANY, ANY, VMEM, VMEM],
        moved=8 * units * width,
        scratch=[pltpu.SemaphoreType.DMA((3,))],
    )(inflow_compressor.T, gate, up, rows[0])
    for i, q in enumerate(hops):
        if i:
            rows[i] = swap(rows[i], "exp", q)
            crossed.append(swap(rows[i], "dp", half))
    blocks = {0: rows, half: crossed}
    step = half // 2
    while step > 1:
        for d in list(blocks):
            blocks[d ^ step] = [swap(r, "dp", step) for r in blocks[d]]
        step //= 2

    partials, grads = [], None
    ends = sorted(blocks)
    for ds in [ends] if small else [[d] for d in ends]:
        parts = [r for d in ds for r in blocks[d]]
        *made, first = call(
            functools.partial(sketch_kernel, [size] * len(ds)),
            [shape((rank, size), BF16 if d else F32) for d in ds]
            + [shape((size, EX_DEV * rank), BF16)],
            [VMEM] * (6 + len(parts)),
            20 * MIB,
            flops=8 * len(ds) * size * width * units,
            moved=8 * width * units + 2 * len(ds) * size * packed,
        )(gate, up, pair_gate, pair_up, *chosen, *parts)
        grads = first if grads is None else grads
        partials += [swap(p, "dp", d) if d else p for d, p in zip(ds, made)]
    out = call(
        outer_kernel,
        shape((EX_DEV, rank * rank // 128, 128), F32),
        [VMEM] * (1 + len(partials)),
        8 * MIB,
        flops=2 * size * rank * 2 * rank,
        moved=4 * EX_DEV * rank * rank,
    )(grads, *partials)
    return out.reshape(EX_DEV, 1, rank * rank)


def solution(mesh):
    in_specs = (
        P(("grp", "exp", "dp"), None),
        P(("grp", "exp", "dp"), None),
        P(("grp", "exp", "dp"), None),
        P(("grp", "exp", "dp"), None),
        P(("grp", "exp", "dp")),
        P("grp"),
        P("exp", None, "dp"),
        P("exp", None, "dp"),
        P(),
        P(),
    )
    out_specs = P(("grp", "dp"), "exp", None)
    return jax.shard_map(body, mesh=mesh, in_specs=in_specs, out_specs=out_specs, check_vma=False)
```

```python
import functools

import jax
import jax.numpy as jnp
from jax import lax
from jax.experimental import pallas as pl
from jax.experimental.pallas import tpu as pltpu
from jax.sharding import PartitionSpec as P

EX_DEV = 2
LOCAL_SEATS = 12
ROWS = 16
SPARE = ROWS - LOCAL_SEATS
PARTS = LOCAL_SEATS // SPARE
HALF = ROWS // 2
MIB = 1024 * 1024
KEEP_LIMIT = 49
PIECES = 6
SEND_LIMIT = 56
BF16 = jnp.bfloat16
F32 = jnp.float32


def dot(a, b):
    return jnp.dot(a, b, preferred_element_type=F32)


def dot_t(a, b):
    return lax.dot_general(a, b, (((1,), (1,)), ((), ())), preferred_element_type=F32)


def one_hot(mask):
    return mask.astype(F32).astype(BF16)


def seats_of(limits_ref, picked, experts):
    tokens = picked.shape[1]
    flags = [jnp.max((picked == e).astype(F32), axis=0, keepdims=True) for e in experts]
    flags = jnp.concatenate(flags, axis=0)
    earlier = lax.broadcasted_iota(jnp.int32, (tokens, tokens), 0)
    later = lax.broadcasted_iota(jnp.int32, (tokens, tokens), 1)
    position = dot(flags.astype(BF16), one_hot(earlier < later)).astype(jnp.int32)
    rows = []
    for i, e in enumerate(experts):
        limit = jnp.minimum(limits_ref[e], LOCAL_SEATS)
        at = position[i : i + 1]
        rows.append(jnp.where((flags[i : i + 1] > 0.0) & (at < limit), at, -1))
    return rows


def send_kernel(hops, *refs):
    count = len(hops)
    in_refs, (gate_hbm, up_hbm), refs = refs[:7], refs[7:9], refs[9:]
    out_refs, weights_ref, scratch, sems = refs[:count], refs[count], refs[count + 1 : -1], refs[-1]
    *scratch, held_ref = scratch
    limits_ref, picked_ref, shares_ref, owner_ref, tokens_ref, derivs_ref, compressor_ref = scratch
    units = gate_hbm.shape[0]
    tokens, width = tokens_ref.shape
    chunk = width // (PARTS + 1)
    columns = [slice(i * chunk, (i + 1) * chunk) for i in range(PARTS + 1)]
    copies = [
        pltpu.make_async_copy(a, b, sems.at[i]) for i, (a, b) in enumerate(zip(in_refs, scratch))
    ]
    loads, stores = [], []
    piece = units // PIECES
    for k, source in enumerate((gate_hbm, up_hbm)):
        for j in range(PIECES):
            lines = pl.ds(k * units + j * piece, piece)
            load_sem, store_sem = [sems.at[len(copies) + len(loads) + n] for n in (0, 2 * PIECES)]
            loads.append(
                pltpu.make_async_copy(
                    source.at[pl.ds(j * piece, piece)], held_ref.at[lines], load_sem
                )
            )
            stores.append(
                pltpu.make_async_copy(held_ref.at[lines], weights_ref.at[lines], store_sem)
            )
    for copy in copies[:4] + copies[5:] + copies[4:5] + loads:
        copy.start()
    for copy in copies[:4]:
        copy.wait()
    me = lax.axis_index("exp")
    experts = [jnp.bitwise_xor(me, q) for q in hops]
    picked = picked_ref[...]
    seats = seats_of(limits_ref, picked, experts)
    slot = lax.broadcasted_iota(jnp.int32, (ROWS, tokens), 0)
    near = jnp.concatenate([one_hot(slot == s) for s in seats], axis=0)
    masks = []
    for i in range(PARTS):
        shifted = jnp.where(slot >= LOCAL_SEATS, slot - LOCAL_SEATS + SPARE * i, -2)
        far = jnp.concatenate([one_hot(shifted == s) for s in seats], axis=0)
        masks.append(jnp.concatenate([near, far], axis=1))
    owner = owner_ref[...] - lax.axis_index("dp") * EX_DEV
    owned = [
        jnp.concatenate([one_hot((slot == s) & (owner == n)) for n in range(EX_DEV)], axis=0)
        for s in seats
    ]
    share_rows = [
        jnp.sum(jnp.where(picked == e, shares_ref[...], 0.0), axis=0, keepdims=True)
        for e in experts
    ]
    pad = [jnp.zeros((-count % 8, tokens), F32)] if count % 8 else []
    shares = jnp.concatenate(share_rows + pad, axis=0).T
    for load, store in zip(loads, stores):
        load.wait()
        store.start()
    for copy in copies[4:]:
        copy.wait()
    proj = dot_t(derivs_ref[...], compressor_ref[...])
    last = tokens_ref[:, columns[-1]]
    for i in range(PARTS):
        source = jnp.concatenate([tokens_ref[:, columns[i]], last], axis=0)
        packed = dot(masks[i], source).astype(BF16)
        for q in range(count):
            out_refs[q][:, columns[i]] = packed[q * ROWS : (q + 1) * ROWS]
    for q in range(count):
        grad = (shares[:, q : q + 1] * proj).astype(BF16)
        both = dot(owned[q], grad)
        halves = [both[n * ROWS : (n + 1) * ROWS] for n in range(EX_DEV)]
        out_refs[q][:, PARTS * chunk :] = jnp.concatenate(halves, axis=1).astype(BF16)
    for store in stores:
        store.wait()


def keep_kernel(compressor_ref, weights_hbm, rows_hbm, *refs):
    weights_ref, rows_ref, first_ref, second_ref, sems = refs
    piece = weights_ref.shape[0] // PIECES
    copies = [
        pltpu.make_async_copy(
            weights_hbm.at[pl.ds(i * piece, piece)],
            weights_ref.at[pl.ds(i * piece, piece)],
            sems.at[i],
        )
        for i in range(PIECES)
    ]
    copies.append(pltpu.make_async_copy(rows_hbm, rows_ref, sems.at[PIECES]))
    for copy in copies:
        copy.start()
    chosen = chosen_compressors(compressor_ref, first_ref.shape[1])
    first_ref[...], second_ref[...] = chosen
    for copy in copies:
        copy.wait()


def chosen_compressors(compressor_ref, units):
    place = lax.axis_index("dp")
    rank, total = compressor_ref.shape
    to = lax.broadcasted_iota(jnp.int32, (rank, rank), 0)
    at = lax.broadcasted_iota(jnp.int32, (rank, rank), 1)
    order = one_hot(at == jnp.where(to < rank // 2, 2 * to, 2 * to - rank + 1))
    turned = dot(order, compressor_ref[...]).astype(BF16)
    line = lax.broadcasted_iota(jnp.int32, (total, units), 0)
    unit = lax.broadcasted_iota(jnp.int32, (total, units), 1)
    return [
        dot(turned, one_hot(line == unit + jnp.bitwise_xor(place, k) * units)).astype(BF16)
        for k in range(2)
    ]


def sketch_kernel(sizes, own_ref, pair_ref, first_ref, second_ref, *refs):
    out_refs, grads_ref = refs[-1 - len(sizes) : -1], refs[-1]
    block_refs = refs[: -1 - len(sizes)]
    units, width = own_ref.shape[0] // 2, own_ref.shape[1]
    chunk = width // (PARTS + 1)
    size = sum(sizes)
    messages = size // ROWS
    low = lax.broadcasted_iota(jnp.int32, (1, HALF, 1), 1) < SPARE
    columns = [slice(i * chunk, (i + 1) * chunk) for i in range(PARTS + 1)]
    rows = [jnp.concatenate([r[:, c] for r in block_refs], axis=0) for c in columns[:PARTS]]
    tails = [r.astype(F32).reshape(messages, 2, HALF, chunk)[:, 1] for r in rows]

    def turn(a):
        return jnp.concatenate([a[:, SPARE:], a[:, :SPARE]], axis=1)

    top = jnp.where(low, turn(tails[0]), tails[1])
    bottom = jnp.where(low, turn(tails[2]), 0.0)
    rows.append(jnp.stack([top, bottom], axis=1).reshape(size, chunk).astype(BF16))
    seat = lax.broadcasted_iota(jnp.int32, (size, 1), 0) % ROWS

    def product(w, lines):
        total = dot_t(rows[0], w[lines, columns[0]])
        for c, r in zip(columns[1:], rows[1:]):
            total = total + dot_t(r, w[lines, c])
        return total

    sketch = None
    for ref, compressor in ((own_ref, first_ref), (pair_ref, second_ref)):
        gate, up = product(ref, slice(0, units)), product(ref, slice(units, 2 * units))
        hidden = gate / (1.0 + jnp.exp(-gate)) * up
        hidden = jnp.where(seat < LOCAL_SEATS, hidden, 0.0).astype(BF16)
        term = dot_t(compressor[...], hidden)
        sketch = term if sketch is None else sketch + term
    at = 0
    for n, ref in zip(sizes, out_refs):
        ref[...] = sketch[:, at : at + n].astype(ref.dtype)
        at += n
    first = 0
    for r in block_refs:
        if first < sizes[0]:
            grads_ref[first : first + r.shape[0]] = r[:, PARTS * chunk :]
        first += r.shape[0]


def outer_kernel(grads_ref, *refs):
    partial_refs, out_ref = refs[:-1], refs[-1]
    total = partial_refs[0][...]
    for r in partial_refs[1:]:
        total = total + r[...].astype(F32)
    rank = total.shape[0]
    product = dot(total.astype(BF16), grads_ref[...])
    even, odd = product[: rank // 2], product[rank // 2 :]
    for n in range(EX_DEV):
        columns = slice(n * rank, (n + 1) * rank)
        out_ref[n] = jnp.concatenate([even[:, columns], odd[:, columns]], axis=1)


VMEM = pl.BlockSpec(memory_space=pltpu.VMEM)
SMEM = pl.BlockSpec(memory_space=pltpu.SMEM)
HBM = pl.BlockSpec(memory_space=pltpu.HBM)
ANY = pl.BlockSpec(memory_space=pl.ANY)


def call(kernel, out_shape, in_specs, limit, flops=0, moved=0, scratch=(), out_specs=None):
    return pl.pallas_call(
        kernel,
        out_shape=out_shape,
        in_specs=in_specs,
        out_specs=out_specs or jax.tree.map(lambda _: VMEM, out_shape),
        scratch_shapes=list(scratch),
        compiler_params=pltpu.CompilerParams(vmem_limit_bytes=limit),
        cost_estimate=pl.CostEstimate(flops=flops, bytes_accessed=moved, transcendentals=0),
    )


def swap(a, axis, q):
    n = lax.axis_size(axis)
    return lax.ppermute(a, axis, [(i, i ^ q) for i in range(n)])


def body(
    layer_inflows,
    output_derivatives,
    picked_specialists,
    dispatch_shares,
    item_sample,
    send_limits,
    gating_projection,
    raising_projection,
    inflow_compressor,
    outgrad_compressor,
):
    n_exp, n_dp = lax.axis_size("exp"), lax.axis_size("dp")
    small = n_exp <= 8
    tokens, width = layer_inflows.shape
    rank = outgrad_compressor.shape[1]
    packed = width * LOCAL_SEATS // ROWS
    units = gating_projection.shape[2]
    size = n_exp * ROWS
    shape = jax.ShapeDtypeStruct

    gate, up = gating_projection[0].T, raising_projection[0].T
    arguments = (
        send_limits,
        picked_specialists.T,
        dispatch_shares.T,
        item_sample.reshape(1, tokens),
        layer_inflows,
        output_derivatives,
        outgrad_compressor.T,
    )
    hops = [0, 1] + list(range(n_exp - 1, 1, -1))
    spaces = [pltpu.SMEM] + [pltpu.VMEM] * (len(arguments) - 1)
    *rows, weights = call(
        functools.partial(send_kernel, hops),
        [shape((ROWS, packed + EX_DEV * rank), BF16)] * n_exp + [shape((2 * units, width), BF16)],
        [HBM] * (len(arguments) + 2),
        SEND_LIMIT * MIB,
        out_specs=[VMEM] * n_exp + [ANY],
        flops=4 * size * tokens * packed + 2 * tokens * width * rank,
        moved=4 * tokens * width + 2 * rank * width + 8 * units * width,
        scratch=[space(a.shape, a.dtype) for space, a in zip(spaces, arguments)]
        + [pltpu.VMEM((2 * units, width), BF16), pltpu.SemaphoreType.DMA((len(arguments) + 4 * PIECES,))],
    )(*arguments, gate, up)
    pair_weights = swap(weights, "dp", 1)

    half = n_dp // 2
    crossed = [swap(rows[0], "dp", half)]
    chosen_shape = shape((rank, units), BF16)
    weights, rows[0], *chosen = call(
        keep_kernel,
        [shape(weights.shape, BF16), shape(rows[0].shape, BF16), chosen_shape, chosen_shape],
        [VMEM, ANY, ANY],
        KEEP_LIMIT * MIB,
        out_specs=[ANY, ANY, VMEM, VMEM],
        moved=8 * units * width,
        scratch=[pltpu.SemaphoreType.DMA((PIECES + 1,))],
    )(inflow_compressor.T, weights, rows[0])
    for i, q in enumerate(hops):
        if i:
            rows[i] = swap(rows[i], "exp", q)
            crossed.append(swap(rows[i], "dp", half))
    blocks = {0: rows, half: crossed}
    step = half // 2
    while step > 1:
        for d in list(blocks):
            blocks[d ^ step] = [swap(r, "dp", step) for r in blocks[d]]
        step //= 2

    partials, grads = [], None
    ends = sorted(blocks)
    for ds in [ends] if small else [[d] for d in ends]:
        parts = [r for d in ds for r in blocks[d]]
        *made, first = call(
            functools.partial(sketch_kernel, [size] * len(ds)),
            [shape((rank, size), BF16 if d else F32) for d in ds]
            + [shape((size, EX_DEV * rank), BF16)],
            [VMEM] * (4 + len(parts)),
            20 * MIB,
            flops=8 * len(ds) * size * width * units,
            moved=8 * width * units + 2 * len(ds) * size * packed,
        )(weights, pair_weights, *chosen, *parts)
        grads = first if grads is None else grads
        partials += [swap(p, "dp", d) if d else p for d, p in zip(ds, made)]
    out = call(
        outer_kernel,
        shape((EX_DEV, rank * rank // 128, 128), F32),
        [VMEM] * (1 + len(partials)),
        8 * MIB,
        flops=2 * size * rank * 2 * rank,
        moved=4 * EX_DEV * rank * rank,
    )(grads, *partials)
    return out.reshape(EX_DEV, 1, rank * rank)


def solution(mesh):
    in_specs = (
        P(("grp", "exp", "dp"), None),
        P(("grp", "exp", "dp"), None),
        P(("grp", "exp", "dp"), None),
        P(("grp", "exp", "dp"), None),
        P(("grp", "exp", "dp")),
        P("grp"),
        P("exp", None, "dp"),
        P("exp", None, "dp"),
        P(),
        P(),
    )
    out_specs = P(("grp", "dp"), "exp", None)
    return jax.shard_map(body, mesh=mesh, in_specs=in_specs, out_specs=out_specs, check_vma=False)
```

```python
import functools

import jax
import jax.numpy as jnp
from jax import lax
from jax.experimental import pallas as pl
from jax.experimental.pallas import tpu as pltpu
from jax.sharding import PartitionSpec as P

EX_DEV = 2
LOCAL_SEATS = 12
ROWS = 16
SPARE = ROWS - LOCAL_SEATS
PARTS = LOCAL_SEATS // SPARE
HALF = ROWS // 2
MIB = 1024 * 1024
KEEP_LIMIT = 49
PIECES = 6
SEND_LIMIT = 56
BF16 = jnp.bfloat16
F32 = jnp.float32


def dot(a, b):
    return jnp.dot(a, b, preferred_element_type=F32)


def dot_t(a, b):
    return lax.dot_general(a, b, (((1,), (1,)), ((), ())), preferred_element_type=F32)


def one_hot(mask):
    return mask.astype(F32).astype(BF16)


def seats_of(limits_ref, picked, experts):
    tokens = picked.shape[1]
    flags = [jnp.max((picked == e).astype(F32), axis=0, keepdims=True) for e in experts]
    flags = jnp.concatenate(flags, axis=0)
    earlier = lax.broadcasted_iota(jnp.int32, (tokens, tokens), 0)
    later = lax.broadcasted_iota(jnp.int32, (tokens, tokens), 1)
    position = dot(flags.astype(BF16), one_hot(earlier < later)).astype(jnp.int32)
    rows = []
    for i, e in enumerate(experts):
        limit = jnp.minimum(limits_ref[e], LOCAL_SEATS)
        at = position[i : i + 1]
        rows.append(jnp.where((flags[i : i + 1] > 0.0) & (at < limit), at, -1))
    return rows


def send_kernel(hops, *refs):
    count = len(hops)
    in_refs, (gate_hbm, up_hbm), refs = refs[:7], refs[7:9], refs[9:]
    out_refs, weights_ref, scratch, sems = refs[:count], refs[count], refs[count + 1 : -1], refs[-1]
    *scratch, held_ref = scratch
    limits_ref, picked_ref, shares_ref, owner_ref, tokens_ref, derivs_ref, compressor_ref = scratch
    units = gate_hbm.shape[0]
    tokens, width = tokens_ref.shape
    chunk = width // (PARTS + 1)
    columns = [slice(i * chunk, (i + 1) * chunk) for i in range(PARTS + 1)]
    copies = [
        pltpu.make_async_copy(a, b, sems.at[i]) for i, (a, b) in enumerate(zip(in_refs, scratch))
    ]
    loads, stores = [], []
    piece = units // PIECES
    for k, source in enumerate((gate_hbm, up_hbm)):
        for j in range(PIECES):
            lines = pl.ds(k * units + j * piece, piece)
            load_sem, store_sem = [sems.at[len(copies) + len(loads) + n] for n in (0, 2 * PIECES)]
            loads.append(
                pltpu.make_async_copy(
                    source.at[pl.ds(j * piece, piece)], held_ref.at[lines], load_sem
                )
            )
            stores.append(
                pltpu.make_async_copy(held_ref.at[lines], weights_ref.at[lines], store_sem)
            )
    for copy in copies[:4] + copies[5:] + copies[4:5] + loads:
        copy.start()
    for copy in copies[:4]:
        copy.wait()
    me = lax.axis_index("exp")
    experts = [jnp.bitwise_xor(me, q) for q in hops]
    picked = picked_ref[...]
    seats = seats_of(limits_ref, picked, experts)
    slot = lax.broadcasted_iota(jnp.int32, (ROWS, tokens), 0)
    near = jnp.concatenate([one_hot(slot == s) for s in seats], axis=0)
    masks = []
    for i in range(PARTS):
        shifted = jnp.where(slot >= LOCAL_SEATS, slot - LOCAL_SEATS + SPARE * i, -2)
        far = jnp.concatenate([one_hot(shifted == s) for s in seats], axis=0)
        masks.append(jnp.concatenate([near, far], axis=1))
    owner = owner_ref[...] - lax.axis_index("dp") * EX_DEV
    owned = [
        jnp.concatenate([one_hot((slot == s) & (owner == n)) for n in range(EX_DEV)], axis=0)
        for s in seats
    ]
    share_rows = [
        jnp.sum(jnp.where(picked == e, shares_ref[...], 0.0), axis=0, keepdims=True)
        for e in experts
    ]
    pad = [jnp.zeros((-count % 8, tokens), F32)] if count % 8 else []
    shares = jnp.concatenate(share_rows + pad, axis=0).T
    for load, store in zip(loads, stores):
        load.wait()
        store.start()
    for copy in copies[4:]:
        copy.wait()
    proj = dot_t(derivs_ref[...], compressor_ref[...])
    last = tokens_ref[:, columns[-1]]
    for i in range(PARTS):
        source = jnp.concatenate([tokens_ref[:, columns[i]], last], axis=0)
        packed = dot(masks[i], source).astype(BF16)
        for q in range(count):
            out_refs[q][:, columns[i]] = packed[q * ROWS : (q + 1) * ROWS]
    for q in range(count):
        grad = (shares[:, q : q + 1] * proj).astype(BF16)
        both = dot(owned[q], grad)
        halves = [both[n * ROWS : (n + 1) * ROWS] for n in range(EX_DEV)]
        out_refs[q][:, PARTS * chunk :] = jnp.concatenate(halves, axis=1).astype(BF16)
    for store in stores:
        store.wait()


def keep_kernel(compressor_ref, weights_hbm, rows_hbm, *refs):
    weights_ref, rows_ref, first_ref, second_ref, sems = refs
    piece = weights_ref.shape[0] // PIECES
    copies = [
        pltpu.make_async_copy(
            weights_hbm.at[pl.ds(i * piece, piece)],
            weights_ref.at[pl.ds(i * piece, piece)],
            sems.at[i],
        )
        for i in range(PIECES)
    ]
    copies.append(pltpu.make_async_copy(rows_hbm, rows_ref, sems.at[PIECES]))
    for copy in copies:
        copy.start()
    chosen = chosen_compressors(compressor_ref, first_ref.shape[1])
    first_ref[...], second_ref[...] = chosen
    for copy in copies:
        copy.wait()


def chosen_compressors(compressor_ref, units):
    place = lax.axis_index("dp")
    rank, total = compressor_ref.shape
    to = lax.broadcasted_iota(jnp.int32, (rank, rank), 0)
    at = lax.broadcasted_iota(jnp.int32, (rank, rank), 1)
    order = one_hot(at == jnp.where(to < rank // 2, 2 * to, 2 * to - rank + 1))
    turned = dot(order, compressor_ref[...]).astype(BF16)
    line = lax.broadcasted_iota(jnp.int32, (total, units), 0)
    unit = lax.broadcasted_iota(jnp.int32, (total, units), 1)
    return [
        dot(turned, one_hot(line == unit + jnp.bitwise_xor(place, k) * units)).astype(BF16)
        for k in range(2)
    ]


def sketch_kernel(sizes, own_ref, pair_ref, first_ref, second_ref, *refs):
    out_refs, grads_ref = refs[-1 - len(sizes) : -1], refs[-1]
    block_refs = refs[: -1 - len(sizes)]
    units, width = own_ref.shape[0] // 2, own_ref.shape[1]
    chunk = width // (PARTS + 1)
    size = sum(sizes)
    messages = size // ROWS
    low = lax.broadcasted_iota(jnp.int32, (1, HALF, 1), 1) < SPARE
    columns = [slice(i * chunk, (i + 1) * chunk) for i in range(PARTS + 1)]
    rows = [jnp.concatenate([r[:, c] for r in block_refs], axis=0) for c in columns[:PARTS]]
    tails = [r.astype(F32).reshape(messages, 2, HALF, chunk)[:, 1] for r in rows]

    def turn(a):
        return jnp.concatenate([a[:, SPARE:], a[:, :SPARE]], axis=1)

    top = jnp.where(low, turn(tails[0]), tails[1])
    bottom = jnp.where(low, turn(tails[2]), 0.0)
    rows.append(jnp.stack([top, bottom], axis=1).reshape(size, chunk).astype(BF16))
    seat = lax.broadcasted_iota(jnp.int32, (size, 1), 0) % ROWS

    def product(w, lines):
        total = dot_t(rows[0], w[lines, columns[0]])
        for c, r in zip(columns[1:], rows[1:]):
            total = total + dot_t(r, w[lines, c])
        return total

    sketch = None
    for ref, compressor in ((own_ref, first_ref), (pair_ref, second_ref)):
        gate, up = product(ref, slice(0, units)), product(ref, slice(units, 2 * units))
        hidden = gate / (1.0 + jnp.exp(-gate)) * up
        hidden = jnp.where(seat < LOCAL_SEATS, hidden, 0.0).astype(BF16)
        term = dot_t(compressor[...], hidden)
        sketch = term if sketch is None else sketch + term
    at = 0
    for n, ref in zip(sizes, out_refs):
        ref[...] = sketch[:, at : at + n].astype(ref.dtype)
        at += n
    first = 0
    for r in block_refs:
        if first < sizes[0]:
            grads_ref[first : first + r.shape[0]] = r[:, PARTS * chunk :]
        first += r.shape[0]


def outer_kernel(grads_ref, *refs):
    partial_refs, out_ref = refs[:-1], refs[-1]
    total = partial_refs[0][...]
    for r in partial_refs[1:]:
        total = total + r[...].astype(F32)
    rank = total.shape[0]
    product = dot(total.astype(BF16), grads_ref[...])
    even, odd = product[: rank // 2], product[rank // 2 :]
    for n in range(EX_DEV):
        columns = slice(n * rank, (n + 1) * rank)
        out_ref[n] = jnp.concatenate([even[:, columns], odd[:, columns]], axis=1)


VMEM = pl.BlockSpec(memory_space=pltpu.VMEM)
SMEM = pl.BlockSpec(memory_space=pltpu.SMEM)
HBM = pl.BlockSpec(memory_space=pltpu.HBM)
ANY = pl.BlockSpec(memory_space=pl.ANY)


def call(kernel, out_shape, in_specs, limit, flops=0, moved=0, scratch=(), out_specs=None):
    return pl.pallas_call(
        kernel,
        out_shape=out_shape,
        in_specs=in_specs,
        out_specs=out_specs or jax.tree.map(lambda _: VMEM, out_shape),
        scratch_shapes=list(scratch),
        compiler_params=pltpu.CompilerParams(vmem_limit_bytes=limit),
        cost_estimate=pl.CostEstimate(flops=flops, bytes_accessed=moved, transcendentals=0),
    )


def swap(a, axis, q):
    n = lax.axis_size(axis)
    return lax.ppermute(a, axis, [(i, i ^ q) for i in range(n)])


def body(
    layer_inflows,
    output_derivatives,
    picked_specialists,
    dispatch_shares,
    item_sample,
    send_limits,
    gating_projection,
    raising_projection,
    inflow_compressor,
    outgrad_compressor,
):
    n_exp, n_dp = lax.axis_size("exp"), lax.axis_size("dp")
    small = n_exp <= 8
    tokens, width = layer_inflows.shape
    rank = outgrad_compressor.shape[1]
    packed = width * LOCAL_SEATS // ROWS
    units = gating_projection.shape[2]
    size = n_exp * ROWS
    shape = jax.ShapeDtypeStruct

    gate, up = gating_projection[0].T, raising_projection[0].T
    arguments = (
        send_limits,
        picked_specialists.T,
        dispatch_shares.T,
        item_sample.reshape(1, tokens),
        layer_inflows,
        output_derivatives,
        outgrad_compressor.T,
    )
    hops = [0] + list(range(n_exp - 1, 0, -1))
    spaces = [pltpu.SMEM] + [pltpu.VMEM] * (len(arguments) - 1)
    *rows, weights = call(
        functools.partial(send_kernel, hops),
        [shape((ROWS, packed + EX_DEV * rank), BF16)] * n_exp + [shape((2 * units, width), BF16)],
        [HBM] * (len(arguments) + 2),
        SEND_LIMIT * MIB,
        out_specs=[VMEM] * n_exp + [ANY],
        flops=4 * size * tokens * packed + 2 * tokens * width * rank,
        moved=4 * tokens * width + 2 * rank * width + 8 * units * width,
        scratch=[space(a.shape, a.dtype) for space, a in zip(spaces, arguments)]
        + [pltpu.VMEM((2 * units, width), BF16), pltpu.SemaphoreType.DMA((len(arguments) + 4 * PIECES,))],
    )(*arguments, gate, up)
    pair_weights = swap(weights, "dp", 1)

    half = n_dp // 2
    crossed = [swap(rows[0], "dp", half)]
    chosen_shape = shape((rank, units), BF16)
    weights, rows[0], *chosen = call(
        keep_kernel,
        [shape(weights.shape, BF16), shape(rows[0].shape, BF16), chosen_shape, chosen_shape],
        [VMEM, ANY, ANY],
        KEEP_LIMIT * MIB,
        out_specs=[ANY, ANY, VMEM, VMEM],
        moved=8 * units * width,
        scratch=[pltpu.SemaphoreType.DMA((PIECES + 1,))],
    )(inflow_compressor.T, weights, rows[0])
    for i, q in enumerate(hops):
        if i:
            rows[i] = swap(rows[i], "exp", q)
            crossed.append(swap(rows[i], "dp", half))
    blocks = {0: rows, half: crossed}
    step = half // 2
    while step > 1:
        for d in list(blocks):
            blocks[d ^ step] = [swap(r, "dp", step) for r in blocks[d]]
        step //= 2

    partials, grads = [], None
    ends = sorted(blocks)
    for ds in [ends] if small else [[d] for d in ends]:
        parts = [r for d in ds for r in blocks[d]]
        *made, first = call(
            functools.partial(sketch_kernel, [size] * len(ds)),
            [shape((rank, size), BF16 if d else F32) for d in ds]
            + [shape((size, EX_DEV * rank), BF16)],
            [VMEM] * (4 + len(parts)),
            20 * MIB,
            flops=8 * len(ds) * size * width * units,
            moved=8 * width * units + 2 * len(ds) * size * packed,
        )(weights, pair_weights, *chosen, *parts)
        grads = first if grads is None else grads
        partials += [swap(p, "dp", d) if d else p for d, p in zip(ds, made)]
    out = call(
        outer_kernel,
        shape((EX_DEV, rank * rank // 128, 128), F32),
        [VMEM] * (1 + len(partials)),
        8 * MIB,
        flops=2 * size * rank * 2 * rank,
        moved=4 * EX_DEV * rank * rank,
    )(grads, *partials)
    return out.reshape(EX_DEV, 1, rank * rank)


def solution(mesh):
    in_specs = (
        P(("grp", "exp", "dp"), None),
        P(("grp", "exp", "dp"), None),
        P(("grp", "exp", "dp"), None),
        P(("grp", "exp", "dp"), None),
        P(("grp", "exp", "dp")),
        P("grp"),
        P("exp", None, "dp"),
        P("exp", None, "dp"),
        P(),
        P(),
    )
    out_specs = P(("grp", "dp"), "exp", None)
    return jax.shard_map(body, mesh=mesh, in_specs=in_specs, out_specs=out_specs, check_vma=False)
```

```python
import functools

import jax
import jax.numpy as jnp
from jax import lax
from jax.experimental import pallas as pl
from jax.experimental.pallas import tpu as pltpu
from jax.sharding import PartitionSpec as P

EX_DEV = 2
LOCAL_SEATS = 12
ROWS = 16
SPARE = ROWS - LOCAL_SEATS
PARTS = LOCAL_SEATS // SPARE
HALF = ROWS // 2
MIB = 1024 * 1024
KEEP_LIMIT = 48
SEND_LIMIT = 56
BF16 = jnp.bfloat16
F32 = jnp.float32


def dot(a, b):
    return jnp.dot(a, b, preferred_element_type=F32)


def dot_t(a, b):
    return lax.dot_general(a, b, (((1,), (1,)), ((), ())), preferred_element_type=F32)


def one_hot(mask):
    return mask.astype(F32).astype(BF16)


def seats_of(limits_ref, picked, experts):
    tokens = picked.shape[1]
    flags = [jnp.max((picked == e).astype(F32), axis=0, keepdims=True) for e in experts]
    flags = jnp.concatenate(flags, axis=0)
    earlier = lax.broadcasted_iota(jnp.int32, (tokens, tokens), 0)
    later = lax.broadcasted_iota(jnp.int32, (tokens, tokens), 1)
    position = dot(flags.astype(BF16), one_hot(earlier < later)).astype(jnp.int32)
    rows = []
    for i, e in enumerate(experts):
        limit = jnp.minimum(limits_ref[e], LOCAL_SEATS)
        at = position[i : i + 1]
        rows.append(jnp.where((flags[i : i + 1] > 0.0) & (at < limit), at, -1))
    return rows


def send_kernel(hops, *refs):
    count = len(hops)
    in_refs, out_refs, scratch, sems = refs[:7], refs[7 : 7 + count], refs[7 + count : -1], refs[-1]
    limits_ref, picked_ref, shares_ref, owner_ref, tokens_ref, derivs_ref, compressor_ref = scratch
    tokens, width = tokens_ref.shape
    chunk = width // (PARTS + 1)
    columns = [slice(i * chunk, (i + 1) * chunk) for i in range(PARTS + 1)]
    copies = [
        pltpu.make_async_copy(a, b, sems.at[i]) for i, (a, b) in enumerate(zip(in_refs, scratch))
    ]
    for copy in copies:
        copy.start()
    for copy in copies[:4]:
        copy.wait()
    me = lax.axis_index("exp")
    experts = [jnp.bitwise_xor(me, q) for q in hops]
    picked = picked_ref[...]
    seats = seats_of(limits_ref, picked, experts)
    slot = lax.broadcasted_iota(jnp.int32, (ROWS, tokens), 0)
    near = jnp.concatenate([one_hot(slot == s) for s in seats], axis=0)
    masks = []
    for i in range(PARTS):
        shifted = jnp.where(slot >= LOCAL_SEATS, slot - LOCAL_SEATS + SPARE * i, -2)
        far = jnp.concatenate([one_hot(shifted == s) for s in seats], axis=0)
        masks.append(jnp.concatenate([near, far], axis=1))
    owner = owner_ref[...] - lax.axis_index("dp") * EX_DEV
    owned = [
        jnp.concatenate([one_hot((slot == s) & (owner == n)) for n in range(EX_DEV)], axis=0)
        for s in seats
    ]
    share_rows = [
        jnp.sum(jnp.where(picked == e, shares_ref[...], 0.0), axis=0, keepdims=True)
        for e in experts
    ]
    pad = [jnp.zeros((-count % 8, tokens), F32)] if count % 8 else []
    shares = jnp.concatenate(share_rows + pad, axis=0).T
    for copy in copies[4:]:
        copy.wait()
    proj = dot_t(derivs_ref[...], compressor_ref[...])
    last = tokens_ref[:, columns[-1]]
    for i in range(PARTS):
        source = jnp.concatenate([tokens_ref[:, columns[i]], last], axis=0)
        packed = dot(masks[i], source).astype(BF16)
        for q in range(count):
            out_refs[q][:, columns[i]] = packed[q * ROWS : (q + 1) * ROWS]
    for q in range(count):
        grad = (shares[:, q : q + 1] * proj).astype(BF16)
        both = dot(owned[q], grad)
        halves = [both[n * ROWS : (n + 1) * ROWS] for n in range(EX_DEV)]
        out_refs[q][:, PARTS * chunk :] = jnp.concatenate(halves, axis=1).astype(BF16)


def keep_kernel(compressor_ref, gate_hbm, up_hbm, rows_hbm, *refs):
    gate_ref, up_ref, rows_ref, first_ref, second_ref, sems = refs
    pairs = ((gate_hbm, gate_ref), (up_hbm, up_ref), (rows_hbm, rows_ref))
    copies = [pltpu.make_async_copy(a, b, sems.at[i]) for i, (a, b) in enumerate(pairs)]
    for copy in copies:
        copy.start()
    chosen = chosen_compressors(compressor_ref, first_ref.shape[1])
    first_ref[...], second_ref[...] = chosen
    for copy in copies:
        copy.wait()


def chosen_compressors(compressor_ref, units):
    place = lax.axis_index("dp")
    rank, total = compressor_ref.shape
    to = lax.broadcasted_iota(jnp.int32, (rank, rank), 0)
    at = lax.broadcasted_iota(jnp.int32, (rank, rank), 1)
    order = one_hot(at == jnp.where(to < rank // 2, 2 * to, 2 * to - rank + 1))
    turned = dot(order, compressor_ref[...]).astype(BF16)
    line = lax.broadcasted_iota(jnp.int32, (total, units), 0)
    unit = lax.broadcasted_iota(jnp.int32, (total, units), 1)
    return [
        dot(turned, one_hot(line == unit + jnp.bitwise_xor(place, k) * units)).astype(BF16)
        for k in range(2)
    ]


def sketch_kernel(sizes, gate_ref, up_ref, pair_gate_ref, pair_up_ref, first_ref, second_ref, *refs):
    out_refs, grads_ref = refs[-1 - len(sizes) : -1], refs[-1]
    block_refs = refs[: -1 - len(sizes)]
    units, width = gate_ref.shape
    chunk = width // (PARTS + 1)
    size = sum(sizes)
    messages = size // ROWS
    low = lax.broadcasted_iota(jnp.int32, (1, HALF, 1), 1) < SPARE
    columns = [slice(i * chunk, (i + 1) * chunk) for i in range(PARTS + 1)]
    rows = [jnp.concatenate([r[:, c] for r in block_refs], axis=0) for c in columns[:PARTS]]
    tails = [r.astype(F32).reshape(messages, 2, HALF, chunk)[:, 1] for r in rows]

    def turn(a):
        return jnp.concatenate([a[:, SPARE:], a[:, :SPARE]], axis=1)

    top = jnp.where(low, turn(tails[0]), tails[1])
    bottom = jnp.where(low, turn(tails[2]), 0.0)
    rows.append(jnp.stack([top, bottom], axis=1).reshape(size, chunk).astype(BF16))
    seat = lax.broadcasted_iota(jnp.int32, (size, 1), 0) % ROWS

    def product(w):
        total = dot_t(rows[0], w[:, columns[0]])
        for c, r in zip(columns[1:], rows[1:]):
            total = total + dot_t(r, w[:, c])
        return total

    sketch = None
    for gate_w, up_w, compressor in (
        (gate_ref, up_ref, first_ref),
        (pair_gate_ref, pair_up_ref, second_ref),
    ):
        gate, up = product(gate_w), product(up_w)
        hidden = gate / (1.0 + jnp.exp(-gate)) * up
        hidden = jnp.where(seat < LOCAL_SEATS, hidden, 0.0).astype(BF16)
        term = dot_t(compressor[...], hidden)
        sketch = term if sketch is None else sketch + term
    at = 0
    for n, ref in zip(sizes, out_refs):
        ref[...] = sketch[:, at : at + n].astype(ref.dtype)
        at += n
    first = 0
    for r in block_refs:
        if first < sizes[0]:
            grads_ref[first : first + r.shape[0]] = r[:, PARTS * chunk :]
        first += r.shape[0]


def outer_kernel(grads_ref, *refs):
    partial_refs, out_ref = refs[:-1], refs[-1]
    total = partial_refs[0][...]
    for r in partial_refs[1:]:
        total = total + r[...].astype(F32)
    rank = total.shape[0]
    product = dot(total.astype(BF16), grads_ref[...])
    even, odd = product[: rank // 2], product[rank // 2 :]
    for n in range(EX_DEV):
        columns = slice(n * rank, (n + 1) * rank)
        out_ref[n] = jnp.concatenate([even[:, columns], odd[:, columns]], axis=1)


VMEM = pl.BlockSpec(memory_space=pltpu.VMEM)
SMEM = pl.BlockSpec(memory_space=pltpu.SMEM)
HBM = pl.BlockSpec(memory_space=pltpu.HBM)
ANY = pl.BlockSpec(memory_space=pl.ANY)


def call(kernel, out_shape, in_specs, limit, flops=0, moved=0, scratch=(), out_specs=None):
    return pl.pallas_call(
        kernel,
        out_shape=out_shape,
        in_specs=in_specs,
        out_specs=out_specs or jax.tree.map(lambda _: VMEM, out_shape),
        scratch_shapes=list(scratch),
        compiler_params=pltpu.CompilerParams(vmem_limit_bytes=limit),
        cost_estimate=pl.CostEstimate(flops=flops, bytes_accessed=moved, transcendentals=0),
    )


def swap(a, axis, q):
    n = lax.axis_size(axis)
    return lax.ppermute(a, axis, [(i, i ^ q) for i in range(n)])


def body(
    layer_inflows,
    output_derivatives,
    picked_specialists,
    dispatch_shares,
    item_sample,
    send_limits,
    gating_projection,
    raising_projection,
    inflow_compressor,
    outgrad_compressor,
):
    n_exp, n_dp = lax.axis_size("exp"), lax.axis_size("dp")
    small = n_exp <= 8
    tokens, width = layer_inflows.shape
    rank = outgrad_compressor.shape[1]
    packed = width * LOCAL_SEATS // ROWS
    units = gating_projection.shape[2]
    size = n_exp * ROWS
    shape = jax.ShapeDtypeStruct

    gate, up = gating_projection[0].T, raising_projection[0].T
    pair_gate, pair_up = swap(gate, "dp", 1), swap(up, "dp", 1)
    arguments = (
        send_limits,
        picked_specialists.T,
        dispatch_shares.T,
        item_sample.reshape(1, tokens),
        layer_inflows,
        output_derivatives,
        outgrad_compressor.T,
    )
    hops = [0, n_exp - 1] + list(range(1, n_exp - 1))
    spaces = [pltpu.SMEM] + [pltpu.VMEM] * (len(arguments) - 1)
    rows = call(
        functools.partial(send_kernel, hops),
        [shape((ROWS, packed + EX_DEV * rank), BF16)] * n_exp,
        [HBM] * len(arguments),
        SEND_LIMIT * MIB,
        flops=4 * size * tokens * packed + 2 * tokens * width * rank,
        moved=4 * tokens * width + 2 * rank * width,
        scratch=[space(a.shape, a.dtype) for space, a in zip(spaces, arguments)]
        + [pltpu.SemaphoreType.DMA((len(arguments),))],
    )(*arguments)

    half = n_dp // 2
    hold = lax.optimization_barrier
    rows = list(rows)
    crossed = [swap(rows[0], "dp", half)]
    chosen_shape = shape((rank, units), BF16)
    gate, up, rows[0], *chosen = call(
        keep_kernel,
        [shape(a.shape, BF16) for a in (gate, up, rows[0])] + [chosen_shape] * 2,
        [VMEM, ANY, ANY, ANY],
        KEEP_LIMIT * MIB,
        out_specs=[ANY, ANY, ANY, VMEM, VMEM],
        moved=8 * units * width,
        scratch=[pltpu.SemaphoreType.DMA((3,))],
    )(inflow_compressor.T, gate, up, rows[0])
    for i, q in enumerate(hops):
        if i:
            rows[i] = swap(rows[i], "exp", q)
            if i == n_exp - 1:
                pair_gate, crossed[0], rows[i] = hold((pair_gate, crossed[0], rows[i]))
            crossed.append(swap(rows[i], "dp", half))
    blocks = {0: rows, half: crossed}
    step = half // 2
    while step > 1:
        for d in list(blocks):
            blocks[d ^ step] = [swap(r, "dp", step) for r in blocks[d]]
        step //= 2

    partials, grads = [], None
    ends = sorted(blocks)
    for ds in [ends] if small else [[d] for d in ends]:
        parts = [r for d in ds for r in blocks[d]]
        *made, first = call(
            functools.partial(sketch_kernel, [size] * len(ds)),
            [shape((rank, size), BF16 if d else F32) for d in ds]
            + [shape((size, EX_DEV * rank), BF16)],
            [VMEM] * (6 + len(parts)),
            20 * MIB,
            flops=8 * len(ds) * size * width * units,
            moved=8 * width * units + 2 * len(ds) * size * packed,
        )(gate, up, pair_gate, pair_up, *chosen, *parts)
        grads = first if grads is None else grads
        partials += [swap(p, "dp", d) if d else p for d, p in zip(ds, made)]
    out = call(
        outer_kernel,
        shape((EX_DEV, rank * rank // 128, 128), F32),
        [VMEM] * (1 + len(partials)),
        8 * MIB,
        flops=2 * size * rank * 2 * rank,
        moved=4 * EX_DEV * rank * rank,
    )(grads, *partials)
    return out.reshape(EX_DEV, 1, rank * rank)


def solution(mesh):
    in_specs = (
        P(("grp", "exp", "dp"), None),
        P(("grp", "exp", "dp"), None),
        P(("grp", "exp", "dp"), None),
        P(("grp", "exp", "dp"), None),
        P(("grp", "exp", "dp")),
        P("grp"),
        P("exp", None, "dp"),
        P("exp", None, "dp"),
        P(),
        P(),
    )
    out_specs = P(("grp", "dp"), "exp", None)
    return jax.shard_map(body, mesh=mesh, in_specs=in_specs, out_specs=out_specs, check_vma=False)
```

```python
import functools

import jax
import jax.numpy as jnp
from jax import lax
from jax.experimental import pallas as pl
from jax.experimental.pallas import tpu as pltpu
from jax.sharding import PartitionSpec as P

EX_DEV = 2
LOCAL_SEATS = 12
ROWS = 16
SPARE = ROWS - LOCAL_SEATS
PARTS = LOCAL_SEATS // SPARE
HALF = ROWS // 2
MIB = 1024 * 1024
KEEP_LIMIT = 48
SEND_LIMIT = 56
BF16 = jnp.bfloat16
F32 = jnp.float32


def dot(a, b):
    return jnp.dot(a, b, preferred_element_type=F32)


def dot_t(a, b):
    return lax.dot_general(a, b, (((1,), (1,)), ((), ())), preferred_element_type=F32)


def one_hot(mask):
    return mask.astype(F32).astype(BF16)


def seats_of(limits_ref, picked, experts):
    tokens = picked.shape[1]
    flags = [jnp.max((picked == e).astype(F32), axis=0, keepdims=True) for e in experts]
    flags = jnp.concatenate(flags, axis=0)
    earlier = lax.broadcasted_iota(jnp.int32, (tokens, tokens), 0)
    later = lax.broadcasted_iota(jnp.int32, (tokens, tokens), 1)
    position = dot(flags.astype(BF16), one_hot(earlier < later)).astype(jnp.int32)
    rows = []
    for i, e in enumerate(experts):
        limit = jnp.minimum(limits_ref[e], LOCAL_SEATS)
        at = position[i : i + 1]
        rows.append(jnp.where((flags[i : i + 1] > 0.0) & (at < limit), at, -1))
    return rows


def send_kernel(hops, *refs):
    count = len(hops)
    in_refs, out_refs, scratch, sems = refs[:7], refs[7 : 7 + count], refs[7 + count : -1], refs[-1]
    limits_ref, picked_ref, shares_ref, owner_ref, tokens_ref, derivs_ref, compressor_ref = scratch
    tokens, width = tokens_ref.shape
    chunk = width // (PARTS + 1)
    columns = [slice(i * chunk, (i + 1) * chunk) for i in range(PARTS + 1)]
    copies = [
        pltpu.make_async_copy(a, b, sems.at[i]) for i, (a, b) in enumerate(zip(in_refs, scratch))
    ]
    for copy in copies[:4] + copies[5:] + copies[4:5]:
        copy.start()
    for copy in copies[:4]:
        copy.wait()
    me = lax.axis_index("exp")
    experts = [jnp.bitwise_xor(me, q) for q in hops]
    picked = picked_ref[...]
    seats = seats_of(limits_ref, picked, experts)
    slot = lax.broadcasted_iota(jnp.int32, (ROWS, tokens), 0)
    near = jnp.concatenate([one_hot(slot == s) for s in seats], axis=0)
    masks = []
    for i in range(PARTS):
        shifted = jnp.where(slot >= LOCAL_SEATS, slot - LOCAL_SEATS + SPARE * i, -2)
        far = jnp.concatenate([one_hot(shifted == s) for s in seats], axis=0)
        masks.append(jnp.concatenate([near, far], axis=1))
    owner = owner_ref[...] - lax.axis_index("dp") * EX_DEV
    owned = [
        jnp.concatenate([one_hot((slot == s) & (owner == n)) for n in range(EX_DEV)], axis=0)
        for s in seats
    ]
    share_rows = [
        jnp.sum(jnp.where(picked == e, shares_ref[...], 0.0), axis=0, keepdims=True)
        for e in experts
    ]
    pad = [jnp.zeros((-count % 8, tokens), F32)] if count % 8 else []
    shares = jnp.concatenate(share_rows + pad, axis=0).T
    for copy in copies[5:]:
        copy.wait()
    proj = dot_t(derivs_ref[...], compressor_ref[...])
    for q in range(count):
        grad = (shares[:, q : q + 1] * proj).astype(BF16)
        both = dot(owned[q], grad)
        halves = [both[n * ROWS : (n + 1) * ROWS] for n in range(EX_DEV)]
        out_refs[q][:, PARTS * chunk :] = jnp.concatenate(halves, axis=1).astype(BF16)
    copies[4].wait()
    last = tokens_ref[:, columns[-1]]
    for i in range(PARTS):
        source = jnp.concatenate([tokens_ref[:, columns[i]], last], axis=0)
        packed = dot(masks[i], source).astype(BF16)
        for q in range(count):
            out_refs[q][:, columns[i]] = packed[q * ROWS : (q + 1) * ROWS]


def keep_kernel(compressor_ref, gate_hbm, up_hbm, rows_hbm, *refs):
    gate_ref, up_ref, rows_ref, first_ref, second_ref, sems = refs
    pairs = ((gate_hbm, gate_ref), (up_hbm, up_ref), (rows_hbm, rows_ref))
    copies = [pltpu.make_async_copy(a, b, sems.at[i]) for i, (a, b) in enumerate(pairs)]
    for copy in copies:
        copy.start()
    chosen = chosen_compressors(compressor_ref, first_ref.shape[1])
    first_ref[...], second_ref[...] = chosen
    for copy in copies:
        copy.wait()


def chosen_compressors(compressor_ref, units):
    place = lax.axis_index("dp")
    rank, total = compressor_ref.shape
    to = lax.broadcasted_iota(jnp.int32, (rank, rank), 0)
    at = lax.broadcasted_iota(jnp.int32, (rank, rank), 1)
    order = one_hot(at == jnp.where(to < rank // 2, 2 * to, 2 * to - rank + 1))
    turned = dot(order, compressor_ref[...]).astype(BF16)
    line = lax.broadcasted_iota(jnp.int32, (total, units), 0)
    unit = lax.broadcasted_iota(jnp.int32, (total, units), 1)
    return [
        dot(turned, one_hot(line == unit + jnp.bitwise_xor(place, k) * units)).astype(BF16)
        for k in range(2)
    ]


def sketch_kernel(sizes, gate_ref, up_ref, pair_gate_ref, pair_up_ref, first_ref, second_ref, *refs):
    out_refs, grads_ref = refs[-1 - len(sizes) : -1], refs[-1]
    block_refs = refs[: -1 - len(sizes)]
    units, width = gate_ref.shape
    chunk = width // (PARTS + 1)
    size = sum(sizes)
    messages = size // ROWS
    low = lax.broadcasted_iota(jnp.int32, (1, HALF, 1), 1) < SPARE
    columns = [slice(i * chunk, (i + 1) * chunk) for i in range(PARTS + 1)]
    rows = [jnp.concatenate([r[:, c] for r in block_refs], axis=0) for c in columns[:PARTS]]
    tails = [r.astype(F32).reshape(messages, 2, HALF, chunk)[:, 1] for r in rows]

    def turn(a):
        return jnp.concatenate([a[:, SPARE:], a[:, :SPARE]], axis=1)

    top = jnp.where(low, turn(tails[0]), tails[1])
    bottom = jnp.where(low, turn(tails[2]), 0.0)
    rows.append(jnp.stack([top, bottom], axis=1).reshape(size, chunk).astype(BF16))
    seat = lax.broadcasted_iota(jnp.int32, (size, 1), 0) % ROWS

    def product(w):
        total = dot_t(rows[0], w[:, columns[0]])
        for c, r in zip(columns[1:], rows[1:]):
            total = total + dot_t(r, w[:, c])
        return total

    sketch = None
    for gate_w, up_w, compressor in (
        (gate_ref, up_ref, first_ref),
        (pair_gate_ref, pair_up_ref, second_ref),
    ):
        gate, up = product(gate_w), product(up_w)
        hidden = gate / (1.0 + jnp.exp(-gate)) * up
        hidden = jnp.where(seat < LOCAL_SEATS, hidden, 0.0).astype(BF16)
        term = dot_t(compressor[...], hidden)
        sketch = term if sketch is None else sketch + term
    at = 0
    for n, ref in zip(sizes, out_refs):
        ref[...] = sketch[:, at : at + n].astype(ref.dtype)
        at += n
    first = 0
    for r in block_refs:
        if first < sizes[0]:
            grads_ref[first : first + r.shape[0]] = r[:, PARTS * chunk :]
        first += r.shape[0]


def outer_kernel(grads_ref, *refs):
    partial_refs, out_ref = refs[:-1], refs[-1]
    total = partial_refs[0][...]
    for r in partial_refs[1:]:
        total = total + r[...].astype(F32)
    rank = total.shape[0]
    product = dot(total.astype(BF16), grads_ref[...])
    even, odd = product[: rank // 2], product[rank // 2 :]
    for n in range(EX_DEV):
        columns = slice(n * rank, (n + 1) * rank)
        out_ref[n] = jnp.concatenate([even[:, columns], odd[:, columns]], axis=1)


VMEM = pl.BlockSpec(memory_space=pltpu.VMEM)
SMEM = pl.BlockSpec(memory_space=pltpu.SMEM)
HBM = pl.BlockSpec(memory_space=pltpu.HBM)
ANY = pl.BlockSpec(memory_space=pl.ANY)


def call(kernel, out_shape, in_specs, limit, flops=0, moved=0, scratch=(), out_specs=None):
    return pl.pallas_call(
        kernel,
        out_shape=out_shape,
        in_specs=in_specs,
        out_specs=out_specs or jax.tree.map(lambda _: VMEM, out_shape),
        scratch_shapes=list(scratch),
        compiler_params=pltpu.CompilerParams(vmem_limit_bytes=limit),
        cost_estimate=pl.CostEstimate(flops=flops, bytes_accessed=moved, transcendentals=0),
    )


def swap(a, axis, q):
    n = lax.axis_size(axis)
    return lax.ppermute(a, axis, [(i, i ^ q) for i in range(n)])


def body(
    layer_inflows,
    output_derivatives,
    picked_specialists,
    dispatch_shares,
    item_sample,
    send_limits,
    gating_projection,
    raising_projection,
    inflow_compressor,
    outgrad_compressor,
):
    n_exp, n_dp = lax.axis_size("exp"), lax.axis_size("dp")
    small = n_exp <= 8
    tokens, width = layer_inflows.shape
    rank = outgrad_compressor.shape[1]
    packed = width * LOCAL_SEATS // ROWS
    units = gating_projection.shape[2]
    size = n_exp * ROWS
    shape = jax.ShapeDtypeStruct

    gate, up = gating_projection[0].T, raising_projection[0].T
    pair_gate, pair_up = swap(gate, "dp", 1), swap(up, "dp", 1)
    arguments = (
        send_limits,
        picked_specialists.T,
        dispatch_shares.T,
        item_sample.reshape(1, tokens),
        layer_inflows,
        output_derivatives,
        outgrad_compressor.T,
    )
    hops = [0, n_exp - 1] + list(range(1, n_exp - 1))
    spaces = [pltpu.SMEM] + [pltpu.VMEM] * (len(arguments) - 1)
    rows = call(
        functools.partial(send_kernel, hops),
        [shape((ROWS, packed + EX_DEV * rank), BF16)] * n_exp,
        [HBM] * len(arguments),
        SEND_LIMIT * MIB,
        flops=4 * size * tokens * packed + 2 * tokens * width * rank,
        moved=4 * tokens * width + 2 * rank * width,
        scratch=[space(a.shape, a.dtype) for space, a in zip(spaces, arguments)]
        + [pltpu.SemaphoreType.DMA((len(arguments),))],
    )(*arguments)

    half = n_dp // 2
    hold = lax.optimization_barrier
    rows = list(rows)
    crossed = [swap(rows[0], "dp", half)]
    chosen_shape = shape((rank, units), BF16)
    gate, up, rows[0], *chosen = call(
        keep_kernel,
        [shape(a.shape, BF16) for a in (gate, up, rows[0])] + [chosen_shape] * 2,
        [VMEM, ANY, ANY, ANY],
        KEEP_LIMIT * MIB,
        out_specs=[ANY, ANY, ANY, VMEM, VMEM],
        moved=8 * units * width,
        scratch=[pltpu.SemaphoreType.DMA((3,))],
    )(inflow_compressor.T, gate, up, rows[0])
    for i, q in enumerate(hops):
        if i:
            rows[i] = swap(rows[i], "exp", q)
            if i == n_exp - 1:
                pair_gate, crossed[0], rows[i] = hold((pair_gate, crossed[0], rows[i]))
            crossed.append(swap(rows[i], "dp", half))
    blocks = {0: rows, half: crossed}
    step = half // 2
    while step > 1:
        for d in list(blocks):
            blocks[d ^ step] = [swap(r, "dp", step) for r in blocks[d]]
        step //= 2

    partials, grads = [], None
    ends = sorted(blocks)
    for ds in [ends] if small else [[d] for d in ends]:
        parts = [r for d in ds for r in blocks[d]]
        *made, first = call(
            functools.partial(sketch_kernel, [size] * len(ds)),
            [shape((rank, size), BF16 if d else F32) for d in ds]
            + [shape((size, EX_DEV * rank), BF16)],
            [VMEM] * (6 + len(parts)),
            20 * MIB,
            flops=8 * len(ds) * size * width * units,
            moved=8 * width * units + 2 * len(ds) * size * packed,
        )(gate, up, pair_gate, pair_up, *chosen, *parts)
        grads = first if grads is None else grads
        partials += [swap(p, "dp", d) if d else p for d, p in zip(ds, made)]
    out = call(
        outer_kernel,
        shape((EX_DEV, rank * rank // 128, 128), F32),
        [VMEM] * (1 + len(partials)),
        8 * MIB,
        flops=2 * size * rank * 2 * rank,
        moved=4 * EX_DEV * rank * rank,
    )(grads, *partials)
    return out.reshape(EX_DEV, 1, rank * rank)


def solution(mesh):
    in_specs = (
        P(("grp", "exp", "dp"), None),
        P(("grp", "exp", "dp"), None),
        P(("grp", "exp", "dp"), None),
        P(("grp", "exp", "dp"), None),
        P(("grp", "exp", "dp")),
        P("grp"),
        P("exp", None, "dp"),
        P("exp", None, "dp"),
        P(),
        P(),
    )
    out_specs = P(("grp", "dp"), "exp", None)
    return jax.shard_map(body, mesh=mesh, in_specs=in_specs, out_specs=out_specs, check_vma=False)
```

```python
import functools

import jax
import jax.numpy as jnp
from jax import lax
from jax.experimental import pallas as pl
from jax.experimental.pallas import tpu as pltpu
from jax.sharding import PartitionSpec as P

EX_DEV = 2
LOCAL_SEATS = 12
ROWS = 16
SPARE = ROWS - LOCAL_SEATS
PARTS = LOCAL_SEATS // SPARE
HALF = ROWS // 2
MIB = 1024 * 1024
KEEP_LIMIT = 48
SEND_LIMIT = 56
BF16 = jnp.bfloat16
F32 = jnp.float32


def dot(a, b):
    return jnp.dot(a, b, preferred_element_type=F32)


def dot_t(a, b):
    return lax.dot_general(a, b, (((1,), (1,)), ((), ())), preferred_element_type=F32)


def one_hot(mask):
    return mask.astype(F32).astype(BF16)


def seats_of(limits_ref, picked, experts):
    tokens = picked.shape[1]
    flags = [jnp.max((picked == e).astype(F32), axis=0, keepdims=True) for e in experts]
    flags = jnp.concatenate(flags, axis=0)
    earlier = lax.broadcasted_iota(jnp.int32, (tokens, tokens), 0)
    later = lax.broadcasted_iota(jnp.int32, (tokens, tokens), 1)
    position = dot(flags.astype(BF16), one_hot(earlier < later)).astype(jnp.int32)
    rows = []
    for i, e in enumerate(experts):
        limit = jnp.minimum(limits_ref[e], LOCAL_SEATS)
        at = position[i : i + 1]
        rows.append(jnp.where((flags[i : i + 1] > 0.0) & (at < limit), at, -1))
    return rows


def send_kernel(hops, *refs):
    count = len(hops)
    in_refs, out_refs, scratch, sems = refs[:7], refs[7 : 7 + count], refs[7 + count : -1], refs[-1]
    limits_ref, picked_ref, shares_ref, owner_ref, tokens_ref, derivs_ref, compressor_ref = scratch
    tokens, width = tokens_ref.shape
    chunk = width // (PARTS + 1)
    columns = [slice(i * chunk, (i + 1) * chunk) for i in range(PARTS + 1)]
    copies = [
        pltpu.make_async_copy(a, b, sems.at[i]) for i, (a, b) in enumerate(zip(in_refs, scratch))
    ]
    for copy in copies:
        copy.start()
    for copy in copies[:4]:
        copy.wait()
    me = lax.axis_index("exp")
    experts = [jnp.bitwise_xor(me, q) for q in hops]
    picked = picked_ref[...]
    seats = seats_of(limits_ref, picked, experts)
    slot = lax.broadcasted_iota(jnp.int32, (ROWS, tokens), 0)
    near = jnp.concatenate([one_hot(slot == s) for s in seats], axis=0)
    masks = []
    for i in range(PARTS):
        shifted = jnp.where(slot >= LOCAL_SEATS, slot - LOCAL_SEATS + SPARE * i, -2)
        far = jnp.concatenate([one_hot(shifted == s) for s in seats], axis=0)
        masks.append(jnp.concatenate([near, far], axis=1))
    owner = owner_ref[...] - lax.axis_index("dp") * EX_DEV
    owned = [
        jnp.concatenate([one_hot((slot == s) & (owner == n)) for n in range(EX_DEV)], axis=0)
        for s in seats
    ]
    share_rows = [
        jnp.sum(jnp.where(picked == e, shares_ref[...], 0.0), axis=0, keepdims=True)
        for e in experts
    ]
    pad = [jnp.zeros((-count % 8, tokens), F32)] if count % 8 else []
    shares = jnp.concatenate(share_rows + pad, axis=0).T
    for copy in copies[4:]:
        copy.wait()
    proj = dot_t(derivs_ref[...], compressor_ref[...])
    last = tokens_ref[:, columns[-1]]
    for i in range(PARTS):
        source = jnp.concatenate([tokens_ref[:, columns[i]], last], axis=0)
        packed = dot(masks[i], source).astype(BF16)
        for q in range(count):
            out_refs[q][:, columns[i]] = packed[q * ROWS : (q + 1) * ROWS]
    for q in range(count):
        grad = (shares[:, q : q + 1] * proj).astype(BF16)
        both = dot(owned[q], grad)
        halves = [both[n * ROWS : (n + 1) * ROWS] for n in range(EX_DEV)]
        out_refs[q][:, PARTS * chunk :] = jnp.concatenate(halves, axis=1).astype(BF16)


def keep_kernel(compressor_ref, gate_hbm, up_hbm, rows_hbm, *refs):
    gate_ref, up_ref, rows_ref, first_ref, second_ref, sems = refs
    pairs = ((gate_hbm, gate_ref), (up_hbm, up_ref), (rows_hbm, rows_ref))
    copies = [pltpu.make_async_copy(a, b, sems.at[i]) for i, (a, b) in enumerate(pairs)]
    for copy in copies:
        copy.start()
    chosen = chosen_compressors(compressor_ref, first_ref.shape[1])
    first_ref[...], second_ref[...] = chosen
    for copy in copies:
        copy.wait()


def chosen_compressors(compressor_ref, units):
    place = lax.axis_index("dp")
    rank, total = compressor_ref.shape
    to = lax.broadcasted_iota(jnp.int32, (rank, rank), 0)
    at = lax.broadcasted_iota(jnp.int32, (rank, rank), 1)
    order = one_hot(at == jnp.where(to < rank // 2, 2 * to, 2 * to - rank + 1))
    turned = dot(order, compressor_ref[...]).astype(BF16)
    line = lax.broadcasted_iota(jnp.int32, (total, units), 0)
    unit = lax.broadcasted_iota(jnp.int32, (total, units), 1)
    return [
        dot(turned, one_hot(line == unit + jnp.bitwise_xor(place, k) * units)).astype(BF16)
        for k in range(2)
    ]


def sketch_kernel(sizes, gate_ref, up_ref, pair_gate_ref, pair_up_ref, first_ref, second_ref, *refs):
    out_refs, grads_ref = refs[-1 - len(sizes) : -1], refs[-1]
    block_refs = refs[: -1 - len(sizes)]
    units, width = gate_ref.shape
    chunk = width // (PARTS + 1)
    size = sum(sizes)
    messages = size // ROWS
    low = lax.broadcasted_iota(jnp.int32, (1, HALF, 1), 1) < SPARE
    columns = [slice(i * chunk, (i + 1) * chunk) for i in range(PARTS + 1)]
    rows = [jnp.concatenate([r[:, c] for r in block_refs], axis=0) for c in columns[:PARTS]]
    tails = [r.astype(F32).reshape(messages, 2, HALF, chunk)[:, 1] for r in rows]

    def turn(a):
        return jnp.concatenate([a[:, SPARE:], a[:, :SPARE]], axis=1)

    top = jnp.where(low, turn(tails[0]), tails[1])
    bottom = jnp.where(low, turn(tails[2]), 0.0)
    rows.append(jnp.stack([top, bottom], axis=1).reshape(size, chunk).astype(BF16))
    seat = lax.broadcasted_iota(jnp.int32, (size, 1), 0) % ROWS

    def product(w):
        total = dot_t(rows[0], w[:, columns[0]])
        for c, r in zip(columns[1:], rows[1:]):
            total = total + dot_t(r, w[:, c])
        return total

    sketch = None
    for gate_w, up_w, compressor in (
        (gate_ref, up_ref, first_ref),
        (pair_gate_ref, pair_up_ref, second_ref),
    ):
        gate, up = product(gate_w), product(up_w)
        hidden = gate / (1.0 + jnp.exp(-gate)) * up
        hidden = jnp.where(seat < LOCAL_SEATS, hidden, 0.0).astype(BF16)
        term = dot_t(compressor[...], hidden)
        sketch = term if sketch is None else sketch + term
    at = 0
    for n, ref in zip(sizes, out_refs):
        ref[...] = sketch[:, at : at + n].astype(ref.dtype)
        at += n
    first = 0
    for r in block_refs:
        if first < sizes[0]:
            grads_ref[first : first + r.shape[0]] = r[:, PARTS * chunk :]
        first += r.shape[0]


def outer_kernel(grads_ref, *refs):
    partial_refs, out_ref = refs[:-1], refs[-1]
    total = partial_refs[0][...]
    for r in partial_refs[1:]:
        total = total + r[...].astype(F32)
    rank = total.shape[0]
    product = dot(total.astype(BF16), grads_ref[...])
    even, odd = product[: rank // 2], product[rank // 2 :]
    for n in range(EX_DEV):
        columns = slice(n * rank, (n + 1) * rank)
        out_ref[n] = jnp.concatenate([even[:, columns], odd[:, columns]], axis=1)


VMEM = pl.BlockSpec(memory_space=pltpu.VMEM)
SMEM = pl.BlockSpec(memory_space=pltpu.SMEM)
HBM = pl.BlockSpec(memory_space=pltpu.HBM)
ANY = pl.BlockSpec(memory_space=pl.ANY)


def call(kernel, out_shape, in_specs, limit, flops=0, moved=0, scratch=(), out_specs=None):
    return pl.pallas_call(
        kernel,
        out_shape=out_shape,
        in_specs=in_specs,
        out_specs=out_specs or jax.tree.map(lambda _: VMEM, out_shape),
        scratch_shapes=list(scratch),
        compiler_params=pltpu.CompilerParams(vmem_limit_bytes=limit),
        cost_estimate=pl.CostEstimate(flops=flops, bytes_accessed=moved, transcendentals=0),
    )


def swap(a, axis, q):
    n = lax.axis_size(axis)
    return lax.ppermute(a, axis, [(i, i ^ q) for i in range(n)])


def body(
    layer_inflows,
    output_derivatives,
    picked_specialists,
    dispatch_shares,
    item_sample,
    send_limits,
    gating_projection,
    raising_projection,
    inflow_compressor,
    outgrad_compressor,
):
    n_exp, n_dp = lax.axis_size("exp"), lax.axis_size("dp")
    small = n_exp <= 8
    tokens, width = layer_inflows.shape
    rank = outgrad_compressor.shape[1]
    packed = width * LOCAL_SEATS // ROWS
    units = gating_projection.shape[2]
    size = n_exp * ROWS
    shape = jax.ShapeDtypeStruct

    gate, up = gating_projection[0].T, raising_projection[0].T
    pair_gate, pair_up = swap(gate, "dp", 1), swap(up, "dp", 1)
    arguments = (
        send_limits,
        picked_specialists.T,
        dispatch_shares.T,
        item_sample.reshape(1, tokens),
        layer_inflows,
        output_derivatives,
        outgrad_compressor.T,
    )
    hops = [0] + list(range(n_exp - 1, 0, -1))
    spaces = [pltpu.SMEM] + [pltpu.VMEM] * (len(arguments) - 1)
    rows = call(
        functools.partial(send_kernel, hops),
        [shape((ROWS, packed + EX_DEV * rank), BF16)] * n_exp,
        [HBM] * len(arguments),
        SEND_LIMIT * MIB,
        flops=4 * size * tokens * packed + 2 * tokens * width * rank,
        moved=4 * tokens * width + 2 * rank * width,
        scratch=[space(a.shape, a.dtype) for space, a in zip(spaces, arguments)]
        + [pltpu.SemaphoreType.DMA((len(arguments),))],
    )(*arguments)

    half = n_dp // 2
    hold = lax.optimization_barrier
    rows = list(rows)
    crossed = [swap(rows[0], "dp", half)]
    chosen_shape = shape((rank, units), BF16)
    gate, up, rows[0], *chosen = call(
        keep_kernel,
        [shape(a.shape, BF16) for a in (gate, up, rows[0])] + [chosen_shape] * 2,
        [VMEM, ANY, ANY, ANY],
        KEEP_LIMIT * MIB,
        out_specs=[ANY, ANY, ANY, VMEM, VMEM],
        moved=8 * units * width,
        scratch=[pltpu.SemaphoreType.DMA((3,))],
    )(inflow_compressor.T, gate, up, rows[0])
    for i, q in enumerate(hops):
        if i:
            rows[i] = swap(rows[i], "exp", q)
            if i == n_exp - 1:
                pair_gate, crossed[0], rows[i] = hold((pair_gate, crossed[0], rows[i]))
            crossed.append(swap(rows[i], "dp", half))
    blocks = {0: rows, half: crossed}
    step = half // 2
    while step > 1:
        for d in list(blocks):
            blocks[d ^ step] = [swap(r, "dp", step) for r in blocks[d]]
        step //= 2

    partials, grads = [], None
    ends = sorted(blocks)
    for ds in [ends] if small else [[d] for d in ends]:
        parts = [r for d in ds for r in blocks[d]]
        *made, first = call(
            functools.partial(sketch_kernel, [size] * len(ds)),
            [shape((rank, size), BF16 if d else F32) for d in ds]
            + [shape((size, EX_DEV * rank), BF16)],
            [VMEM] * (6 + len(parts)),
            20 * MIB,
            flops=8 * len(ds) * size * width * units,
            moved=8 * width * units + 2 * len(ds) * size * packed,
        )(gate, up, pair_gate, pair_up, *chosen, *parts)
        grads = first if grads is None else grads
        partials += [swap(p, "dp", d) if d else p for d, p in zip(ds, made)]
    out = call(
        outer_kernel,
        shape((EX_DEV, rank * rank // 128, 128), F32),
        [VMEM] * (1 + len(partials)),
        8 * MIB,
        flops=2 * size * rank * 2 * rank,
        moved=4 * EX_DEV * rank * rank,
    )(grads, *partials)
    return out.reshape(EX_DEV, 1, rank * rank)


def solution(mesh):
    in_specs = (
        P(("grp", "exp", "dp"), None),
        P(("grp", "exp", "dp"), None),
        P(("grp", "exp", "dp"), None),
        P(("grp", "exp", "dp"), None),
        P(("grp", "exp", "dp")),
        P("grp"),
        P("exp", None, "dp"),
        P("exp", None, "dp"),
        P(),
        P(),
    )
    out_specs = P(("grp", "dp"), "exp", None)
    return jax.shard_map(body, mesh=mesh, in_specs=in_specs, out_specs=out_specs, check_vma=False)
```

```python
import functools

import jax
import jax.numpy as jnp
from jax import lax
from jax.experimental import pallas as pl
from jax.experimental.pallas import tpu as pltpu
from jax.sharding import PartitionSpec as P

EX_DEV = 2
LOCAL_SEATS = 12
ROWS = 16
SPARE = ROWS - LOCAL_SEATS
PARTS = LOCAL_SEATS // SPARE
HALF = ROWS // 2
MIB = 1024 * 1024
KEEP_LIMIT = 48
SEND_LIMIT = 56
BF16 = jnp.bfloat16
F32 = jnp.float32


def dot(a, b):
    return jnp.dot(a, b, preferred_element_type=F32)


def dot_t(a, b):
    return lax.dot_general(a, b, (((1,), (1,)), ((), ())), preferred_element_type=F32)


def one_hot(mask):
    return mask.astype(F32).astype(BF16)


def seats_of(limits_ref, picked, experts):
    tokens = picked.shape[1]
    flags = [jnp.max((picked == e).astype(F32), axis=0, keepdims=True) for e in experts]
    flags = jnp.concatenate(flags, axis=0)
    earlier = lax.broadcasted_iota(jnp.int32, (tokens, tokens), 0)
    later = lax.broadcasted_iota(jnp.int32, (tokens, tokens), 1)
    position = dot(flags.astype(BF16), one_hot(earlier < later)).astype(jnp.int32)
    rows = []
    for i, e in enumerate(experts):
        limit = jnp.minimum(limits_ref[e], LOCAL_SEATS)
        at = position[i : i + 1]
        rows.append(jnp.where((flags[i : i + 1] > 0.0) & (at < limit), at, -1))
    return rows


def send_kernel(hops, *refs):
    count = len(hops)
    in_refs, out_refs, scratch, sems = refs[:7], refs[7 : 7 + count], refs[7 + count : -1], refs[-1]
    limits_ref, picked_ref, shares_ref, owner_ref, tokens_ref, derivs_ref, compressor_ref = scratch
    tokens, width = tokens_ref.shape
    chunk = width // (PARTS + 1)
    columns = [slice(i * chunk, (i + 1) * chunk) for i in range(PARTS + 1)]
    copies = [
        pltpu.make_async_copy(a, b, sems.at[i]) for i, (a, b) in enumerate(zip(in_refs, scratch))
    ]
    for copy in copies:
        copy.start()
    for copy in copies[:4]:
        copy.wait()
    me = lax.axis_index("exp")
    experts = [jnp.bitwise_xor(me, q) for q in hops]
    picked = picked_ref[...]
    seats = seats_of(limits_ref, picked, experts)
    slot = lax.broadcasted_iota(jnp.int32, (ROWS, tokens), 0)
    near = jnp.concatenate([one_hot(slot == s) for s in seats], axis=0)
    masks = []
    for i in range(PARTS):
        shifted = jnp.where(slot >= LOCAL_SEATS, slot - LOCAL_SEATS + SPARE * i, -2)
        far = jnp.concatenate([one_hot(shifted == s) for s in seats], axis=0)
        masks.append(jnp.concatenate([near, far], axis=1))
    owner = owner_ref[...] - lax.axis_index("dp") * EX_DEV
    owned = [
        jnp.concatenate([one_hot((slot == s) & (owner == n)) for n in range(EX_DEV)], axis=0)
        for s in seats
    ]
    share_rows = [
        jnp.sum(jnp.where(picked == e, shares_ref[...], 0.0), axis=0, keepdims=True)
        for e in experts
    ]
    pad = [jnp.zeros((-count % 8, tokens), F32)] if count % 8 else []
    shares = jnp.concatenate(share_rows + pad, axis=0).T
    for copy in copies[4:]:
        copy.wait()
    proj = dot_t(derivs_ref[...], compressor_ref[...])
    last = tokens_ref[:, columns[-1]]
    for i in range(PARTS):
        source = jnp.concatenate([tokens_ref[:, columns[i]], last], axis=0)
        packed = dot(masks[i], source).astype(BF16)
        for q in range(count):
            out_refs[q][:, columns[i]] = packed[q * ROWS : (q + 1) * ROWS]
    for q in range(count):
        grad = (shares[:, q : q + 1] * proj).astype(BF16)
        both = dot(owned[q], grad)
        halves = [both[n * ROWS : (n + 1) * ROWS] for n in range(EX_DEV)]
        out_refs[q][:, PARTS * chunk :] = jnp.concatenate(halves, axis=1).astype(BF16)


def keep_kernel(compressor_ref, gate_hbm, up_hbm, rows_hbm, *refs):
    gate_ref, up_ref, rows_ref, first_ref, second_ref, sems = refs
    pairs = ((gate_hbm, gate_ref), (up_hbm, up_ref), (rows_hbm, rows_ref))
    copies = [pltpu.make_async_copy(a, b, sems.at[i]) for i, (a, b) in enumerate(pairs)]
    for copy in copies:
        copy.start()
    chosen = chosen_compressors(compressor_ref, first_ref.shape[1])
    first_ref[...], second_ref[...] = chosen
    for copy in copies:
        copy.wait()


def chosen_compressors(compressor_ref, units):
    place = lax.axis_index("dp")
    rank, total = compressor_ref.shape
    to = lax.broadcasted_iota(jnp.int32, (rank, rank), 0)
    at = lax.broadcasted_iota(jnp.int32, (rank, rank), 1)
    order = one_hot(at == jnp.where(to < rank // 2, 2 * to, 2 * to - rank + 1))
    turned = dot(order, compressor_ref[...]).astype(BF16)
    line = lax.broadcasted_iota(jnp.int32, (total, units), 0)
    unit = lax.broadcasted_iota(jnp.int32, (total, units), 1)
    return [
        dot(turned, one_hot(line == unit + jnp.bitwise_xor(place, k) * units)).astype(BF16)
        for k in range(2)
    ]


def sketch_kernel(sizes, gate_ref, up_ref, pair_gate_ref, pair_up_ref, first_ref, second_ref, *refs):
    out_refs, grads_ref = refs[-1 - len(sizes) : -1], refs[-1]
    block_refs = refs[: -1 - len(sizes)]
    units, width = gate_ref.shape
    chunk = width // (PARTS + 1)
    size = sum(sizes)
    messages = size // ROWS
    low = lax.broadcasted_iota(jnp.int32, (1, HALF, 1), 1) < SPARE
    columns = [slice(i * chunk, (i + 1) * chunk) for i in range(PARTS + 1)]
    rows = [jnp.concatenate([r[:, c] for r in block_refs], axis=0) for c in columns[:PARTS]]
    tails = [r.astype(F32).reshape(messages, 2, HALF, chunk)[:, 1] for r in rows]

    def turn(a):
        return jnp.concatenate([a[:, SPARE:], a[:, :SPARE]], axis=1)

    top = jnp.where(low, turn(tails[0]), tails[1])
    bottom = jnp.where(low, turn(tails[2]), 0.0)
    rows.append(jnp.stack([top, bottom], axis=1).reshape(size, chunk).astype(BF16))
    seat = lax.broadcasted_iota(jnp.int32, (size, 1), 0) % ROWS

    def product(w):
        total = dot_t(rows[0], w[:, columns[0]])
        for c, r in zip(columns[1:], rows[1:]):
            total = total + dot_t(r, w[:, c])
        return total

    sketch = None
    for gate_w, up_w, compressor in (
        (gate_ref, up_ref, first_ref),
        (pair_gate_ref, pair_up_ref, second_ref),
    ):
        gate, up = product(gate_w), product(up_w)
        hidden = gate / (1.0 + jnp.exp(-gate)) * up
        hidden = jnp.where(seat < LOCAL_SEATS, hidden, 0.0).astype(BF16)
        term = dot_t(compressor[...], hidden)
        sketch = term if sketch is None else sketch + term
    at = 0
    for n, ref in zip(sizes, out_refs):
        ref[...] = sketch[:, at : at + n].astype(ref.dtype)
        at += n
    first = 0
    for r in block_refs:
        if first < sizes[0]:
            grads_ref[first : first + r.shape[0]] = r[:, PARTS * chunk :]
        first += r.shape[0]


def outer_kernel(grads_ref, *refs):
    partial_refs, out_ref = refs[:-1], refs[-1]
    total = partial_refs[0][...]
    for r in partial_refs[1:]:
        total = total + r[...].astype(F32)
    rank = total.shape[0]
    product = dot(total.astype(BF16), grads_ref[...])
    even, odd = product[: rank // 2], product[rank // 2 :]
    for n in range(EX_DEV):
        columns = slice(n * rank, (n + 1) * rank)
        out_ref[n] = jnp.concatenate([even[:, columns], odd[:, columns]], axis=1)


VMEM = pl.BlockSpec(memory_space=pltpu.VMEM)
SMEM = pl.BlockSpec(memory_space=pltpu.SMEM)
HBM = pl.BlockSpec(memory_space=pltpu.HBM)
ANY = pl.BlockSpec(memory_space=pl.ANY)


def call(kernel, out_shape, in_specs, limit, flops=0, moved=0, scratch=(), out_specs=None):
    return pl.pallas_call(
        kernel,
        out_shape=out_shape,
        in_specs=in_specs,
        out_specs=out_specs or jax.tree.map(lambda _: VMEM, out_shape),
        scratch_shapes=list(scratch),
        compiler_params=pltpu.CompilerParams(vmem_limit_bytes=limit),
        cost_estimate=pl.CostEstimate(flops=flops, bytes_accessed=moved, transcendentals=0),
    )


def swap(a, axis, q):
    n = lax.axis_size(axis)
    return lax.ppermute(a, axis, [(i, i ^ q) for i in range(n)])


def body(
    layer_inflows,
    output_derivatives,
    picked_specialists,
    dispatch_shares,
    item_sample,
    send_limits,
    gating_projection,
    raising_projection,
    inflow_compressor,
    outgrad_compressor,
):
    n_exp, n_dp = lax.axis_size("exp"), lax.axis_size("dp")
    small = n_exp <= 8
    tokens, width = layer_inflows.shape
    rank = outgrad_compressor.shape[1]
    packed = width * LOCAL_SEATS // ROWS
    units = gating_projection.shape[2]
    size = n_exp * ROWS
    shape = jax.ShapeDtypeStruct

    gate, up = gating_projection[0].T, raising_projection[0].T
    pair_gate, pair_up = swap(gate, "dp", 1), swap(up, "dp", 1)
    arguments = (
        send_limits,
        picked_specialists.T,
        dispatch_shares.T,
        item_sample.reshape(1, tokens),
        layer_inflows,
        output_derivatives,
        outgrad_compressor.T,
    )
    hops = [0] + list(range(n_exp - 2, 0, -1)) + [n_exp - 1]
    spaces = [pltpu.SMEM] + [pltpu.VMEM] * (len(arguments) - 1)
    rows = call(
        functools.partial(send_kernel, hops),
        [shape((ROWS, packed + EX_DEV * rank), BF16)] * n_exp,
        [HBM] * len(arguments),
        SEND_LIMIT * MIB,
        flops=4 * size * tokens * packed + 2 * tokens * width * rank,
        moved=4 * tokens * width + 2 * rank * width,
        scratch=[space(a.shape, a.dtype) for space, a in zip(spaces, arguments)]
        + [pltpu.SemaphoreType.DMA((len(arguments),))],
    )(*arguments)

    half = n_dp // 2
    hold = lax.optimization_barrier
    rows = list(rows)
    crossed = [swap(rows[0], "dp", half)]
    chosen_shape = shape((rank, units), BF16)
    gate, up, rows[0], *chosen = call(
        keep_kernel,
        [shape(a.shape, BF16) for a in (gate, up, rows[0])] + [chosen_shape] * 2,
        [VMEM, ANY, ANY, ANY],
        KEEP_LIMIT * MIB,
        out_specs=[ANY, ANY, ANY, VMEM, VMEM],
        moved=8 * units * width,
        scratch=[pltpu.SemaphoreType.DMA((3,))],
    )(inflow_compressor.T, gate, up, rows[0])
    for i, q in enumerate(hops):
        if i:
            rows[i] = swap(rows[i], "exp", q)
            if i == n_exp - 1:
                pair_gate, crossed[0], rows[i] = hold((pair_gate, crossed[0], rows[i]))
            crossed.append(swap(rows[i], "dp", half))
    blocks = {0: rows, half: crossed}
    step = half // 2
    while step > 1:
        for d in list(blocks):
            blocks[d ^ step] = [swap(r, "dp", step) for r in blocks[d]]
        step //= 2

    partials, grads = [], None
    ends = sorted(blocks)
    for ds in [ends] if small else [[d] for d in ends]:
        parts = [r for d in ds for r in blocks[d]]
        *made, first = call(
            functools.partial(sketch_kernel, [size] * len(ds)),
            [shape((rank, size), BF16 if d else F32) for d in ds]
            + [shape((size, EX_DEV * rank), BF16)],
            [VMEM] * (6 + len(parts)),
            20 * MIB,
            flops=8 * len(ds) * size * width * units,
            moved=8 * width * units + 2 * len(ds) * size * packed,
        )(gate, up, pair_gate, pair_up, *chosen, *parts)
        grads = first if grads is None else grads
        partials += [swap(p, "dp", d) if d else p for d, p in zip(ds, made)]
    out = call(
        outer_kernel,
        shape((EX_DEV, rank * rank // 128, 128), F32),
        [VMEM] * (1 + len(partials)),
        8 * MIB,
        flops=2 * size * rank * 2 * rank,
        moved=4 * EX_DEV * rank * rank,
    )(grads, *partials)
    return out.reshape(EX_DEV, 1, rank * rank)


def solution(mesh):
    in_specs = (
        P(("grp", "exp", "dp"), None),
        P(("grp", "exp", "dp"), None),
        P(("grp", "exp", "dp"), None),
        P(("grp", "exp", "dp"), None),
        P(("grp", "exp", "dp")),
        P("grp"),
        P("exp", None, "dp"),
        P("exp", None, "dp"),
        P(),
        P(),
    )
    out_specs = P(("grp", "dp"), "exp", None)
    return jax.shard_map(body, mesh=mesh, in_specs=in_specs, out_specs=out_specs, check_vma=False)
```

```python
import functools

import jax
import jax.numpy as jnp
from jax import lax
from jax.experimental import pallas as pl
from jax.experimental.pallas import tpu as pltpu
from jax.sharding import PartitionSpec as P

EX_DEV = 2
LOCAL_SEATS = 12
ROWS = 16
SPARE = ROWS - LOCAL_SEATS
PARTS = LOCAL_SEATS // SPARE
HALF = ROWS // 2
MIB = 1024 * 1024
KEEP_LIMIT = 48
TOKEN_PIECES = 4
SEND_LIMIT = 56
BF16 = jnp.bfloat16
F32 = jnp.float32


def dot(a, b):
    return jnp.dot(a, b, preferred_element_type=F32)


def dot_t(a, b):
    return lax.dot_general(a, b, (((1,), (1,)), ((), ())), preferred_element_type=F32)


def one_hot(mask):
    return mask.astype(F32).astype(BF16)


def seats_of(limits_ref, picked, experts):
    tokens = picked.shape[1]
    flags = [jnp.max((picked == e).astype(F32), axis=0, keepdims=True) for e in experts]
    flags = jnp.concatenate(flags, axis=0)
    earlier = lax.broadcasted_iota(jnp.int32, (tokens, tokens), 0)
    later = lax.broadcasted_iota(jnp.int32, (tokens, tokens), 1)
    position = dot(flags.astype(BF16), one_hot(earlier < later)).astype(jnp.int32)
    rows = []
    for i, e in enumerate(experts):
        limit = jnp.minimum(limits_ref[e], LOCAL_SEATS)
        at = position[i : i + 1]
        rows.append(jnp.where((flags[i : i + 1] > 0.0) & (at < limit), at, -1))
    return rows


def send_kernel(hops, *refs):
    count = len(hops)
    in_refs, out_refs, scratch, sems = refs[:7], refs[7 : 7 + count], refs[7 + count : -1], refs[-1]
    limits_ref, picked_ref, shares_ref, owner_ref, tokens_ref, derivs_ref, compressor_ref = scratch
    tokens, width = tokens_ref.shape
    chunk = width // (PARTS + 1)
    columns = [slice(i * chunk, (i + 1) * chunk) for i in range(PARTS + 1)]
    pairs = list(zip(in_refs, scratch))
    piece = tokens // TOKEN_PIECES
    pairs = pairs[:4] + pairs[6:] + [
        (a.at[pl.ds(i * piece, piece)], b.at[pl.ds(i * piece, piece)])
        for i in range(TOKEN_PIECES)
        for a, b in pairs[4:6]
    ]
    copies = [pltpu.make_async_copy(a, b, sems.at[i]) for i, (a, b) in enumerate(pairs)]
    for copy in copies:
        copy.start()
    for copy in copies[:4]:
        copy.wait()
    me = lax.axis_index("exp")
    experts = [jnp.bitwise_xor(me, q) for q in hops]
    picked = picked_ref[...]
    seats = seats_of(limits_ref, picked, experts)
    slot = lax.broadcasted_iota(jnp.int32, (ROWS, tokens), 0)
    near = jnp.concatenate([one_hot(slot == s) for s in seats], axis=0)
    masks = []
    for i in range(PARTS):
        shifted = jnp.where(slot >= LOCAL_SEATS, slot - LOCAL_SEATS + SPARE * i, -2)
        far = jnp.concatenate([one_hot(shifted == s) for s in seats], axis=0)
        masks.append(jnp.concatenate([near, far], axis=1))
    owner = owner_ref[...] - lax.axis_index("dp") * EX_DEV
    owned = [
        jnp.concatenate([one_hot((slot == s) & (owner == n)) for n in range(EX_DEV)], axis=0)
        for s in seats
    ]
    share_rows = [
        jnp.sum(jnp.where(picked == e, shares_ref[...], 0.0), axis=0, keepdims=True)
        for e in experts
    ]
    pad = [jnp.zeros((-count % 8, tokens), F32)] if count % 8 else []
    shares = jnp.concatenate(share_rows + pad, axis=0).T
    for copy in copies[4:]:
        copy.wait()
    proj = dot_t(derivs_ref[...], compressor_ref[...])
    last = tokens_ref[:, columns[-1]]
    for i in range(PARTS):
        source = jnp.concatenate([tokens_ref[:, columns[i]], last], axis=0)
        packed = dot(masks[i], source).astype(BF16)
        for q in range(count):
            out_refs[q][:, columns[i]] = packed[q * ROWS : (q + 1) * ROWS]
    for q in range(count):
        grad = (shares[:, q : q + 1] * proj).astype(BF16)
        both = dot(owned[q], grad)
        halves = [both[n * ROWS : (n + 1) * ROWS] for n in range(EX_DEV)]
        out_refs[q][:, PARTS * chunk :] = jnp.concatenate(halves, axis=1).astype(BF16)


def keep_kernel(compressor_ref, gate_hbm, up_hbm, rows_hbm, *refs):
    gate_ref, up_ref, rows_ref, first_ref, second_ref, sems = refs
    pairs = ((gate_hbm, gate_ref), (up_hbm, up_ref), (rows_hbm, rows_ref))
    copies = [pltpu.make_async_copy(a, b, sems.at[i]) for i, (a, b) in enumerate(pairs)]
    for copy in copies:
        copy.start()
    chosen = chosen_compressors(compressor_ref, first_ref.shape[1])
    first_ref[...], second_ref[...] = chosen
    for copy in copies:
        copy.wait()


def chosen_compressors(compressor_ref, units):
    place = lax.axis_index("dp")
    rank, total = compressor_ref.shape
    to = lax.broadcasted_iota(jnp.int32, (rank, rank), 0)
    at = lax.broadcasted_iota(jnp.int32, (rank, rank), 1)
    order = one_hot(at == jnp.where(to < rank // 2, 2 * to, 2 * to - rank + 1))
    turned = dot(order, compressor_ref[...]).astype(BF16)
    line = lax.broadcasted_iota(jnp.int32, (total, units), 0)
    unit = lax.broadcasted_iota(jnp.int32, (total, units), 1)
    return [
        dot(turned, one_hot(line == unit + jnp.bitwise_xor(place, k) * units)).astype(BF16)
        for k in range(2)
    ]


def sketch_kernel(sizes, gate_ref, up_ref, pair_gate_ref, pair_up_ref, first_ref, second_ref, *refs):
    out_refs, grads_ref = refs[-1 - len(sizes) : -1], refs[-1]
    block_refs = refs[: -1 - len(sizes)]
    units, width = gate_ref.shape
    chunk = width // (PARTS + 1)
    size = sum(sizes)
    messages = size // ROWS
    low = lax.broadcasted_iota(jnp.int32, (1, HALF, 1), 1) < SPARE
    columns = [slice(i * chunk, (i + 1) * chunk) for i in range(PARTS + 1)]
    rows = [jnp.concatenate([r[:, c] for r in block_refs], axis=0) for c in columns[:PARTS]]
    tails = [r.astype(F32).reshape(messages, 2, HALF, chunk)[:, 1] for r in rows]

    def turn(a):
        return jnp.concatenate([a[:, SPARE:], a[:, :SPARE]], axis=1)

    top = jnp.where(low, turn(tails[0]), tails[1])
    bottom = jnp.where(low, turn(tails[2]), 0.0)
    rows.append(jnp.stack([top, bottom], axis=1).reshape(size, chunk).astype(BF16))
    seat = lax.broadcasted_iota(jnp.int32, (size, 1), 0) % ROWS

    def product(w):
        total = dot_t(rows[0], w[:, columns[0]])
        for c, r in zip(columns[1:], rows[1:]):
            total = total + dot_t(r, w[:, c])
        return total

    sketch = None
    for gate_w, up_w, compressor in (
        (gate_ref, up_ref, first_ref),
        (pair_gate_ref, pair_up_ref, second_ref),
    ):
        gate, up = product(gate_w), product(up_w)
        hidden = gate / (1.0 + jnp.exp(-gate)) * up
        hidden = jnp.where(seat < LOCAL_SEATS, hidden, 0.0).astype(BF16)
        term = dot_t(compressor[...], hidden)
        sketch = term if sketch is None else sketch + term
    at = 0
    for n, ref in zip(sizes, out_refs):
        ref[...] = sketch[:, at : at + n].astype(ref.dtype)
        at += n
    first = 0
    for r in block_refs:
        if first < sizes[0]:
            grads_ref[first : first + r.shape[0]] = r[:, PARTS * chunk :]
        first += r.shape[0]


def outer_kernel(grads_ref, *refs):
    partial_refs, out_ref = refs[:-1], refs[-1]
    total = partial_refs[0][...]
    for r in partial_refs[1:]:
        total = total + r[...].astype(F32)
    rank = total.shape[0]
    product = dot(total.astype(BF16), grads_ref[...])
    even, odd = product[: rank // 2], product[rank // 2 :]
    for n in range(EX_DEV):
        columns = slice(n * rank, (n + 1) * rank)
        out_ref[n] = jnp.concatenate([even[:, columns], odd[:, columns]], axis=1)


VMEM = pl.BlockSpec(memory_space=pltpu.VMEM)
SMEM = pl.BlockSpec(memory_space=pltpu.SMEM)
HBM = pl.BlockSpec(memory_space=pltpu.HBM)
ANY = pl.BlockSpec(memory_space=pl.ANY)


def call(kernel, out_shape, in_specs, limit, flops=0, moved=0, scratch=(), out_specs=None):
    return pl.pallas_call(
        kernel,
        out_shape=out_shape,
        in_specs=in_specs,
        out_specs=out_specs or jax.tree.map(lambda _: VMEM, out_shape),
        scratch_shapes=list(scratch),
        compiler_params=pltpu.CompilerParams(vmem_limit_bytes=limit),
        cost_estimate=pl.CostEstimate(flops=flops, bytes_accessed=moved, transcendentals=0),
    )


def swap(a, axis, q):
    n = lax.axis_size(axis)
    return lax.ppermute(a, axis, [(i, i ^ q) for i in range(n)])


def body(
    layer_inflows,
    output_derivatives,
    picked_specialists,
    dispatch_shares,
    item_sample,
    send_limits,
    gating_projection,
    raising_projection,
    inflow_compressor,
    outgrad_compressor,
):
    n_exp, n_dp = lax.axis_size("exp"), lax.axis_size("dp")
    small = n_exp <= 8
    tokens, width = layer_inflows.shape
    rank = outgrad_compressor.shape[1]
    packed = width * LOCAL_SEATS // ROWS
    units = gating_projection.shape[2]
    size = n_exp * ROWS
    shape = jax.ShapeDtypeStruct

    gate, up = gating_projection[0].T, raising_projection[0].T
    pair_gate, pair_up = swap(gate, "dp", 1), swap(up, "dp", 1)
    arguments = (
        send_limits,
        picked_specialists.T,
        dispatch_shares.T,
        item_sample.reshape(1, tokens),
        layer_inflows,
        output_derivatives,
        outgrad_compressor.T,
    )
    hops = [0, n_exp - 1] + list(range(1, n_exp - 1))
    spaces = [pltpu.SMEM] + [pltpu.VMEM] * (len(arguments) - 1)
    rows = call(
        functools.partial(send_kernel, hops),
        [shape((ROWS, packed + EX_DEV * rank), BF16)] * n_exp,
        [HBM] * len(arguments),
        SEND_LIMIT * MIB,
        flops=4 * size * tokens * packed + 2 * tokens * width * rank,
        moved=4 * tokens * width + 2 * rank * width,
        scratch=[space(a.shape, a.dtype) for space, a in zip(spaces, arguments)]
        + [pltpu.SemaphoreType.DMA((len(arguments) - 2 + 2 * TOKEN_PIECES,))],
    )(*arguments)

    half = n_dp // 2
    hold = lax.optimization_barrier
    rows = list(rows)
    crossed = [swap(rows[0], "dp", half)]
    chosen_shape = shape((rank, units), BF16)
    gate, up, rows[0], *chosen = call(
        keep_kernel,
        [shape(a.shape, BF16) for a in (gate, up, rows[0])] + [chosen_shape] * 2,
        [VMEM, ANY, ANY, ANY],
        KEEP_LIMIT * MIB,
        out_specs=[ANY, ANY, ANY, VMEM, VMEM],
        moved=8 * units * width,
        scratch=[pltpu.SemaphoreType.DMA((3,))],
    )(inflow_compressor.T, gate, up, rows[0])
    for i, q in enumerate(hops):
        if i:
            rows[i] = swap(rows[i], "exp", q)
            if i == n_exp - 1:
                pair_gate, crossed[0], rows[i] = hold((pair_gate, crossed[0], rows[i]))
            crossed.append(swap(rows[i], "dp", half))
    blocks = {0: rows, half: crossed}
    step = half // 2
    while step > 1:
        for d in list(blocks):
            blocks[d ^ step] = [swap(r, "dp", step) for r in blocks[d]]
        step //= 2

    partials, grads = [], None
    ends = sorted(blocks)
    for ds in [ends] if small else [[d] for d in ends]:
        parts = [r for d in ds for r in blocks[d]]
        *made, first = call(
            functools.partial(sketch_kernel, [size] * len(ds)),
            [shape((rank, size), BF16 if d else F32) for d in ds]
            + [shape((size, EX_DEV * rank), BF16)],
            [VMEM] * (6 + len(parts)),
            20 * MIB,
            flops=8 * len(ds) * size * width * units,
            moved=8 * width * units + 2 * len(ds) * size * packed,
        )(gate, up, pair_gate, pair_up, *chosen, *parts)
        grads = first if grads is None else grads
        partials += [swap(p, "dp", d) if d else p for d, p in zip(ds, made)]
    out = call(
        outer_kernel,
        shape((EX_DEV, rank * rank // 128, 128), F32),
        [VMEM] * (1 + len(partials)),
        8 * MIB,
        flops=2 * size * rank * 2 * rank,
        moved=4 * EX_DEV * rank * rank,
    )(grads, *partials)
    return out.reshape(EX_DEV, 1, rank * rank)


def solution(mesh):
    in_specs = (
        P(("grp", "exp", "dp"), None),
        P(("grp", "exp", "dp"), None),
        P(("grp", "exp", "dp"), None),
        P(("grp", "exp", "dp"), None),
        P(("grp", "exp", "dp")),
        P("grp"),
        P("exp", None, "dp"),
        P("exp", None, "dp"),
        P(),
        P(),
    )
    out_specs = P(("grp", "dp"), "exp", None)
    return jax.shard_map(body, mesh=mesh, in_specs=in_specs, out_specs=out_specs, check_vma=False)
```
